32 devices in a mesh: groups: 2 (over x), azim: 16 (over z, y, core).
Axes of the slice: x: 2, y: 2, z: 4, core: 2. Of those that a mesh axis runs over, the one named last changes fastest.
Arguments:
- v_init: float32 [16, 16384], P('groups', 'azim'), parts along dimension 0, may hold values from -4 to 4
- g_init: float32 [16, 16384], P('groups', 'azim'), parts along dimension 0, may hold values from 0 to 1.5
- spikes: int32 [4, 16, 16384], P(None, 'groups', 'azim'), parts along dimension 1, may hold values 0 or 1
- decay: float32 [2, 16384], P('groups', 'azim'), parts along dimension 0, may hold values from 0.5 to 0.95
- w_local: bfloat16 [18, 64, 16384], P('groups', None, 'azim'), parts along dimension 0, may hold values from -0.75 to 0.75
- w_long: bfloat16 [128, 16384], P('groups', 'azim'), parts along dimension 0, may hold values from -0.75 to 0.75
- lr_src_tile: int32 [256, 2], P('azim', 'groups'), parts along dimension 1, may hold values from 0 to 15; in each aligned block of 16 rows (0 to 15, 16 to 31, ...) at most 2 rows name the same one
- lr_src_block: int32 [256, 2], P('azim', 'groups'), parts along dimension 1, may hold values from 0 to 15
- lr_tgt_block: int32 [256, 2], P('azim', 'groups'), parts along dimension 1, may hold values from 0 to 15
- adj_v_end: float32 [16, 16384], P('groups', 'azim'), parts along dimension 0, may hold values from -6 to 6
- adj_g_end: float32 [16, 16384], P('groups', 'azim'), parts along dimension 0, may hold values from -6 to 6
Outputs:
- adj_v_init: float32 [16, 16384], P('groups', 'azim'), parts along dimension 0
- adj_g_init: float32 [16, 16384], P('groups', 'azim'), parts along dimension 0
- grad_local: bfloat16 [18, 64, 16384], P('groups', None, 'azim'), parts along dimension 0
- grad_long: bfloat16 [128, 16384], P('groups', 'azim'), parts along dimension 0
The draws below stay inside these ranges and needn't reach their ends.
There are 2 independent parts, one for each index of `groups`. The reference program is written for one: setup_inputs(seed, part) draws one part's arguments, and reference() takes and returns one part's arrays. A program takes and returns all parts, laid end to end along the dimension named above; each array names one. Nothing has to cross between parts.
Inputs may be any that keep to these rules, and one draw needn't show every extreme that they name: `lr_src_tile`: among the 16 entries of one tile no source tile appears more than 2 times; in some tile's list one source tile appears exactly 2 times.
All inputs are finite; a program needn't handle non-finite values. No bound on the sum of `spikes` on one device may be relied on, other than what follows from the above.
Results may differ from the reference program's by a relative error of at most 0.0054.
Values may be sent and summed in bfloat16 or wider, within the bound.
No kernel may reach another device: no remote copies, remote signals or barrier semaphores. Data moves between devices by JAX's collectives and lax.ppermute only.
A program may use at most 128 MiB of HBM per device.

```python
import math
import jax
import jax.numpy as jnp
import numpy as np
from jax import lax

BLK = 64
NB = 16
STIM = 8
CAP = 2
STEPS = 4
NTOT = 16384
LR = 16
LTOT = 256
N_AZIM = 16


def set_ends(entries, rng, smallest, high):
    place = [jax.random.randint(jax.random.fold_in(rng, axis), (), 0, length) for axis, length in enumerate(entries.shape)]
    widest = entries.shape.index(max(entries.shape))
    beside = place[:widest] + [(place[widest] + 1) % entries.shape[widest]] + place[widest + 1:]
    return entries.at[tuple(place)].set(smallest).at[tuple(beside)].set(high)


def levels(stream_key, shape, pieces, low, high):
    level = 1.0
    for axis_at, blocks in pieces:
        steps = jax.random.uniform(jax.random.fold_in(jax.random.fold_in(stream_key, 6), axis_at), (blocks,), jnp.float32, low / len(pieces), high / len(pieces))
        level = level * jnp.repeat(jnp.exp(steps), shape[axis_at] // blocks).reshape((-1,) + (1,) * (len(shape) - 1 - axis_at))
    return level


def routed_block(stream_key, own, number, rows, number_of, top, reach, lean):
    ranking = jax.random.permutation(stream_key, number_of)
    crowded, ordinary = portions_of(number_of, rows * top, reach, lean, True), portions_of(number_of, rows * top, reach, lean, False)
    places = jnp.arange(number_of)

    def named(sizes, offset_by):
        used = int((sizes > 0).sum())
        fixed = max(1, used // 4)
        passed = fixed + (places - fixed + offset_by * (used - fixed)) % max(1, number_of - fixed)
        return jnp.zeros((number_of,), jnp.int32).at[ranking[jnp.where(places < fixed, places, passed)]].set(jnp.asarray(sizes, jnp.int32))

    sizes = jnp.where(number % 4 == 0, named(crowded, number // 4), named(ordinary, number - number // 4 - 1))
    mixed = jax.random.permutation(jax.random.fold_in(own, 3), number_of)
    donor, sink = mixed[0:number_of // 2 * 2:2], mixed[1:number_of // 2 * 2:2]
    margin = jnp.minimum(sizes[donor] - 1, reach - sizes[sink]) // 2
    margin = jnp.where((donor == ranking[0]) | (sink == ranking[0]) | (sizes[sink] == 0), 0, jnp.maximum(margin, 0))
    passed = jax.random.randint(jax.random.fold_in(own, 4), (number_of // 2,), 0, 1 << 20) % (margin + 1)
    sizes = sizes.at[donor].add(-passed).at[sink].add(passed)
    labels = jnp.searchsorted(jnp.cumsum(sizes), jnp.arange(rows * top), side="right").astype(jnp.int32)
    table = labels.reshape(top, rows).T
    table = table[jax.random.permutation(jax.random.fold_in(own, 1), rows)]
    offset_by = jax.random.randint(jax.random.fold_in(own, 2), (rows, 1), 0, top)
    return jnp.take_along_axis(table, (jnp.arange(top)[None, :] + offset_by) % top, axis=1)


def portions_of(count, total, reach, lean, full):
    loads = [(1 << 20) // math.isqrt(rank ** lean) + 1 for rank in range(1, count + 1)]
    largest = reach if full else min(reach, max(-(-total // count), total * loads[0] // sum(loads)))
    least = 1 if total - largest >= count - 1 else 0
    given, rest = [largest] + [least] * (count - 1), total - largest - least * (count - 1)
    while rest > 0:
        free = [i for i in range(1, count) if given[i] < largest] or [i for i in range(1, count) if given[i] < reach]
        pool, remaining = sum([loads[i] for i in free]), rest
        for i in free:
            extra = min(reach - given[i], max(1, remaining * loads[i] // pool), rest)
            given[i] = given[i] + extra
            rest = rest - extra
    return np.array(given)


def normal_values(key, shape, width, most, shards=(), held_as=jnp.bfloat16):
    drawn = jax.random.normal(key, shape, jnp.float32) * width
    if len(shards) > 0:
        drawn = levels(key, shape, shards, -0.22, 0.18) * drawn
    return jnp.clip(drawn, min=-most, max=most).astype(held_as)


def setup_inputs(seed: int = 0, part: int = 0) -> dict:
    key_of = jax.random.split(jax.random.key(seed), 12)
    part_splits = jax.random.split(jax.random.fold_in(key_of[11], part), 12)
    v_init = normal_values(part_splits[0], (STIM, NTOT), 1.0, 4.0, ((1, 16),), jnp.float32)
    g_init = jnp.clip(1.5 * jax.random.uniform(part_splits[1], (STIM, NTOT), jnp.float32) ** levels(part_splits[1], (STIM, NTOT), ((1, 16),), -0.2, 0.2), 0.0, 1.5)
    spikes = set_ends((jax.random.randint(part_splits[2], (STEPS, STIM, NTOT), 0, 3) < 1).astype(jnp.int32), jax.random.fold_in(part_splits[2], 1), 0, 1)
    decay = jnp.clip(0.5 + 0.45 * jax.random.uniform(part_splits[3], (1, NTOT), jnp.float32) ** levels(part_splits[3], (1, NTOT), ((1, 16),), -0.2, 0.2), 0.5, 0.95)
    w_local = normal_values(part_splits[4], (9, BLK, NTOT), BLK ** -0.5, 0.75, ((2, 16),))
    w_long = normal_values(part_splits[5], (BLK, LTOT * BLK), BLK ** -0.5, 0.75, ((1, 16),))
    lr_src_tile_keys = jax.random.split(jax.random.fold_in(part_splits[6], 1), LTOT // LR)
    lr_src_tile_turns = jax.random.permutation(jax.random.fold_in(part_splits[6], 3), LTOT // LR)
    lr_src_tile = jax.vmap(lambda own, number: routed_block(jax.random.fold_in(part_splits[6], 2), own, number, LR, N_AZIM, 1, CAP, 2))(lr_src_tile_keys, lr_src_tile_turns).reshape((LTOT, 1))
    lr_src_block = set_ends(jax.random.randint(part_splits[7], (LTOT, 1), 0, NB), jax.random.fold_in(part_splits[7], 1), 0, NB - 1).astype(jnp.int32)
    lr_tgt_block = set_ends(jax.random.randint(part_splits[8], (LTOT, 1), 0, NB), jax.random.fold_in(part_splits[8], 1), 0, NB - 1).astype(jnp.int32)
    adj_v_end = normal_values(part_splits[9], (STIM, NTOT), 1.0, 6.0, ((1, 16),), jnp.float32)
    adj_g_end = normal_values(part_splits[10], (STIM, NTOT), 1.0, 6.0, ((1, 16),), jnp.float32)
    return {"v_init": v_init, "g_init": g_init, "spikes": spikes, "decay": decay, "w_local": w_local, "w_long": w_long, "lr_src_tile": lr_src_tile, "lr_src_block": lr_src_block, "lr_tgt_block": lr_tgt_block, "adj_v_end": adj_v_end, "adj_g_end": adj_g_end}


offset_table = ((-1, -1), (-1, 0), (-1, 1), (0, -1), (0, 0), (0, 1), (1, -1), (1, 0), (1, 1))


def surrogate(voltage):
    return jax.nn.sigmoid(2.0 * (voltage - 1.0))


def rounded(values):
    return lax.optimization_barrier(values.astype(jnp.bfloat16)).astype(jnp.float32)


def displace(values, step_a, step_e):
    tile_count = values.shape[1]
    row_count = values.shape[2]
    padded = jnp.pad(values, ((0, 0), (1, 1), (1, 1), (0, 0)))
    return padded[:, 1 + step_a:1 + step_a + tile_count, 1 + step_e:1 + step_e + row_count, :]


def long_drive(act_grid, w_tiles, tiles_in, blocks_in, targets):
    def per_tile(inputs):
        weights, tile_row, block_row, target_row = inputs
        picked = act_grid[:, tile_row, block_row, :]
        product = jnp.einsum("bls,lst->blt", picked, weights.astype(jnp.float32))
        target_hit = (target_row[:, None] == jnp.arange(NB, dtype=jnp.int32)[None, :]).astype(jnp.float32)
        return jnp.einsum("blt,le->bet", product, target_hit, precision=lax.Precision.HIGHEST)

    result = lax.map(per_tile, (w_tiles, tiles_in, blocks_in, targets))
    return jnp.transpose(result, (1, 0, 2, 3))


def long_back(act_grid, adj_grid, w_tiles, tiles_in, blocks_in, targets):
    def per_tile(carry, inputs):
        weights, tile_row, block_row, target_row, tile_number = inputs
        gathered = adj_grid[:, tile_number, target_row, :]
        partial_value = rounded(jnp.einsum("blt,lst->bls", gathered, weights.astype(jnp.float32)))
        carry = carry.at[:, tile_row, block_row, :].add(partial_value)
        picked = act_grid[:, tile_row, block_row, :]
        return carry, jnp.einsum("bls,blt->lst", picked, gathered)

    numbers = jnp.arange(N_AZIM, dtype=jnp.int32)
    start = jnp.zeros(act_grid.shape, jnp.float32)
    return lax.scan(per_tile, start, (w_tiles, tiles_in, blocks_in, targets, numbers))


def reference(v_init, g_init, spikes, decay, w_local, w_long, lr_src_tile, lr_src_block, lr_tgt_block, adj_v_end, adj_g_end):
    grid_shape = (STIM, N_AZIM, NB, BLK)
    w_grid = w_local.reshape(9, BLK, N_AZIM, NB, BLK)
    w_tiles = jnp.transpose(w_long.reshape(BLK, N_AZIM, LR, BLK), (1, 2, 0, 3))
    tiles_in = lr_src_tile.reshape(N_AZIM, LR).astype(jnp.int32)
    blocks_in = lr_src_block.reshape(N_AZIM, LR).astype(jnp.int32)
    targets = lr_tgt_block.reshape(N_AZIM, LR).astype(jnp.int32)
    voltage = v_init
    conduct = g_init
    records = []
    for moment in range(STEPS):
        spiking = spikes[moment].astype(jnp.float32)
        activity = rounded(spiking * surrogate(voltage))
        act_grid = activity.reshape(grid_shape)
        drive = jnp.zeros(grid_shape, jnp.float32)
        for number, (step_a, step_e) in enumerate(offset_table):
            source = displace(act_grid, step_a, step_e)
            drive = drive + jnp.einsum("baes,saet->baet", source, w_grid[number].astype(jnp.float32))
        drive = drive + long_drive(act_grid, w_tiles, tiles_in, blocks_in, targets)
        drive = drive.reshape(STIM, NTOT)
        cond_next = decay * conduct + jax.nn.softplus(drive)
        volt_next = voltage + 0.1 * (cond_next * (3.0 - voltage) - voltage) - spiking
        records.append((voltage, cond_next, drive, act_grid, spiking))
        voltage = volt_next
        conduct = cond_next
    adj_volt = adj_v_end
    adj_cond = adj_g_end
    grad_list = [jnp.zeros((BLK, N_AZIM, NB, BLK), jnp.float32) for number in range(9)]
    grad_entry = jnp.zeros((N_AZIM, LR, BLK, BLK), jnp.float32)
    for moment in reversed(range(STEPS)):
        voltage, cond_next, drive, act_grid, spiking = records[moment]
        total_g = adj_cond + adj_volt * 0.1 * (3.0 - voltage)
        adj_drive = rounded(total_g * jax.nn.sigmoid(drive))
        adj_cond = decay * total_g
        adj_grid = adj_drive.reshape(grid_shape)
        adj_act = jnp.zeros(grid_shape, jnp.float32)
        for number, (step_a, step_e) in enumerate(offset_table):
            weights = w_grid[number].astype(jnp.float32)
            partial_value = jnp.einsum("baet,saet->baes", adj_grid, weights)
            adj_act = adj_act + displace(partial_value, -step_a, -step_e)
            source = displace(act_grid, step_a, step_e)
            grad_list[number] = grad_list[number] + jnp.einsum("baes,baet->saet", source, adj_grid)
        long_adj, long_grad = long_back(act_grid, adj_grid, w_tiles, tiles_in, blocks_in, targets)
        adj_act = adj_act + long_adj
        grad_entry = grad_entry + long_grad
        slope = surrogate(voltage)
        slope = 2.0 * slope * (1.0 - slope)
        adj_volt = adj_volt * (0.9 - 0.1 * cond_next) + adj_act.reshape(STIM, NTOT) * spiking * slope
    grad_local = jnp.stack(grad_list).reshape(9, BLK, NTOT).astype(jnp.bfloat16)
    grad_long = jnp.transpose(grad_entry, (2, 0, 1, 3)).reshape(BLK, LTOT * BLK).astype(jnp.bfloat16)
    return (adj_volt, adj_cond, grad_local, grad_long)
```

```python
import functools

import jax
import jax.numpy as jnp
from jax import lax
from jax.experimental import pallas as pl
from jax.experimental.pallas import tpu as pltpu
from jax.sharding import PartitionSpec as P

BLK = 64
CAP = 2
STEPS = 4
LANES = 128
GROUP = 4
WIDE = GROUP * BLK
SIDE = 3 * BLK

f32 = jnp.float32
bf16 = jnp.bfloat16


def surrogate(voltage):
    return jax.nn.sigmoid(2.0 * (voltage - 1.0))


def lane_half(rows):
    return lax.broadcasted_iota(jnp.int32, (rows, LANES), 1) // BLK


def half_only(piece, half, which):
    return jnp.where(half == which, piece, 0.0)


def half_pair(first, second, half):
    return jnp.where(half == 0, first, second)


def swapped(piece):
    return pltpu.roll(piece, BLK, 1)


def chunks_of(values):
    return [values[:, c * LANES : (c + 1) * LANES] for c in range(values.shape[1] // LANES)]


def odd_chunks(chunks, half):
    turned = [swapped(piece) for piece in chunks]
    zero = jnp.zeros_like(chunks[0])
    return [
        half_pair(left, right, half) for left, right in zip([zero] + turned, turned + [zero])
    ]


def product(left, right):
    return lax.dot_general(left, right, (((1,), (0,)), ((), ())), preferred_element_type=f32)


def product_back(left, right):
    return lax.dot_general(left, right, (((1,), (1,)), ((), ())), preferred_element_type=f32)


def product_over(left, right):
    return lax.dot_general(left, right, (((0,), (0,)), ((), ())), preferred_element_type=f32)


def stacked(pieces):
    return jnp.concatenate(pieces, axis=0)


def folded(acc_ref, half):
    totals = []
    for block in range(acc_ref.shape[0]):
        piece = acc_ref[block]
        totals.append(piece + swapped(piece))
    return [half_pair(totals[b], totals[b + 1], half) for b in range(0, len(totals), 2)]


def start_kernel(v_ref, spikes_ref, table_ref, tile_ref, out_ref, rank_ref, ask_ref):
    chips = out_ref.shape[0]
    rows, neurons = v_ref.shape
    entries = table_ref.shape[1]
    activity = (spikes_ref[0].astype(f32) * surrogate(v_ref[...])).astype(bf16)
    table = table_ref[...]
    same = tile_ref[...] == table[0:1, :]
    before = lax.broadcasted_iota(jnp.int32, (entries, entries), 1) < lax.broadcasted_iota(
        jnp.int32, (entries, entries), 0
    )
    rank = jnp.sum(jnp.where(same & before, 1.0, 0.0), axis=1, keepdims=True).astype(jnp.int32)
    rank_ref[...] = rank
    ask_ref[...] = jnp.zeros_like(ask_ref)
    lane = lax.broadcasted_iota(jnp.int32, (rows, LANES), 1)
    for entry in range(entries):
        tile = table[0, entry]
        chip = tile // 2
        place = CAP * (tile - 2 * chip) + rank[entry, 0]
        ask_ref[chip] = jnp.where(lane == place, table[1, entry].astype(f32), ask_ref[chip])
    for chip in range(chips):
        out_ref[chip, :, :neurons] = activity
        out_ref[chip, :, neurons:] = ask_ref[chip].astype(bf16)


def forward_part(
    first, near_ref, far_ref, table_ref, w_ref, w_long_ref, source_ref, fetched_ref, acc_ref
):
    rows = near_ref.shape[1]
    neurons = w_ref.shape[1]
    blocks = neurons // BLK
    chips = near_ref.shape[0]
    entries = table_ref.shape[1]
    half = lane_half(rows)
    table = table_ref[...]
    me = table[3, 0]
    chip = me // 2
    core = me - 2 * chip
    low = chip - 1 + core
    high = chip + core
    own = near_ref[chip, :, :neurons].astype(f32)
    left = far_ref[jnp.maximum(low, 0), :, :neurons].astype(f32)
    right = far_ref[jnp.minimum(high, chips - 1), :, :neurons].astype(f32)
    left = jnp.where(low >= 0, left, 0.0)
    right = jnp.where(high < chips, right, 0.0)
    zero = jnp.zeros((rows, LANES), f32)
    for side, values in enumerate((left, own, right)):
        even = chunks_of(values)
        odd = odd_chunks(even, half)
        even = even + [zero]
        for group in range(blocks // GROUP):
            pieces = []
            for block in range(GROUP * group, GROUP * (group + 1)):
                line = even if block % 2 else odd
                pieces.append((line[block // 2], line[block // 2 + 1]))
            source_ref[group, :, side * WIDE : side * WIDE + LANES] = stacked(
                [piece[0] for piece in pieces]
            ).astype(bf16)
            source_ref[group, :, side * WIDE + LANES : (side + 1) * WIDE] = stacked(
                [piece[1] for piece in pieces]
            ).astype(bf16)
    drive = []
    for group in range(blocks // GROUP):
        columns = slice(group * WIDE, (group + 1) * WIDE)
        total = jnp.zeros((GROUP * rows, WIDE), f32)
        for side in range(3):
            total = total + product(
                source_ref[group, :, side * WIDE : side * WIDE + SIDE],
                w_ref[side * SIDE : (side + 1) * SIDE, columns],
            )
        for pair in range(GROUP // 2):
            lanes = slice(pair * LANES, (pair + 1) * LANES)
            at = 2 * pair * rows
            drive.append(
                half_pair(
                    total[at : at + rows, lanes], total[at + rows : at + 2 * rows, lanes], half
                )
            )
    acc_ref[...] = jnp.zeros_like(acc_ref)
    for group in range(entries // GROUP):
        columns = slice(group * WIDE, (group + 1) * WIDE)
        pieces = []
        for entry in range(GROUP * group, GROUP * (group + 1)):
            tile = table[0, entry]
            block = table[1, entry]
            place = tile // 2
            lanes = pl.ds(pl.multiple_of(block // 2 * LANES, LANES), LANES)
            piece = jnp.where(
                tile - 2 * place == core, near_ref[place, :, lanes], far_ref[place, :, lanes]
            )
            pieces.append(half_only(piece.astype(f32), half, block % 2))
        fetched = stacked(pieces).astype(bf16)
        fetched_ref[group] = fetched
        weights = w_long_ref[:, columns]
        total = product(fetched, stacked([weights, weights]))
        for at in range(GROUP):
            lanes = slice(at // 2 * LANES, (at // 2 + 1) * LANES)
            target = table[2, GROUP * group + at]
            acc_ref[target] += half_only(total[at * rows : (at + 1) * rows, lanes], half, at % 2)
    extra = folded(acc_ref, half)
    return jnp.concatenate([a + b for a, b in zip(drive, extra)], axis=1)


def forward_kernel(moment, *refs):
    (
        near_ref, far_ref, table_ref, w_ref, w_long_ref, v_ref, g_ref, decay_ref, spikes_ref,
    ) = refs[:9]
    v_out, g_out, gate_out, source_ref, fetched_ref, act_ref = refs[9:15]
    acc_ref = refs[-1]
    neurons = w_ref.shape[1]
    drive = forward_part(
        moment == 0, near_ref, far_ref, table_ref, w_ref, w_long_ref, source_ref, fetched_ref,
        acc_ref,
    )
    voltage = v_ref[...]
    conduct = decay_ref[...] * g_ref[...] + jax.nn.softplus(drive)
    voltage = (
        voltage + 0.1 * (conduct * (3.0 - voltage) - voltage) - spikes_ref[moment].astype(f32)
    )
    v_out[...] = voltage
    g_out[...] = conduct
    gate_out[...] = jax.nn.sigmoid(drive)
    activity = (spikes_ref[moment + 1].astype(f32) * surrogate(voltage)).astype(bf16)
    for chip in range(act_ref.shape[0]):
        act_ref[chip] = activity
    if moment == 0:
        wanted_ref = refs[15]
        core = table_ref[3, 0] % 2
        for chip in range(near_ref.shape[0]):
            for ref, place in ((near_ref, 2 * chip + core), (far_ref, 2 * chip + 1 - core)):
                asked = ref[chip, :, neurons:].astype(f32)
                asked = jnp.where(core == 1, pltpu.roll(asked, LANES - CAP, 1), asked)
                wanted_ref[place] = asked.astype(jnp.int32)


def backward_part(
    adj_cond, adj_volt, voltage, gate, decay, table_ref, rank_ref, w_ref, w_long_ref,
    adj_ref, gathered_ref, cond_out, own_out, pair_out, cross_out, placed_out, acc_ref, slot_ref,
):
    rows, neurons = voltage.shape
    blocks = neurons // BLK
    entries = table_ref.shape[1]
    half = lane_half(rows)
    table = table_ref[...]
    rank = rank_ref[...]
    core = table[3, 0] % 2
    total_g = adj_cond + adj_volt * 0.1 * (3.0 - voltage)
    adj_drive = (total_g * gate).astype(bf16).astype(f32)
    cond_out[...] = decay * total_g
    chunks = chunks_of(adj_drive)
    zero = jnp.zeros((rows, LANES), f32)
    for number, piece in enumerate(chunks):
        turned = swapped(piece)
        acc_ref[2 * number] = half_pair(piece, turned, half)
        acc_ref[2 * number + 1] = half_pair(turned, piece, half)
    even = [[zero] * (blocks // 2 + 1) for side in range(3)]
    odd = [[zero] * (blocks // 2 + 1) for side in range(3)]
    for group in range(blocks // GROUP):
        columns = slice(group * WIDE, (group + 1) * WIDE)
        left = stacked([half_only(chunks[2 * group], half, k) for k in range(2)] + [zero, zero])
        right = stacked(
            [zero, zero] + [half_only(chunks[2 * group + 1], half, k) for k in range(2)]
        )
        adj = jnp.concatenate([left, right], axis=1).astype(bf16)
        adj_ref[group] = adj
        for side in range(3):
            back = product_back(adj, w_ref[side * SIDE : (side + 1) * SIDE, columns])
            for at in range(GROUP):
                block = GROUP * group + at
                line = even[side] if block % 2 else odd[side]
                lower = back[at * rows : (at + 1) * rows, :LANES]
                upper = back[at * rows : (at + 1) * rows, LANES:]
                upper = jnp.concatenate([upper, jnp.zeros_like(upper)], axis=1)
                line[block // 2] = line[block // 2] + lower
                line[block // 2 + 1] = line[block // 2 + 1] + upper
    toward = []
    for side in range(3):
        turned = [swapped(piece) for piece in odd[side]]
        toward.append(
            jnp.concatenate(
                [
                    even[side][c] + half_pair(turned[c], turned[c + 1], half)
                    for c in range(blocks // 2)
                ],
                axis=1,
            )
        )
    own_out[...] = toward[1]
    pair_out[...] = jnp.where(core == 0, toward[2], toward[0]).astype(bf16)
    cross_out[...] = jnp.where(core == 0, toward[0], toward[2]).astype(bf16)
    slot_ref[...] = jnp.zeros_like(slot_ref)
    for group in range(entries // GROUP):
        columns = slice(group * WIDE, (group + 1) * WIDE)
        left, right = [], []
        for at in range(GROUP):
            piece = half_only(acc_ref[table[2, GROUP * group + at]], half, at % 2)
            left.append(piece if at < 2 else zero)
            right.append(zero if at < 2 else piece)
        gathered = jnp.concatenate([stacked(left), stacked(right)], axis=1).astype(bf16)
        gathered_ref[group] = gathered
        weights = w_long_ref[:, columns]
        back = product_back(gathered, stacked([weights, weights]))
        for at in range(GROUP):
            entry = GROUP * group + at
            tile = table[0, entry]
            slot_ref[tile] += half_only(back[at * rows : (at + 1) * rows], half, rank[entry, 0])
    placed_out[...] = slot_ref[...].astype(bf16)


def turn_kernel(*refs):
    (
        near_ref, far_ref, table_ref, rank_ref, w_ref, w_long_ref, v_ref, g_ref, decay_ref,
        adj_v_ref, adj_g_ref,
    ) = refs[:11]
    g_out, source_ref, fetched_ref = refs[11:14]
    outs = refs[14:21]
    acc_ref, slot_ref = refs[21:]
    drive = forward_part(
        False, near_ref, far_ref, table_ref, w_ref, w_long_ref, source_ref, fetched_ref, acc_ref
    )
    decay = decay_ref[...]
    g_out[...] = decay * g_ref[...] + jax.nn.softplus(drive)
    backward_part(
        adj_g_ref[...], adj_v_ref[...], v_ref[...], jax.nn.sigmoid(drive), decay,
        table_ref, rank_ref, w_ref, w_long_ref, *outs, acc_ref, slot_ref,
    )


def receive_part(
    moment, placed_ref, pair_ref, cross_ref, own_ref, wanted_ref, adj_v_ref, v_ref, g_ref,
    spikes_ref, acc_ref,
):
    rows = v_ref.shape[0]
    half = lane_half(rows)
    acc_ref[...] = jnp.zeros_like(acc_ref)
    for tile in range(placed_ref.shape[0]):
        arrived = placed_ref[tile].astype(f32)
        asked = wanted_ref[tile, 0:1, :]
        for slot in range(CAP):
            acc_ref[asked[0, slot]] += half_only(arrived, half, slot)
    adj_act = own_ref[...] + (pair_ref[...].astype(f32) + cross_ref[...].astype(f32))
    adj_act = adj_act + jnp.concatenate(folded(acc_ref, half), axis=1)
    slope = surrogate(v_ref[...])
    slope = 2.0 * slope * (1.0 - slope)
    return (
        adj_v_ref[...] * (0.9 - 0.1 * g_ref[...])
        + adj_act * spikes_ref[moment].astype(f32) * slope
    )


def backward_kernel(moment, *refs):
    received = refs[:9]
    (
        adj_g_ref, v_ref, gate_ref, decay_ref, table_ref, rank_ref, w_ref, w_long_ref,
    ) = refs[9:17]
    adj_v_out = refs[17]
    outs = refs[18:25]
    acc_ref, slot_ref = refs[25:]
    adj_volt = receive_part(moment, *received, acc_ref)
    adj_v_out[...] = adj_volt
    backward_part(
        adj_g_ref[...], adj_volt, v_ref[...], gate_ref[...], decay_ref[...],
        table_ref, rank_ref, w_ref, w_long_ref, *outs, acc_ref, slot_ref,
    )


def last_kernel(*refs):
    refs[9][...] = receive_part(0, *refs[:9], refs[10])


def grad_kernel(*refs):
    sources, fetched, adjs, gathered = (refs[k * STEPS : (k + 1) * STEPS] for k in range(4))
    local_ref, long_ref = refs[4 * STEPS :]
    for group in range(adjs[0].shape[0]):
        columns = slice(group * WIDE, (group + 1) * WIDE)
        adj = stacked([ref[group] for ref in adjs])
        for side in range(3):
            source = stacked([ref[group, :, side * WIDE : side * WIDE + SIDE] for ref in sources])
            local_ref[side * SIDE : (side + 1) * SIDE, columns] = product_over(
                source, adj
            ).astype(bf16)
    for group in range(gathered[0].shape[0]):
        columns = slice(group * WIDE, (group + 1) * WIDE)
        total = product_over(
            stacked([ref[group] for ref in fetched]), stacked([ref[group] for ref in gathered])
        )
        long_ref[:, columns] = (total[:BLK] + total[BLK:]).astype(bf16)


def call(kernel, outs, args, scratch=()):
    vmem = pl.BlockSpec(memory_space=pltpu.VMEM)
    return pl.pallas_call(
        kernel,
        out_shape=[jax.ShapeDtypeStruct(shape, dtype) for shape, dtype in outs],
        in_specs=[vmem] * len(args),
        out_specs=[vmem] * len(outs),
        scratch_shapes=[pltpu.VMEM(shape, dtype) for shape, dtype in scratch],
        compiler_params=pltpu.CompilerParams(vmem_limit_bytes=24 * 2**20),
    )(*args)


def local(
    v_init, g_init, spikes, decay, w_local, w_long, lr_src_tile, lr_src_block, lr_tgt_block,
    adj_v_end, adj_g_end,
):
    rows, neurons = v_init.shape
    blocks = neurons // BLK
    tiles = lax.axis_size("azim")
    chips = tiles // 2
    entries = lr_src_tile.shape[0]
    me = lax.axis_index("azim")
    cores = [list(range(core, tiles, 2)) for core in range(2)]
    pair = [(i, i ^ 1) for i in range(tiles)]
    cross = [(i, i + 1) for i in range(1, tiles - 1, 2)]
    cross = cross + [(target, source) for source, target in cross]
    table = jnp.concatenate(
        [
            jnp.concatenate([lr_src_tile, lr_src_block, lr_tgt_block], axis=1).T,
            jnp.full((1, entries), me, jnp.int32),
        ]
    )
    w_all = w_local.reshape(9 * BLK, neurons)

    def spread(values):
        near = lax.all_to_all(
            values, "azim", split_axis=0, concat_axis=0, tiled=True, axis_index_groups=cores
        )
        return near, lax.ppermute(near, "azim", pair)

    state = ((rows, neurons), f32)
    block_sum = ((blocks, rows, LANES), f32)
    slots = ((tiles, rows, LANES), f32)
    source = ((blocks // GROUP, GROUP * rows, 3 * WIDE), bf16)
    fetched = ((entries // GROUP, GROUP * rows, LANES), bf16)
    back_outs = [
        ((blocks // GROUP, GROUP * rows, WIDE), bf16),
        ((entries // GROUP, GROUP * rows, WIDE), bf16),
        state,
        state,
        ((rows, neurons), bf16),
        ((rows, neurons), bf16),
        ((tiles, rows, LANES), bf16),
    ]
    out, rank = call(
        start_kernel,
        [((chips, rows, neurons + LANES), bf16), ((entries, 1), jnp.int32)],
        (v_init, spikes, table, lr_src_tile),
        [((chips, rows, LANES), f32)],
    )
    voltages, conducts, gates, sources, fetches = [v_init], [g_init], [], [], []
    for moment in range(STEPS - 1):
        near, far = spread(out)
        outs = [state, state, state, source, fetched, ((chips, rows, neurons), bf16)]
        if moment == 0:
            outs.append(((tiles, rows, LANES), jnp.int32))
        results = call(
            functools.partial(forward_kernel, moment),
            outs,
            (
                near, far, table, w_all, w_long, voltages[-1], conducts[-1], decay, spikes,
            ),
            [block_sum],
        )
        if moment == 0:
            wanted = results[6]
        voltage, conduct, gate, source_t, fetched_t, out = results[:6]
        voltages.append(voltage)
        conducts.append(conduct)
        gates.append(gate)
        sources.append(source_t)
        fetches.append(fetched_t)
    near, far = spread(out)
    conduct, source_t, fetched_t, *back = call(
        turn_kernel,
        [state, source, fetched] + back_outs,
        (
            near, far, table, rank, w_all, w_long, voltages[-1], conducts[-1], decay,
            adj_v_end, adj_g_end,
        ),
        [block_sum, slots],
    )
    conducts.append(conduct)
    sources.append(source_t)
    fetches.append(fetched_t)
    adj_volt = adj_v_end
    adjs, gathers = [], []
    for moment in reversed(range(STEPS)):
        adj_t, gathered_t, adj_cond, own, to_pair, to_cross, placed = back
        adjs.insert(0, adj_t)
        gathers.insert(0, gathered_t)
        arrived = lax.all_to_all(placed, "azim", split_axis=0, concat_axis=0, tiled=True)
        from_pair = lax.ppermute(to_pair, "azim", pair)
        from_cross = lax.ppermute(to_cross, "azim", cross)
        received = (
            arrived, from_pair, from_cross, own, wanted, adj_volt, voltages[moment],
            conducts[moment + 1], spikes,
        )
        if moment > 0:
            adj_volt, *back = call(
                functools.partial(backward_kernel, moment),
                [state] + back_outs,
                received
                + (
                    adj_cond, voltages[moment - 1], gates[moment - 1], decay, table, rank, w_all,
                    w_long,
                ),
                [block_sum, slots],
            )
    grad_local, grad_long = call(
        grad_kernel,
        [((9 * BLK, neurons), bf16), ((BLK, entries * BLK), bf16)],
        (*sources, *fetches, *adjs, *gathers),
    )
    (adj_volt,) = call(last_kernel, [state], received, [block_sum])
    return (adj_volt, adj_cond, grad_local.reshape(9, BLK, neurons), grad_long)


def solution(mesh):
    return jax.shard_map(
        local,
        mesh=mesh,
        in_specs=(
            P("groups", "azim"),
            P("groups", "azim"),
            P(None, "groups", "azim"),
            P("groups", "azim"),
            P("groups", None, "azim"),
            P("groups", "azim"),
            P("azim", "groups"),
            P("azim", "groups"),
            P("azim", "groups"),
            P("groups", "azim"),
            P("groups", "azim"),
        ),
        out_specs=(
            P("groups", "azim"),
            P("groups", "azim"),
            P("groups", None, "azim"),
            P("groups", "azim"),
        ),
        check_vma=False,
    )
```

```python
import functools

import jax
import jax.numpy as jnp
from jax import lax
from jax.experimental import pallas as pl
from jax.experimental.pallas import tpu as pltpu
from jax.sharding import PartitionSpec as P

BLK = 64
CAP = 2
STEPS = 4
LANES = 128
GROUP = 4
WIDE = GROUP * BLK
SIDE = 3 * BLK

f32 = jnp.float32
bf16 = jnp.bfloat16


def surrogate(voltage):
    return jax.nn.sigmoid(2.0 * (voltage - 1.0))


def lane_half(rows):
    return lax.broadcasted_iota(jnp.int32, (rows, LANES), 1) // BLK


def half_only(piece, half, which):
    return jnp.where(half == which, piece, 0.0)


def half_pair(first, second, half):
    return jnp.where(half == 0, first, second)


def swapped(piece):
    return pltpu.roll(piece, BLK, 1)


def chunks_of(values):
    return [values[:, c * LANES : (c + 1) * LANES] for c in range(values.shape[1] // LANES)]


def odd_chunks(chunks, half):
    turned = [swapped(piece) for piece in chunks]
    zero = jnp.zeros_like(chunks[0])
    return [
        half_pair(left, right, half) for left, right in zip([zero] + turned, turned + [zero])
    ]


def product(left, right):
    return lax.dot_general(left, right, (((1,), (0,)), ((), ())), preferred_element_type=f32)


def product_back(left, right):
    return lax.dot_general(left, right, (((1,), (1,)), ((), ())), preferred_element_type=f32)


def product_over(left, right):
    return lax.dot_general(left, right, (((0,), (0,)), ((), ())), preferred_element_type=f32)


def stacked(pieces):
    return jnp.concatenate(pieces, axis=0)


def folded(acc_ref, half):
    totals = []
    for block in range(acc_ref.shape[1]):
        piece = half_pair(acc_ref[0, block], acc_ref[1, block], half)
        totals.append(piece + swapped(piece))
    return [half_pair(totals[b], totals[b + 1], half) for b in range(0, len(totals), 2)]


def entry_code(tile, block, target, rank):
    return ((tile * 256 + rank) * 16 + target) * 16 + block


def decoded(code):
    return code >> 16, (code >> 8) & 1, (code >> 4) & 15, code & 15


def hold_kernel(
    entry_ref, pack_ref, w_ref, w_long_ref,
    me_out, table_out, v_out, g_out, decay_out, spikes_out, w_out, w_long_out,
):
    rows = v_out.shape[0]
    v_out[...] = pack_ref[:rows]
    g_out[...] = pack_ref[rows : 2 * rows]
    for moment in range(STEPS):
        spikes_out[moment] = pack_ref[(2 + moment) * rows : (3 + moment) * rows]
    decay_out[...] = pack_ref[(2 + STEPS) * rows :]
    w_out[...] = w_ref[...]
    w_long_out[...] = w_long_ref[...]
    entries = entry_ref.shape[1]
    across = lax.broadcasted_iota(jnp.int32, (entries, entries), 1)
    down = lax.broadcasted_iota(jnp.int32, (entries, entries), 0)
    tiles = entry_ref[0:1, :]
    tiles_down = jnp.sum(
        jnp.where(across == down, tiles.astype(f32), 0.0), axis=1, keepdims=True
    ).astype(jnp.int32)
    earlier = (tiles_down == tiles) & (down < across)
    rank = jnp.sum(jnp.where(earlier, 1.0, 0.0), axis=0, keepdims=True).astype(jnp.int32)
    me_out[...] = jnp.full(me_out.shape, lax.axis_index("azim"), jnp.int32)
    table_out[...] = entry_code(tiles, entry_ref[1:2, :], entry_ref[2:3, :], rank)


def forward_part(
    near_ref, far_ref, me_ref, table_ref, w_ref, w_long_ref, source_ref, fetched_ref, acc_ref
):
    rows = near_ref.shape[1]
    neurons = w_ref.shape[1]
    blocks = neurons // BLK
    chips = near_ref.shape[0]
    entries = table_ref.shape[1]
    half = lane_half(rows)
    table = table_ref[...]
    me = me_ref[...][0, 0]
    chip = me >> 1
    core = me & 1
    acc_ref[...] = jnp.zeros_like(acc_ref)
    for group in range(entries // GROUP):
        columns = slice(group * WIDE, (group + 1) * WIDE)
        pieces, targets = [], []
        for entry in range(GROUP * group, GROUP * (group + 1)):
            tile, _, target, block = decoded(table[0, entry])
            targets.append(target)
            place = tile >> 1
            lanes = pl.ds(pl.multiple_of((block >> 1) * LANES, LANES), LANES)
            piece = jnp.where(
                (tile & 1) == core, near_ref[place, :, lanes], far_ref[place, :, lanes]
            )
            pieces.append(half_only(piece.astype(f32), half, block & 1))
        fetched = stacked(pieces).astype(bf16)
        fetched_ref[group] = fetched
        weights = w_long_ref[:, columns]
        total = product(fetched, stacked([weights, weights]))
        for at, target in enumerate(targets):
            lanes = slice(at // 2 * LANES, (at // 2 + 1) * LANES)
            acc_ref[at % 2, target] += total[at * rows : (at + 1) * rows, lanes]
    low = chip - 1 + core
    high = chip + core
    own = near_ref[chip, :, :neurons].astype(f32)
    left = far_ref[jnp.maximum(low, 0), :, :neurons].astype(f32)
    right = far_ref[jnp.minimum(high, chips - 1), :, :neurons].astype(f32)
    left = jnp.where(low >= 0, left, 0.0)
    right = jnp.where(high < chips, right, 0.0)
    zero = jnp.zeros((rows, LANES), f32)
    for side, values in enumerate((left, own, right)):
        even = chunks_of(values)
        odd = odd_chunks(even, half)
        even = even + [zero]
        for group in range(blocks // GROUP):
            pieces = []
            for block in range(GROUP * group, GROUP * (group + 1)):
                line = even if block % 2 else odd
                pieces.append((line[block // 2], line[block // 2 + 1]))
            source_ref[group, :, side * WIDE : side * WIDE + LANES] = stacked(
                [piece[0] for piece in pieces]
            ).astype(bf16)
            source_ref[group, :, side * WIDE + LANES : (side + 1) * WIDE] = stacked(
                [piece[1] for piece in pieces]
            ).astype(bf16)
    drive = []
    for group in range(blocks // GROUP):
        columns = slice(group * WIDE, (group + 1) * WIDE)
        total = jnp.zeros((GROUP * rows, WIDE), f32)
        for side in range(3):
            total = total + product(
                source_ref[group, :, side * WIDE : side * WIDE + SIDE],
                w_ref[side * SIDE : (side + 1) * SIDE, columns],
            )
        for pair in range(GROUP // 2):
            lanes = slice(pair * LANES, (pair + 1) * LANES)
            at = 2 * pair * rows
            drive.append(
                half_pair(
                    total[at : at + rows, lanes], total[at + rows : at + 2 * rows, lanes], half
                )
            )
    extra = folded(acc_ref, half)
    return jnp.concatenate([a + b for a, b in zip(drive, extra)], axis=1)


def forward_kernel(moment, *refs):
    (
        near_ref, far_ref, me_ref, table_ref, w_ref, w_long_ref, v_ref, g_ref, decay_ref,
        spikes_ref,
    ) = refs[:10]
    v_out, g_out, gate_out, source_ref, fetched_ref, act_ref = refs[10:16]
    acc_ref = refs[-1]
    rows, neurons = v_ref.shape
    chips = act_ref.shape[0]
    drive = forward_part(
        near_ref, far_ref, me_ref, table_ref, w_ref, w_long_ref, source_ref, fetched_ref, acc_ref
    )
    voltage = v_ref[...]
    conduct = decay_ref[...] * g_ref[...] + jax.nn.softplus(drive)
    voltage = (
        voltage + 0.1 * (conduct * (3.0 - voltage) - voltage) - spikes_ref[moment]
    )
    v_out[...] = voltage
    g_out[...] = conduct
    gate_out[...] = jax.nn.sigmoid(drive)
    activity = (spikes_ref[moment + 1] * surrogate(voltage)).astype(bf16)
    for chip in range(chips):
        act_ref[chip, :, :neurons] = activity
    if moment == 0:
        ask_ref = refs[-2]
        table = table_ref[...]
        lane = lax.broadcasted_iota(jnp.int32, (rows, LANES), 1)
        ask_ref[...] = jnp.zeros_like(ask_ref)
        for entry in range(table_ref.shape[1]):
            tile, rank, _, block = decoded(table[0, entry])
            place = CAP * (tile & 1) + rank
            ask_ref[tile >> 1] = jnp.where(lane == place, block.astype(f32), ask_ref[tile >> 1])
        for chip in range(chips):
            act_ref[chip, :, neurons:] = ask_ref[chip].astype(bf16)
    if moment == 1:
        wanted_ref = refs[16]
        core = me_ref[...][0, 0] & 1
        for chip in range(chips):
            for ref, place in ((near_ref, 2 * chip + core), (far_ref, 2 * chip + 1 - core)):
                asked = ref[chip, :, neurons:].astype(f32)
                asked = jnp.where(core == 1, pltpu.roll(asked, LANES - CAP, 1), asked)
                asked = asked + 16.0 * pltpu.roll(asked, LANES - 1, 1)
                wanted_ref[place] = asked.astype(jnp.int32)


def toward_tile(side, adj_ref, w_ref):
    groups, rows, _ = adj_ref.shape
    rows = rows // GROUP
    blocks = groups * GROUP
    half = lane_half(rows)
    zero = jnp.zeros((rows, LANES), f32)
    even = [zero] * (blocks // 2 + 1)
    odd = [zero] * (blocks // 2 + 1)
    for group in range(groups):
        columns = slice(group * WIDE, (group + 1) * WIDE)
        back = product_back(adj_ref[group], w_ref[side * SIDE : (side + 1) * SIDE, columns])
        for at in range(GROUP):
            block = GROUP * group + at
            line = even if block % 2 else odd
            lower = back[at * rows : (at + 1) * rows, :LANES]
            upper = back[at * rows : (at + 1) * rows, LANES:]
            upper = jnp.concatenate([upper, jnp.zeros_like(upper)], axis=1)
            line[block // 2] = line[block // 2] + lower
            line[block // 2 + 1] = line[block // 2 + 1] + upper
    turned = [swapped(piece) for piece in odd]
    return jnp.concatenate(
        [even[c] + half_pair(turned[c], turned[c + 1], half) for c in range(blocks // 2)], axis=1
    )


def backward_part(
    adj_cond, adj_volt, voltage, gate, decay, me_ref, table_ref, w_ref, w_long_ref,
    adj_ref, gathered_ref, cond_out, pair_out, cross_out, placed_out, acc_ref, slot_ref,
    stage_ref, sem,
):
    rows, neurons = voltage.shape
    blocks = neurons // BLK
    entries = table_ref.shape[1]
    half = lane_half(rows)
    table = table_ref[...]
    core = me_ref[...][0, 0] & 1
    total_g = adj_cond + adj_volt * 0.1 * (3.0 - voltage)
    adj_drive = (total_g * gate).astype(bf16).astype(f32)
    cond_out[...] = decay * total_g
    chunks = chunks_of(adj_drive)
    zero = jnp.zeros((rows, LANES), f32)
    for number, piece in enumerate(chunks):
        turned = swapped(piece)
        acc_ref[0, 2 * number] = half_pair(piece, turned, half)
        acc_ref[0, 2 * number + 1] = half_pair(turned, piece, half)
    slot_ref[...] = jnp.zeros_like(slot_ref)
    for group in range(entries // GROUP):
        columns = slice(group * WIDE, (group + 1) * WIDE)
        left, right, slots = [], [], []
        for at in range(GROUP):
            tile, rank, target, _ = decoded(table[0, GROUP * group + at])
            slots.append((rank, tile))
            piece = half_only(acc_ref[0, target], half, at % 2)
            left.append(piece if at < 2 else zero)
            right.append(zero if at < 2 else piece)
        gathered = jnp.concatenate([stacked(left), stacked(right)], axis=1).astype(bf16)
        gathered_ref[group] = gathered
        weights = w_long_ref[:, columns]
        back = product_back(gathered, stacked([weights, weights]))
        for at, slot in enumerate(slots):
            slot_ref[slot] = back[at * rows : (at + 1) * rows]
    for tile in range(stage_ref.shape[0]):
        stage_ref[tile] = half_pair(slot_ref[0, tile], slot_ref[1, tile], half).astype(bf16)
    copy = pltpu.make_async_copy(stage_ref, placed_out, sem)
    copy.start()
    for group in range(blocks // GROUP):
        left = stacked([half_only(chunks[2 * group], half, k) for k in range(2)] + [zero, zero])
        right = stacked(
            [zero, zero] + [half_only(chunks[2 * group + 1], half, k) for k in range(2)]
        )
        adj_ref[group] = jnp.concatenate([left, right], axis=1).astype(bf16)
    before = toward_tile(0, adj_ref, w_ref)
    after = toward_tile(2, adj_ref, w_ref)
    pair_out[...] = jnp.where(core == 0, after, before).astype(bf16)
    cross_out[...] = jnp.where(core == 0, before, after).astype(bf16)
    copy.wait()


def own_kernel(adj_ref, w_ref, own_out):
    own_out[...] = toward_tile(1, adj_ref, w_ref)


def turn_kernel(*refs):
    (
        near_ref, far_ref, me_ref, table_ref, w_ref, w_long_ref, v_ref, g_ref, decay_ref,
        adj_v_ref, adj_g_ref,
    ) = refs[:11]
    g_out, source_ref, fetched_ref = refs[11:14]
    acc_ref = refs[20]
    drive = forward_part(
        near_ref, far_ref, me_ref, table_ref, w_ref, w_long_ref, source_ref, fetched_ref, acc_ref
    )
    decay = decay_ref[...]
    g_out[...] = decay * g_ref[...] + jax.nn.softplus(drive)
    backward_part(
        adj_g_ref[...], adj_v_ref[...], v_ref[...], jax.nn.sigmoid(drive), decay,
        me_ref, table_ref, w_ref, w_long_ref, *refs[14:],
    )


def receive_part(
    moment, placed_ref, pair_ref, cross_ref, own_ref, wanted_ref, adj_v_ref, v_ref, g_ref,
    spikes_ref, acc_ref,
):
    rows = v_ref.shape[0]
    half = lane_half(rows)
    acc_ref[...] = jnp.zeros_like(acc_ref)
    tiles = placed_ref.shape[0]
    for first in range(0, tiles, 3):
        count = min(3, tiles - first)
        codes = wanted_ref[first, 0:1, :]
        for at in range(1, count):
            codes = codes + wanted_ref[first + at, 0:1, :] * 256**at
        code = codes[0, 0]
        for at in range(count):
            arrived = placed_ref[first + at].astype(f32)
            for slot in range(CAP):
                acc_ref[slot, (code >> (8 * at + 4 * slot)) & 15] += arrived
    adj_act = own_ref[...] + (pair_ref[...].astype(f32) + cross_ref[...].astype(f32))
    adj_act = adj_act + jnp.concatenate(folded(acc_ref, half), axis=1)
    slope = surrogate(v_ref[...])
    slope = 2.0 * slope * (1.0 - slope)
    return (
        adj_v_ref[...] * (0.9 - 0.1 * g_ref[...])
        + adj_act * spikes_ref[moment] * slope
    )


def backward_kernel(moment, *refs):
    received = refs[:9]
    (
        adj_g_ref, v_ref, gate_ref, decay_ref, me_ref, table_ref, w_ref, w_long_ref,
    ) = refs[9:17]
    adj_v_out = refs[17]
    acc_ref = refs[24]
    adj_volt = receive_part(moment, *received, acc_ref)
    adj_v_out[...] = adj_volt
    backward_part(
        adj_g_ref[...], adj_volt, v_ref[...], gate_ref[...], decay_ref[...],
        me_ref, table_ref, w_ref, w_long_ref, *refs[18:],
    )


def last_kernel(*refs):
    refs[9][...] = receive_part(0, *refs[:9], refs[10])


def grad_kernel(*refs):
    sources, fetched, adjs, gathered = (refs[k * STEPS : (k + 1) * STEPS] for k in range(4))
    cond_ref, local_ref, long_ref, cond_out = refs[4 * STEPS :]
    cond_out[...] = cond_ref[...]
    for group in range(adjs[0].shape[0]):
        columns = slice(group * WIDE, (group + 1) * WIDE)
        adj = stacked([ref[group] for ref in adjs])
        for side in range(3):
            source = stacked([ref[group, :, side * WIDE : side * WIDE + SIDE] for ref in sources])
            local_ref[side * SIDE : (side + 1) * SIDE, columns] = product_over(
                source, adj
            ).astype(bf16)
    for group in range(gathered[0].shape[0]):
        columns = slice(group * WIDE, (group + 1) * WIDE)
        total = product_over(
            stacked([ref[group] for ref in fetched]), stacked([ref[group] for ref in gathered])
        )
        long_ref[:, columns] = (total[:BLK] + total[BLK:]).astype(bf16)


def call(kernel, outs, args, scratch=(), hbm_outs=(), cost=None):
    vmem = pl.BlockSpec(memory_space=pltpu.VMEM)
    hbm = pl.BlockSpec(memory_space=pltpu.HBM)
    return pl.pallas_call(
        kernel,
        out_shape=[jax.ShapeDtypeStruct(shape, dtype) for shape, dtype in outs],
        in_specs=[vmem] * len(args),
        out_specs=[hbm if k in hbm_outs else vmem for k in range(len(outs))],
        scratch_shapes=scratch,
        compiler_params=pltpu.CompilerParams(vmem_limit_bytes=24 * 2**20),
        cost_estimate=cost,
    )(*args)


def local(
    v_init, g_init, spikes, decay, w_local, w_long, lr_src_tile, lr_src_block, lr_tgt_block,
    adj_v_end, adj_g_end,
):
    rows, neurons = v_init.shape
    blocks = neurons // BLK
    tiles = lax.axis_size("azim")
    chips = tiles // 2
    entries = lr_src_tile.shape[0]
    cores = [list(range(core, tiles, 2)) for core in range(2)]
    pair = [(i, i ^ 1) for i in range(tiles)]
    cross = [(i, i + 1) for i in range(1, tiles - 1, 2)]
    cross = cross + [(target, source) for source, target in cross]

    def spread(values, beside=()):
        near = lax.all_to_all(
            values, "azim", split_axis=0, concat_axis=0, tiled=True, axis_index_groups=cores
        )
        near, *beside = lax.optimization_barrier((near, *beside))
        return near, lax.ppermute(near, "azim", pair), *beside

    state = ((rows, neurons), f32)
    source = ((blocks // GROUP, GROUP * rows, 3 * WIDE), bf16)
    fetched = ((entries // GROUP, GROUP * rows, LANES), bf16)
    block_sum = pltpu.VMEM((CAP, blocks, rows, LANES), f32)
    back_scratch = [
        block_sum,
        pltpu.VMEM((CAP, tiles, rows, LANES), f32),
        pltpu.VMEM((tiles, rows, LANES), bf16),
        pltpu.SemaphoreType.DMA,
    ]
    back_outs = [
        ((blocks // GROUP, GROUP * rows, WIDE), bf16),
        ((entries // GROUP, GROUP * rows, WIDE), bf16),
        state,
        ((rows, neurons), bf16),
        ((rows, neurons), bf16),
        ((tiles, rows, LANES), bf16),
    ]
    activity = (spikes[0].astype(f32) * surrogate(v_init)).astype(bf16)
    out = jnp.broadcast_to(activity[None], (chips, rows, neurons))
    entry_rows = jnp.concatenate([lr_src_tile.T, lr_src_block.T, lr_tgt_block.T])
    pack = jnp.concatenate(
        [v_init, g_init, spikes.astype(f32).reshape(STEPS * rows, neurons), decay]
    )
    w_all = w_local.reshape(9 * BLK, neurons)
    beside = call(
        hold_kernel,
        [
            ((8, LANES), jnp.int32), ((1, entries), jnp.int32), state, state,
            ((1, neurons), f32), ((STEPS, rows, neurons), f32),
            (w_all.shape, bf16), (w_long.shape, bf16),
        ],
        (entry_rows, pack, w_all, w_long),
        cost=pl.CostEstimate(flops=0, bytes_accessed=4 * 2**20, transcendentals=0),
    )
    near, far, me, table, v_start, g_start, decay, spikes, w_all, w_long = spread(out, beside)
    voltages, conducts, gates, sources, fetches = [v_start], [g_start], [], [], []
    for moment in range(STEPS - 1):
        if moment > 0:
            near, far = spread(out)
        width = neurons + LANES if moment == 0 else neurons
        outs = [state, state, state, source, fetched, ((chips, rows, width), bf16)]
        scratch = [block_sum]
        if moment == 0:
            scratch.insert(0, pltpu.VMEM((chips, rows, LANES), f32))
        if moment == 1:
            outs.append(((tiles, rows, LANES), jnp.int32))
        results = call(
            functools.partial(forward_kernel, moment),
            outs,
            (near, far, me, table, w_all, w_long, voltages[-1], conducts[-1], decay, spikes),
            scratch,
        )
        if moment == 1:
            wanted = results[6]
        voltage, conduct, gate, source_t, fetched_t, out = results[:6]
        voltages.append(voltage)
        conducts.append(conduct)
        gates.append(gate)
        sources.append(source_t)
        fetches.append(fetched_t)
    near, far = spread(out)
    conduct, source_t, fetched_t, *back = call(
        turn_kernel,
        [state, source, fetched] + back_outs,
        (
            near, far, me, table, w_all, w_long, voltages[-1], conducts[-1], decay, adj_v_end,
            adj_g_end,
        ),
        back_scratch,
        hbm_outs=(8,),
    )
    conducts.append(conduct)
    sources.append(source_t)
    fetches.append(fetched_t)
    adj_volt = adj_v_end
    adjs, gathers = [], []
    for moment in reversed(range(STEPS)):
        adj_t, gathered_t, adj_cond, to_pair, to_cross, placed = back
        adjs.insert(0, adj_t)
        gathers.insert(0, gathered_t)
        arrived = lax.all_to_all(placed, "azim", split_axis=0, concat_axis=0, tiled=True)
        from_pair = lax.ppermute(to_pair, "azim", pair)
        from_cross = lax.ppermute(to_cross, "azim", cross)
        (own,) = call(own_kernel, [state], (adj_t, w_all))
        received = (
            arrived, from_pair, from_cross, own, wanted, adj_volt, voltages[moment],
            conducts[moment + 1], spikes,
        )
        if moment > 0:
            adj_volt, *back = call(
                functools.partial(backward_kernel, moment),
                [state] + back_outs,
                received
                + (
                    adj_cond, voltages[moment - 1], gates[moment - 1], decay, me, table, w_all,
                    w_long,
                ),
                back_scratch,
                hbm_outs=(6,),
            )
    grad_local, grad_long, adj_cond = call(
        grad_kernel,
        [((9 * BLK, neurons), bf16), ((BLK, entries * BLK), bf16), state],
        (*sources, *fetches, *adjs, *gathers, adj_cond),
    )
    (adj_volt,) = call(last_kernel, [state], received, [block_sum])
    return (adj_volt, adj_cond, grad_local.reshape(9, BLK, neurons), grad_long)


def solution(mesh):
    return jax.shard_map(
        local,
        mesh=mesh,
        in_specs=(
            P("groups", "azim"),
            P("groups", "azim"),
            P(None, "groups", "azim"),
            P("groups", "azim"),
            P("groups", None, "azim"),
            P("groups", "azim"),
            P("azim", "groups"),
            P("azim", "groups"),
            P("azim", "groups"),
            P("groups", "azim"),
            P("groups", "azim"),
        ),
        out_specs=(
            P("groups", "azim"),
            P("groups", "azim"),
            P("groups", None, "azim"),
            P("groups", "azim"),
        ),
        check_vma=False,
    )
```

```python
import functools

import jax
import jax.numpy as jnp
from jax import lax
from jax.experimental import pallas as pl
from jax.experimental.pallas import tpu as pltpu
from jax.sharding import PartitionSpec as P

BLK = 64
CAP = 2
STEPS = 4
LANES = 128
GROUP = 4
WIDE = GROUP * BLK
SIDE = 3 * BLK

f32 = jnp.float32
bf16 = jnp.bfloat16


def surrogate(voltage):
    return jax.nn.sigmoid(2.0 * (voltage - 1.0))


def lane_half(rows):
    return lax.broadcasted_iota(jnp.int32, (rows, LANES), 1) // BLK


def half_only(piece, half, which):
    return jnp.where(half == which, piece, 0.0)


def half_pair(first, second, half):
    return jnp.where(half == 0, first, second)


def swapped(piece):
    return pltpu.roll(piece, BLK, 1)


def chunks_of(values):
    return [values[:, c * LANES : (c + 1) * LANES] for c in range(values.shape[1] // LANES)]


def odd_chunks(chunks, half):
    turned = [swapped(piece) for piece in chunks]
    zero = jnp.zeros_like(chunks[0])
    return [
        half_pair(left, right, half) for left, right in zip([zero] + turned, turned + [zero])
    ]


def product(left, right):
    return lax.dot_general(left, right, (((1,), (0,)), ((), ())), preferred_element_type=f32)


def product_back(left, right):
    return lax.dot_general(left, right, (((1,), (1,)), ((), ())), preferred_element_type=f32)


def product_over(left, right):
    return lax.dot_general(left, right, (((0,), (0,)), ((), ())), preferred_element_type=f32)


def stacked(pieces):
    return jnp.concatenate(pieces, axis=0)


def folded(acc_ref, half):
    totals = []
    for block in range(acc_ref.shape[1]):
        piece = half_pair(acc_ref[0, block], acc_ref[1, block], half)
        totals.append(piece + swapped(piece))
    return [half_pair(totals[b], totals[b + 1], half) for b in range(0, len(totals), 2)]


def in_group(tile):
    return (tile ^ (tile >> 1)) & 1


def source_code(tile, block, target, me):
    far = in_group(tile) ^ in_group(me)
    chunk = (tile >> 1) * 8 + (block >> 1)
    return ((chunk * 2 + far) * 2 + (block & 1)) * 16 + target


def source_of(code):
    return code >> 9, (code >> 6) & 7, (code >> 5) & 1, (code >> 4) & 1, code & 15


def slot_code(tile, rank, target):
    return (tile * CAP + rank) * 16 + target


def slot_of(code):
    return code >> 5, (code >> 4) & 1, code & 15


def start_kernel(*refs):
    heads, rest = refs[:3], refs[3:]
    count = (len(rest) - 8) // 2
    held, (out_ref, me_ref, table_ref), kept = rest[:count], rest[count : count + 3], rest[count + 3 :]
    rows_of, ask_ref, sems = kept[count : count + 3], kept[count + 3], kept[count + 4]
    kept = kept[:count]
    copies = [
        pltpu.make_async_copy(source, target, sems.at[number])
        for number, (source, target) in enumerate(zip((*heads, *held), (*rows_of, *kept)))
    ]
    for copy in copies[3:6] + copies[:3] + copies[6:]:
        copy.start()
    chips = out_ref.shape[0]
    v_ref, spikes_ref = kept[:2]
    rows, neurons = v_ref.shape
    entries = table_ref.shape[1]
    for copy in copies[3:5]:
        copy.wait()
    activity = (spikes_ref[0].astype(f32) * surrogate(v_ref[...])).astype(bf16)
    for chip in range(chips):
        out_ref[chip, :, :neurons] = activity
    me = lax.axis_index("azim")
    me_ref[...] = jnp.full(me_ref.shape, me, jnp.int32)
    ask_ref[...] = jnp.zeros_like(ask_ref)
    across = lax.broadcasted_iota(jnp.int32, (entries, entries), 1)
    down = lax.broadcasted_iota(jnp.int32, (entries, entries), 0)
    lane = lax.broadcasted_iota(jnp.int32, (rows, LANES), 1)
    for copy in copies[:3]:
        copy.wait()
    tiles, block, target = (ref[...] for ref in rows_of)
    tiles_down = jnp.sum(
        jnp.where(across == down, tiles.astype(f32), 0.0), axis=1, keepdims=True
    ).astype(jnp.int32)
    earlier = (tiles_down == tiles) & (down < across)
    rank = jnp.sum(jnp.where(earlier, 1.0, 0.0), axis=0, keepdims=True).astype(jnp.int32)
    table = jnp.concatenate(
        [source_code(tiles, block, target, me), slot_code(tiles, rank, target)], axis=0
    )
    table_ref[...] = table
    for entry in range(entries):
        tile, slot, _ = slot_of(table[1, entry])
        _, chunk, _, side, _ = source_of(table[0, entry])
        asked = (2 * chunk + side).astype(f32)
        place = CAP * (tile & 1) + slot
        ask_ref[tile >> 1] = jnp.where(lane == place, asked, ask_ref[tile >> 1])
    for chip in range(chips):
        out_ref[chip, :, neurons:] = ask_ref[chip].astype(bf16)
    for copy in copies[5:]:
        copy.wait()


def tile_drive(values, weights, source_ref, half):
    rows = values.shape[0]
    even = chunks_of(values)
    odd = odd_chunks(even, half)
    even = even + [jnp.zeros((rows, LANES), f32)]
    drive = []
    for group in range((len(even) - 1) * 2 // GROUP):
        pieces = []
        for block in range(GROUP * group, GROUP * (group + 1)):
            line = even if block % 2 else odd
            pieces.append((line[block // 2], line[block // 2 + 1]))
        source = jnp.concatenate(
            [stacked([piece[k] for piece in pieces]) for k in range(2)], axis=1
        ).astype(bf16)
        source_ref[group] = source
        total = product(source[:, :SIDE], weights(slice(group * WIDE, (group + 1) * WIDE)))
        for pair in range(GROUP // 2):
            lanes = slice(pair * LANES, (pair + 1) * LANES)
            at = 2 * pair * rows
            drive.append(
                half_pair(
                    total[at : at + rows, lanes], total[at + rows : at + 2 * rows, lanes], half
                )
            )
    return drive


def near_kernel(near_ref, me_ref, w_ref, drive_out, source_ref):
    chips = near_ref.shape[0]
    neurons = w_ref.shape[2]
    half = lane_half(near_ref.shape[1])
    me = me_ref[...][0, 0]
    chip = me >> 1
    core = me & 1
    own = near_ref[chip, :, :neurons].astype(f32)
    beyond = chip - 1 + 2 * core
    cross = near_ref[jnp.clip(beyond, 0, chips - 1), :, :neurons].astype(f32)
    cross = jnp.where((beyond >= 0) & (beyond < chips), cross, 0.0)
    first = tile_drive(own, lambda columns: w_ref[1, :, columns], source_ref.at[0], half)
    second = tile_drive(
        cross, lambda columns: w_ref[2 * core, :, columns], source_ref.at[1], half
    )
    drive_out[...] = jnp.concatenate([a + b for a, b in zip(first, second)], axis=1)


def forward_part(
    near_ref, far_ref, partial_ref, me_ref, table_ref, w_ref, w_long_ref, source_ref, fetched_ref,
    acc_ref,
):
    rows = near_ref.shape[1]
    neurons = w_ref.shape[2]
    entries = table_ref.shape[1]
    half = lane_half(rows)
    table = table_ref[...]
    me = me_ref[...][0, 0]
    acc_ref[...] = jnp.zeros_like(acc_ref)
    for group in range(entries // GROUP):
        columns = slice(group * WIDE, (group + 1) * WIDE)
        pieces, targets = [], []
        for entry in range(GROUP * group, GROUP * (group + 1)):
            place, chunk, far, side, target = source_of(table[0, entry])
            targets.append(target)
            lanes = pl.ds(pl.multiple_of(chunk * LANES, LANES), LANES)
            piece = jnp.where(far == 0, near_ref[place, :, lanes], far_ref[place, :, lanes])
            pieces.append(half_only(piece.astype(f32), half, side))
        fetched = stacked(pieces).astype(bf16)
        fetched_ref[group] = fetched
        weights = w_long_ref[:, columns]
        total = product(fetched, stacked([weights, weights]))
        for at, target in enumerate(targets):
            lanes = slice(at // 2 * LANES, (at // 2 + 1) * LANES)
            acc_ref[at % 2, target] += total[at * rows : (at + 1) * rows, lanes]
    mate = far_ref[me >> 1, :, :neurons].astype(f32)
    drive = tile_drive(
        mate, lambda columns: w_ref[2 - 2 * (me & 1), :, columns], source_ref, half
    )
    extra = folded(acc_ref, half)
    return partial_ref[...] + jnp.concatenate([a + b for a, b in zip(drive, extra)], axis=1)


def forward_kernel(moment, *refs):
    (
        near_ref, far_ref, partial_ref, me_ref, table_ref, w_ref, w_long_ref, v_ref, g_ref,
        decay_ref, spikes_ref,
    ) = refs[:11]
    v_out, g_out, gate_out, source_ref, fetched_ref, act_ref = refs[11:17]
    acc_ref = refs[-1]
    rows, neurons = v_ref.shape
    chips = act_ref.shape[0]
    drive = forward_part(
        near_ref, far_ref, partial_ref, me_ref, table_ref, w_ref, w_long_ref, source_ref,
        fetched_ref, acc_ref,
    )
    voltage = v_ref[...]
    conduct = decay_ref[...] * g_ref[...] + jax.nn.softplus(drive)
    voltage = (
        voltage + 0.1 * (conduct * (3.0 - voltage) - voltage) - spikes_ref[moment].astype(f32)
    )
    v_out[...] = voltage
    g_out[...] = conduct
    gate_out[...] = jax.nn.sigmoid(drive)
    activity = (spikes_ref[moment + 1].astype(f32) * surrogate(voltage)).astype(bf16)
    for chip in range(chips):
        act_ref[chip] = activity
    if moment == 0:
        wanted_ref = refs[17]
        core = me_ref[...][0, 0] & 1
        mine = in_group(me_ref[...][0, 0])
        for chip in range(chips):
            near_core = mine ^ (chip & 1)
            for ref, place in ((near_ref, near_core), (far_ref, 1 - near_core)):
                place = 2 * chip + place
                asked = ref[chip, :, neurons:].astype(f32)
                asked = jnp.where(core == 1, pltpu.roll(asked, LANES - CAP, 1), asked)
                asked = asked + 16.0 * pltpu.roll(asked, LANES - 1, 1)
                wanted_ref[place] = asked.astype(jnp.int32)


def toward_tile(side, adj_ref, w_ref):
    groups, rows, _ = adj_ref.shape
    rows = rows // GROUP
    blocks = groups * GROUP
    half = lane_half(rows)
    zero = jnp.zeros((rows, LANES), f32)
    even = [zero] * (blocks // 2 + 1)
    odd = [zero] * (blocks // 2 + 1)
    for group in range(groups):
        columns = slice(group * WIDE, (group + 1) * WIDE)
        back = product_back(adj_ref[group], w_ref[side, :, columns])
        for at in range(GROUP):
            block = GROUP * group + at
            line = even if block % 2 else odd
            lower = back[at * rows : (at + 1) * rows, :LANES]
            upper = back[at * rows : (at + 1) * rows, LANES:]
            upper = jnp.concatenate([upper, jnp.zeros_like(upper)], axis=1)
            line[block // 2] = line[block // 2] + lower
            line[block // 2 + 1] = line[block // 2 + 1] + upper
    turned = [swapped(piece) for piece in odd]
    return jnp.concatenate(
        [even[c] + half_pair(turned[c], turned[c + 1], half) for c in range(blocks // 2)], axis=1
    )


def backward_part(
    adj_cond, adj_volt, voltage, gate, decay, me_ref, table_ref, w_ref, w_long_ref,
    adj_ref, gathered_ref, cond_out, pair_out, cross_out, placed_out, acc_ref, slot_ref,
    stage_ref, sem,
):
    rows, neurons = voltage.shape
    blocks = neurons // BLK
    entries = table_ref.shape[1]
    half = lane_half(rows)
    table = table_ref[...]
    core = me_ref[...][0, 0] & 1
    total_g = adj_cond + adj_volt * 0.1 * (3.0 - voltage)
    adj_drive = (total_g * gate).astype(bf16).astype(f32)
    cond_out[...] = decay * total_g
    chunks = chunks_of(adj_drive)
    zero = jnp.zeros((rows, LANES), f32)
    for number, piece in enumerate(chunks):
        turned = swapped(piece)
        acc_ref[0, 2 * number] = half_pair(piece, turned, half)
        acc_ref[0, 2 * number + 1] = half_pair(turned, piece, half)
    slot_ref[...] = jnp.zeros_like(slot_ref)
    for group in range(entries // GROUP):
        columns = slice(group * WIDE, (group + 1) * WIDE)
        left, right, slots = [], [], []
        for at in range(GROUP):
            tile, rank, target = slot_of(table[1, GROUP * group + at])
            slots.append((rank, tile))
            piece = half_only(acc_ref[0, target], half, at % 2)
            left.append(piece if at < 2 else zero)
            right.append(zero if at < 2 else piece)
        gathered = jnp.concatenate([stacked(left), stacked(right)], axis=1).astype(bf16)
        gathered_ref[group] = gathered
        weights = w_long_ref[:, columns]
        back = product_back(gathered, stacked([weights, weights]))
        for at, slot in enumerate(slots):
            slot_ref[slot] = back[at * rows : (at + 1) * rows]
    for tile in range(stage_ref.shape[0]):
        stage_ref[tile] = half_pair(slot_ref[0, tile], slot_ref[1, tile], half).astype(bf16)
    copy = pltpu.make_async_copy(stage_ref, placed_out, sem)
    copy.start()
    for group in range(blocks // GROUP):
        left = stacked([half_only(chunks[2 * group], half, k) for k in range(2)] + [zero, zero])
        right = stacked(
            [zero, zero] + [half_only(chunks[2 * group + 1], half, k) for k in range(2)]
        )
        adj_ref[group] = jnp.concatenate([left, right], axis=1).astype(bf16)
    cross_out[...] = toward_tile(2 * core, adj_ref, w_ref).astype(bf16)
    pair_out[...] = toward_tile(2 - 2 * core, adj_ref, w_ref).astype(bf16)
    copy.wait()


def own_kernel(
    moment, adj_ref, w_ref, adj_v_ref, v_ref, g_ref, spikes_ref, base_out, gain_out
):
    slope = surrogate(v_ref[...])
    gain = spikes_ref[moment].astype(f32) * (2.0 * slope * (1.0 - slope))
    gain_out[...] = gain
    base_out[...] = (
        adj_v_ref[...] * (0.9 - 0.1 * g_ref[...]) + toward_tile(1, adj_ref, w_ref) * gain
    )


def turn_kernel(*refs):
    (
        near_ref, far_ref, partial_ref, me_ref, table_ref, w_ref, w_long_ref, v_ref, g_ref,
        decay_ref, adj_v_ref, adj_g_ref,
    ) = refs[:12]
    g_out, source_ref, fetched_ref = refs[12:15]
    acc_ref = refs[21]
    drive = forward_part(
        near_ref, far_ref, partial_ref, me_ref, table_ref, w_ref, w_long_ref, source_ref,
        fetched_ref, acc_ref,
    )
    decay = decay_ref[...]
    g_out[...] = decay * g_ref[...] + jax.nn.softplus(drive)
    backward_part(
        adj_g_ref[...], adj_v_ref[...], v_ref[...], jax.nn.sigmoid(drive), decay,
        me_ref, table_ref, w_ref, w_long_ref, *refs[15:],
    )


def receive_part(placed_ref, pair_ref, cross_ref, base_ref, gain_ref, wanted_ref, acc_ref):
    half = lane_half(base_ref.shape[0])
    acc_ref[...] = jnp.zeros_like(acc_ref)
    tiles = placed_ref.shape[0]
    for first in range(0, tiles, 3):
        count = min(3, tiles - first)
        codes = wanted_ref[first, 0:1, :]
        for at in range(1, count):
            codes = codes + wanted_ref[first + at, 0:1, :] * 256**at
        code = codes[0, 0]
        for at in range(count):
            arrived = placed_ref[first + at].astype(f32)
            for slot in range(CAP):
                acc_ref[slot, (code >> (8 * at + 4 * slot)) & 15] += arrived
    rest = pair_ref[...].astype(f32) + cross_ref[...].astype(f32)
    rest = rest + jnp.concatenate(folded(acc_ref, half), axis=1)
    return base_ref[...] + rest * gain_ref[...]


def backward_kernel(*refs):
    adj_g_ref, v_ref, gate_ref, decay_ref, me_ref, table_ref, w_ref, w_long_ref = refs[6:14]
    adj_v_out = refs[14]
    acc_ref = refs[21]
    adj_volt = receive_part(*refs[:6], acc_ref)
    adj_v_out[...] = adj_volt
    backward_part(
        adj_g_ref[...], adj_volt, v_ref[...], gate_ref[...], decay_ref[...],
        me_ref, table_ref, w_ref, w_long_ref, *refs[15:],
    )


def last_kernel(*refs):
    refs[6][...] = receive_part(*refs[:6], refs[7])


def grad_kernel(*refs):
    near, far, fetched, adjs, gathered = (refs[k * STEPS : (k + 1) * STEPS] for k in range(5))
    me_ref, cond_ref, local_ref, long_ref, cond_out = refs[5 * STEPS :]
    cond_out[...] = cond_ref[...]
    core = me_ref[...][0, 0] & 1
    for group in range(adjs[0].shape[0]):
        columns = slice(group * WIDE, (group + 1) * WIDE)
        adj = stacked([ref[group] for ref in adjs])
        for side, sources in (
            (1, [ref[0, group] for ref in near]),
            (2 * core, [ref[1, group] for ref in near]),
            (2 - 2 * core, [ref[group] for ref in far]),
        ):
            total = product_over(stacked(sources)[:, :SIDE], adj)
            local_ref[side, :, columns] = total.astype(bf16)
    for group in range(gathered[0].shape[0]):
        columns = slice(group * WIDE, (group + 1) * WIDE)
        total = product_over(
            stacked([ref[group] for ref in fetched]), stacked([ref[group] for ref in gathered])
        )
        long_ref[:, columns] = (total[:BLK] + total[BLK:]).astype(bf16)


def call(kernel, outs, args, scratch=(), hbm_outs=(), hbm_args=False):
    vmem = pl.BlockSpec(memory_space=pltpu.VMEM)
    hbm = pl.BlockSpec(memory_space=pltpu.HBM)
    if hbm_args:
        args = [pltpu.with_memory_space_constraint(array, pltpu.HBM) for array in args]
    return pl.pallas_call(
        kernel,
        out_shape=[jax.ShapeDtypeStruct(shape, dtype) for shape, dtype in outs],
        in_specs=[hbm if hbm_args else vmem] * len(args),
        out_specs=[hbm if k in hbm_outs else vmem for k in range(len(outs))],
        scratch_shapes=scratch,
        compiler_params=pltpu.CompilerParams(vmem_limit_bytes=24 * 2**20),
    )(*args)


def local(
    v_init, g_init, spikes, decay, w_local, w_long, lr_src_tile, lr_src_block, lr_tgt_block,
    adj_v_end, adj_g_end,
):
    rows, neurons = v_init.shape
    blocks = neurons // BLK
    tiles = lax.axis_size("azim")
    chips = tiles // 2
    entries = lr_src_tile.shape[0]
    members = [[tile for tile in range(tiles) if in_group(tile) == k] for k in range(2)]
    pair = [(i, i ^ 1) for i in range(tiles)]
    cross = [(i, i + 1) for i in range(1, tiles - 1, 2)]
    cross = cross + [(target, source) for source, target in cross]

    def spread(values):
        near = lax.all_to_all(
            values, "azim", split_axis=0, concat_axis=0, tiled=True, axis_index_groups=members
        )
        return near, lax.ppermute(near, "azim", pair)

    state = ((rows, neurons), f32)
    source = ((blocks // GROUP, GROUP * rows, WIDE), bf16)
    sources = ((2, *source[0]), bf16)
    fetched = ((entries // GROUP, GROUP * rows, LANES), bf16)
    block_sum = pltpu.VMEM((CAP, blocks, rows, LANES), f32)
    back_scratch = [
        block_sum,
        pltpu.VMEM((CAP, tiles, rows, LANES), f32),
        pltpu.VMEM((tiles, rows, LANES), bf16),
        pltpu.SemaphoreType.DMA,
    ]
    back_outs = [
        ((blocks // GROUP, GROUP * rows, WIDE), bf16),
        ((entries // GROUP, GROUP * rows, WIDE), bf16),
        state,
        ((rows, neurons), bf16),
        ((rows, neurons), bf16),
        ((tiles, rows, LANES), bf16),
    ]
    held = (
        v_init, spikes, w_local.reshape(3, SIDE, neurons), w_long, g_init, decay, adj_v_end,
        adj_g_end,
    )
    entry_row = pltpu.VMEM((1, entries), jnp.int32)
    out, me, table, v_start, spikes, w_all, w_long, g_start, decay, adj_volt, adj_cond = call(
        start_kernel,
        [
            ((chips, rows, neurons + LANES), bf16), ((8, LANES), jnp.int32),
            ((2, entries), jnp.int32),
        ]
        + [(array.shape, array.dtype) for array in held],
        (lr_src_tile.T, lr_src_block.T, lr_tgt_block.T, *held),
        [
            entry_row, entry_row, entry_row, pltpu.VMEM((chips, rows, LANES), f32),
            pltpu.SemaphoreType.DMA((3 + len(held),)),
        ],
        hbm_args=True,
    )
    voltages, conducts, gates, nears, fars, fetches = [v_start], [g_start], [], [], [], []
    for moment in range(STEPS - 1):
        near, far = spread(out)
        partial, near_t = call(near_kernel, [state, sources], (near, me, w_all))
        nears.append(near_t)
        outs = [state, state, state, source, fetched, ((chips, rows, neurons), bf16)]
        if moment == 0:
            outs.append(((tiles, rows, LANES), jnp.int32))
        results = call(
            functools.partial(forward_kernel, moment),
            outs,
            (
                near, far, partial, me, table, w_all, w_long, voltages[-1], conducts[-1], decay,
                spikes,
            ),
            [block_sum],
        )
        if moment == 0:
            wanted = results[6]
        voltage, conduct, gate, far_t, fetched_t, out = results[:6]
        voltages.append(voltage)
        conducts.append(conduct)
        gates.append(gate)
        fars.append(far_t)
        fetches.append(fetched_t)
    near, far = spread(out)
    partial, near_t = call(near_kernel, [state, sources], (near, me, w_all))
    nears.append(near_t)
    conduct, far_t, fetched_t, *back = call(
        turn_kernel,
        [state, source, fetched] + back_outs,
        (
            near, far, partial, me, table, w_all, w_long, voltages[-1], conducts[-1], decay,
            adj_volt, adj_cond,
        ),
        back_scratch,
        hbm_outs=(8,),
    )
    conducts.append(conduct)
    fars.append(far_t)
    fetches.append(fetched_t)
    adjs, gathers = [], []
    for moment in reversed(range(STEPS)):
        adj_t, gathered_t, adj_cond, to_pair, to_cross, placed = back
        adjs.insert(0, adj_t)
        gathers.insert(0, gathered_t)
        arrived = lax.all_to_all(placed, "azim", split_axis=0, concat_axis=0, tiled=True)
        from_cross = lax.ppermute(to_cross, "azim", cross)
        from_pair = lax.ppermute(to_pair, "azim", pair)
        base, gain = call(
            functools.partial(own_kernel, moment),
            [state, state],
            (adj_t, w_all, adj_volt, voltages[moment], conducts[moment + 1], spikes),
        )
        received = (arrived, from_pair, from_cross, base, gain, wanted)
        if moment > 0:
            adj_volt, *back = call(
                backward_kernel,
                [state] + back_outs,
                received
                + (
                    adj_cond, voltages[moment - 1], gates[moment - 1], decay, me, table, w_all,
                    w_long,
                ),
                back_scratch,
                hbm_outs=(6,),
            )
    grad_local, grad_long, adj_cond = call(
        grad_kernel,
        [((3, SIDE, neurons), bf16), ((BLK, entries * BLK), bf16), state],
        (*nears, *fars, *fetches, *adjs, *gathers, me, adj_cond),
    )
    (adj_volt,) = call(last_kernel, [state], received, [block_sum])
    return (adj_volt, adj_cond, grad_local.reshape(9, BLK, neurons), grad_long)


def solution(mesh):
    return jax.shard_map(
        local,
        mesh=mesh,
        in_specs=(
            P("groups", "azim"),
            P("groups", "azim"),
            P(None, "groups", "azim"),
            P("groups", "azim"),
            P("groups", None, "azim"),
            P("groups", "azim"),
            P("azim", "groups"),
            P("azim", "groups"),
            P("azim", "groups"),
            P("groups", "azim"),
            P("groups", "azim"),
        ),
        out_specs=(
            P("groups", "azim"),
            P("groups", "azim"),
            P("groups", None, "azim"),
            P("groups", "azim"),
        ),
        check_vma=False,
    )
```

```python
import functools

import jax
import jax.numpy as jnp
from jax import lax
from jax.experimental import pallas as pl
from jax.experimental.pallas import tpu as pltpu
from jax.sharding import PartitionSpec as P

BLK = 64
CAP = 2
STEPS = 4
LANES = 128
GROUP = 4
WIDE = GROUP * BLK
SIDE = 3 * BLK

f32 = jnp.float32
bf16 = jnp.bfloat16


def surrogate(voltage):
    return jax.nn.sigmoid(2.0 * (voltage - 1.0))


def lane_half(rows):
    return lax.broadcasted_iota(jnp.int32, (rows, LANES), 1) // BLK


def half_only(piece, half, which):
    return jnp.where(half == which, piece, 0.0)


def half_pair(first, second, half):
    return jnp.where(half == 0, first, second)


def swapped(piece):
    return pltpu.roll(piece, BLK, 1)


def chunks_of(values):
    return [values[:, c * LANES : (c + 1) * LANES] for c in range(values.shape[1] // LANES)]


def odd_chunks(chunks, half):
    turned = [swapped(piece) for piece in chunks]
    zero = jnp.zeros_like(chunks[0])
    return [
        half_pair(left, right, half) for left, right in zip([zero] + turned, turned + [zero])
    ]


def product(left, right):
    return lax.dot_general(left, right, (((1,), (0,)), ((), ())), preferred_element_type=f32)


def product_back(left, right):
    return lax.dot_general(left, right, (((1,), (1,)), ((), ())), preferred_element_type=f32)


def product_over(left, right):
    return lax.dot_general(left, right, (((0,), (0,)), ((), ())), preferred_element_type=f32)


def stacked(pieces):
    return jnp.concatenate(pieces, axis=0)


def folded(acc_refs, half):
    chunks = []
    for block in range(0, acc_refs[0].shape[0], 2):
        (low, low_next), (high, high_next) = (
            (sum(ref[block] for ref in refs), sum(ref[block + 1] for ref in refs))
            for refs in (acc_refs[0::2], acc_refs[1::2])
        )
        chunks.append(half_pair(low, high_next, half) + swapped(half_pair(low_next, high, half)))
    return chunks


def in_group(tile):
    return (tile ^ (tile >> 1)) & 1


FIELDS = 7
ACCS = 4


def source_of(entry_ref, entry):
    return tuple(entry_ref[FIELDS * entry + field] for field in range(5))


def slot_of(entry_ref, entry):
    return tuple(entry_ref[FIELDS * entry + field] for field in range(4, 7))


def start_kernel(*refs):
    heads, rest = refs[:3], refs[3:]
    count = (len(rest) - 9) // 2
    held, (out_ref, me_ref, entry_ref) = rest[:count], rest[count : count + 3]
    kept = rest[count + 3 : 2 * count + 3]
    tile_ref, block_ref, target_ref, used_ref, ask_ref, sems = rest[2 * count + 3 :]
    lists = (tile_ref, block_ref, target_ref)
    copies = [
        pltpu.make_async_copy(source, target, sems.at[number])
        for number, (source, target) in enumerate(zip((*heads, *held), (*lists, *kept)))
    ]
    for copy in copies[3:6] + copies[:3] + copies[6:]:
        copy.start()
    chips = out_ref.shape[0]
    v_ref, spikes_ref = kept[:2]
    rows, neurons = v_ref.shape
    entries = tile_ref.shape[1]
    me = lax.axis_index("azim")
    me_ref[0] = me
    lane = lax.broadcasted_iota(jnp.int32, (rows, LANES), 1)
    ask_ref[...] = jnp.zeros_like(ask_ref)
    for tile in range(2 * chips):
        used_ref[tile] = 0
    for copy in copies[:3]:
        copy.wait()
    for entry in range(entries):
        tile = tile_ref[0, entry]
        block = block_ref[0, entry]
        rank = used_ref[tile]
        used_ref[tile] = rank + 1
        fields = (
            tile >> 1, (block >> 1) * LANES, in_group(tile) ^ in_group(me), block & 1,
            target_ref[0, entry], tile, rank,
        )
        for number, field in enumerate(fields):
            entry_ref[FIELDS * entry + number] = field
        place = CAP * (tile & 1) + rank
        ask_ref[tile >> 1] = jnp.where(lane == place, block.astype(f32), ask_ref[tile >> 1])
    for copy in copies[3:5]:
        copy.wait()
    activity = (spikes_ref[0].astype(f32) * surrogate(v_ref[...])).astype(bf16)
    for chip in range(chips):
        out_ref[chip, :, :neurons] = activity
        out_ref[chip, :, neurons:] = ask_ref[chip].astype(bf16)
    for copy in copies[5:]:
        copy.wait()


def wanted_kernel(near_ref, far_ref, me_ref, wanted_ref):
    chips, _, width = near_ref.shape
    me = me_ref[0]
    for chip in range(chips):
        near_core = in_group(me) ^ (chip & 1)
        for ref, core in ((near_ref, near_core), (far_ref, 1 - near_core)):
            asked = ref[chip, :, width - LANES :].astype(f32)
            asked = jnp.where((me & 1) == 1, pltpu.roll(asked, LANES - CAP, 1), asked)
            asked = asked.astype(jnp.int32)
            for slot in range(CAP):
                wanted_ref[CAP * (2 * chip + core) + slot] = asked[0, slot]


def tile_drive(values, weights, source_ref, half):
    rows = values.shape[0]
    even = chunks_of(values)
    odd = odd_chunks(even, half)
    even = even + [jnp.zeros((rows, LANES), f32)]
    drive = []
    for group in range((len(even) - 1) * 2 // GROUP):
        pieces = []
        for block in range(GROUP * group, GROUP * (group + 1)):
            line = even if block % 2 else odd
            pieces.append((line[block // 2], line[block // 2 + 1]))
        source = jnp.concatenate(
            [stacked([piece[k] for piece in pieces]) for k in range(2)], axis=1
        ).astype(bf16)
        source_ref[group] = source
        total = product(source[:, :SIDE], weights(slice(group * WIDE, (group + 1) * WIDE)))
        for pair in range(GROUP // 2):
            lanes = slice(pair * LANES, (pair + 1) * LANES)
            at = 2 * pair * rows
            drive.append(
                half_pair(
                    total[at : at + rows, lanes], total[at + rows : at + 2 * rows, lanes], half
                )
            )
    return drive


def near_kernel(near_ref, me_ref, w_ref, drive_out, source_ref):
    chips = near_ref.shape[0]
    neurons = w_ref.shape[2]
    half = lane_half(near_ref.shape[1])
    me = me_ref[0]
    chip = me >> 1
    core = me & 1
    own = near_ref[chip, :, :neurons].astype(f32)
    beyond = chip - 1 + 2 * core
    cross = near_ref[jnp.clip(beyond, 0, chips - 1), :, :neurons].astype(f32)
    cross = jnp.where((beyond >= 0) & (beyond < chips), cross, 0.0)
    first = tile_drive(own, lambda columns: w_ref[1, :, columns], source_ref.at[0], half)
    second = tile_drive(
        cross, lambda columns: w_ref[2 * core, :, columns], source_ref.at[1], half
    )
    drive_out[...] = jnp.concatenate([a + b for a, b in zip(first, second)], axis=1)


def forward_part(
    near_ref, far_ref, partial_ref, me_ref, entry_ref, w_ref, w_long_ref, source_ref, fetched_ref,
    acc_refs,
):
    rows = near_ref.shape[1]
    neurons = w_ref.shape[2]
    entries = fetched_ref.shape[0] * GROUP
    half = lane_half(rows)
    me = me_ref[0]
    for ref in acc_refs:
        ref[...] = jnp.zeros_like(ref)
    for group in range(entries // GROUP):
        columns = slice(group * WIDE, (group + 1) * WIDE)
        pieces, targets = [], []
        for entry in range(GROUP * group, GROUP * (group + 1)):
            place, lane, far, side, target = source_of(entry_ref, entry)
            targets.append(target)
            lanes = pl.ds(pl.multiple_of(lane, LANES), LANES)
            piece = jnp.where(far == 0, near_ref[place, :, lanes], far_ref[place, :, lanes])
            pieces.append(half_only(piece.astype(f32), half, side))
        fetched = stacked(pieces).astype(bf16)
        fetched_ref[group] = fetched
        weights = w_long_ref[:, columns]
        total = product(fetched, stacked([weights, weights]))
        for at, target in enumerate(targets):
            lanes = slice(at // 2 * LANES, (at // 2 + 1) * LANES)
            acc_refs[(at + 2 * group) % len(acc_refs)][target] += total[
                at * rows : (at + 1) * rows, lanes
            ]
    mate = far_ref[me >> 1, :, :neurons].astype(f32)
    drive = tile_drive(
        mate, lambda columns: w_ref[2 - 2 * (me & 1), :, columns], source_ref, half
    )
    extra = folded(acc_refs, half)
    return partial_ref[...] + jnp.concatenate([a + b for a, b in zip(drive, extra)], axis=1)


def forward_kernel(moment, *refs):
    (
        near_ref, far_ref, partial_ref, me_ref, entry_ref, w_ref, w_long_ref, v_ref, g_ref,
        decay_ref, spikes_ref,
    ) = refs[:11]
    v_out, g_out, gate_out, source_ref, fetched_ref, act_ref = refs[11:17]
    acc_refs = refs[17:]
    rows, neurons = v_ref.shape
    chips = act_ref.shape[0]
    drive = forward_part(
        near_ref, far_ref, partial_ref, me_ref, entry_ref, w_ref, w_long_ref, source_ref,
        fetched_ref, acc_refs,
    )
    voltage = v_ref[...]
    conduct = decay_ref[...] * g_ref[...] + jax.nn.softplus(drive)
    voltage = (
        voltage + 0.1 * (conduct * (3.0 - voltage) - voltage) - spikes_ref[moment].astype(f32)
    )
    v_out[...] = voltage
    g_out[...] = conduct
    gate_out[...] = jax.nn.sigmoid(drive)
    activity = (spikes_ref[moment + 1].astype(f32) * surrogate(voltage)).astype(bf16)
    for chip in range(chips):
        act_ref[chip] = activity


def toward_tile(side, adj_ref, w_ref):
    groups, rows, _ = adj_ref.shape
    rows = rows // GROUP
    blocks = groups * GROUP
    half = lane_half(rows)
    zero = jnp.zeros((rows, LANES), f32)
    even = [zero] * (blocks // 2 + 1)
    odd = [zero] * (blocks // 2 + 1)
    for group in range(groups):
        columns = slice(group * WIDE, (group + 1) * WIDE)
        back = product_back(adj_ref[group], w_ref[side, :, columns])
        for at in range(GROUP):
            block = GROUP * group + at
            line = even if block % 2 else odd
            lower = back[at * rows : (at + 1) * rows, :LANES]
            upper = back[at * rows : (at + 1) * rows, LANES:]
            upper = jnp.concatenate([upper, jnp.zeros_like(upper)], axis=1)
            line[block // 2] = line[block // 2] + lower
            line[block // 2 + 1] = line[block // 2 + 1] + upper
    turned = [swapped(piece) for piece in odd]
    return jnp.concatenate(
        [even[c] + half_pair(turned[c], turned[c + 1], half) for c in range(blocks // 2)], axis=1
    )


def backward_part(
    adj_cond, adj_volt, voltage, gate, decay, me_ref, entry_ref, w_ref, w_long_ref,
    adj_ref, gathered_ref, cond_out, pair_out, cross_out, placed_out, block_ref, slot_ref,
    stage_ref, sem,
):
    rows, neurons = voltage.shape
    blocks = neurons // BLK
    entries = gathered_ref.shape[0] * GROUP
    half = lane_half(rows)
    core = me_ref[0] & 1
    total_g = adj_cond + adj_volt * 0.1 * (3.0 - voltage)
    adj_drive = (total_g * gate).astype(bf16).astype(f32)
    cond_out[...] = decay * total_g
    chunks = chunks_of(adj_drive)
    zero = jnp.zeros((rows, LANES), f32)
    for number, piece in enumerate(chunks):
        turned = swapped(piece)
        block_ref[2 * number] = half_pair(piece, turned, half)
        block_ref[2 * number + 1] = half_pair(turned, piece, half)
    slot_ref[...] = jnp.zeros_like(slot_ref)
    for group in range(entries // GROUP):
        columns = slice(group * WIDE, (group + 1) * WIDE)
        left, right, slots = [], [], []
        for at in range(GROUP):
            target, tile, rank = slot_of(entry_ref, GROUP * group + at)
            slots.append((rank, tile))
            piece = half_only(block_ref[target], half, at % 2)
            left.append(piece if at < 2 else zero)
            right.append(zero if at < 2 else piece)
        gathered = jnp.concatenate([stacked(left), stacked(right)], axis=1).astype(bf16)
        gathered_ref[group] = gathered
        weights = w_long_ref[:, columns]
        back = product_back(gathered, stacked([weights, weights]))
        for at, slot in enumerate(slots):
            slot_ref[slot] = back[at * rows : (at + 1) * rows]
    for tile in range(stage_ref.shape[0]):
        stage_ref[tile] = half_pair(slot_ref[0, tile], slot_ref[1, tile], half).astype(bf16)
    copy = pltpu.make_async_copy(stage_ref, placed_out, sem)
    copy.start()
    for group in range(blocks // GROUP):
        left = stacked([half_only(chunks[2 * group], half, k) for k in range(2)] + [zero, zero])
        right = stacked(
            [zero, zero] + [half_only(chunks[2 * group + 1], half, k) for k in range(2)]
        )
        adj_ref[group] = jnp.concatenate([left, right], axis=1).astype(bf16)
    cross_out[...] = toward_tile(2 * core, adj_ref, w_ref).astype(bf16)
    pair_out[...] = toward_tile(2 - 2 * core, adj_ref, w_ref).astype(bf16)
    copy.wait()


def own_kernel(
    moment, adj_ref, w_ref, adj_v_ref, v_ref, g_ref, spikes_ref, base_out, gain_out
):
    slope = surrogate(v_ref[...])
    gain = spikes_ref[moment].astype(f32) * (2.0 * slope * (1.0 - slope))
    gain_out[...] = gain
    base_out[...] = (
        adj_v_ref[...] * (0.9 - 0.1 * g_ref[...]) + toward_tile(1, adj_ref, w_ref) * gain
    )


def turn_kernel(*refs):
    (
        near_ref, far_ref, partial_ref, me_ref, entry_ref, w_ref, w_long_ref, v_ref, g_ref,
        decay_ref, adj_v_ref, adj_g_ref,
    ) = refs[:12]
    g_out, source_ref, fetched_ref = refs[12:15]
    acc_refs = refs[25:]
    drive = forward_part(
        near_ref, far_ref, partial_ref, me_ref, entry_ref, w_ref, w_long_ref, source_ref,
        fetched_ref, acc_refs,
    )
    decay = decay_ref[...]
    g_out[...] = decay * g_ref[...] + jax.nn.softplus(drive)
    backward_part(
        adj_g_ref[...], adj_v_ref[...], v_ref[...], jax.nn.sigmoid(drive), decay,
        me_ref, entry_ref, w_ref, w_long_ref, *refs[15:25],
    )


def receive_part(placed_ref, pair_ref, cross_ref, base_ref, gain_ref, wanted_ref, acc_refs):
    half = lane_half(base_ref.shape[0])
    for ref in acc_refs:
        ref[...] = jnp.zeros_like(ref)
    tiles = placed_ref.shape[0]
    for tile in range(tiles):
        arrived = placed_ref[tile].astype(f32)
        for slot in range(CAP):
            number = (slot + CAP * tile) % len(acc_refs)
            acc_refs[number][wanted_ref[CAP * tile + slot]] += arrived
    rest = pair_ref[...].astype(f32) + cross_ref[...].astype(f32)
    rest = rest + jnp.concatenate(folded(acc_refs, half), axis=1)
    return base_ref[...] + rest * gain_ref[...]


def backward_kernel(*refs):
    adj_g_ref, v_ref, gate_ref, decay_ref, me_ref, entry_ref, w_ref, w_long_ref = refs[6:14]
    adj_v_out = refs[14]
    adj_volt = receive_part(*refs[:6], refs[25:])
    adj_v_out[...] = adj_volt
    backward_part(
        adj_g_ref[...], adj_volt, v_ref[...], gate_ref[...], decay_ref[...],
        me_ref, entry_ref, w_ref, w_long_ref, *refs[15:25],
    )


def last_kernel(*refs):
    refs[6][...] = receive_part(*refs[:6], refs[7:])


def grad_kernel(*refs):
    near, far, fetched, adjs, gathered = (refs[k * STEPS : (k + 1) * STEPS] for k in range(5))
    me_ref, cond_ref, local_ref, long_ref, cond_out = refs[5 * STEPS :]
    cond_out[...] = cond_ref[...]
    core = me_ref[0] & 1
    for group in range(adjs[0].shape[0]):
        columns = slice(group * WIDE, (group + 1) * WIDE)
        adj = stacked([ref[group] for ref in adjs])
        for side, sources in (
            (1, [ref[0, group] for ref in near]),
            (2 * core, [ref[1, group] for ref in near]),
            (2 - 2 * core, [ref[group] for ref in far]),
        ):
            total = product_over(stacked(sources)[:, :SIDE], adj)
            local_ref[side, :, columns] = total.astype(bf16)
    for group in range(gathered[0].shape[0]):
        columns = slice(group * WIDE, (group + 1) * WIDE)
        total = product_over(
            stacked([ref[group] for ref in fetched]), stacked([ref[group] for ref in gathered])
        )
        long_ref[:, columns] = (total[:BLK] + total[BLK:]).astype(bf16)


def call(kernel, outs, args, scratch=(), hbm_outs=(), hbm_args=False):
    def spec(space):
        return pl.BlockSpec(memory_space=space)

    vmem, hbm, smem = (spec(space) for space in (pltpu.VMEM, pltpu.HBM, pltpu.SMEM))
    if hbm_args:
        args = [pltpu.with_memory_space_constraint(array, pltpu.HBM) for array in args]
    in_specs = [smem if array.ndim == 1 else hbm if hbm_args else vmem for array in args]
    out_specs = [
        smem if len(shape) == 1 else hbm if number in hbm_outs else vmem
        for number, (shape, _) in enumerate(outs)
    ]
    return pl.pallas_call(
        kernel,
        out_shape=[
            pltpu.SMEM(shape, dtype) if len(shape) == 1 else jax.ShapeDtypeStruct(shape, dtype)
            for shape, dtype in outs
        ],
        in_specs=in_specs,
        out_specs=out_specs,
        scratch_shapes=scratch,
        compiler_params=pltpu.CompilerParams(vmem_limit_bytes=24 * 2**20),
    )(*args)


def local(
    v_init, g_init, spikes, decay, w_local, w_long, lr_src_tile, lr_src_block, lr_tgt_block,
    adj_v_end, adj_g_end,
):
    rows, neurons = v_init.shape
    blocks = neurons // BLK
    tiles = lax.axis_size("azim")
    chips = tiles // 2
    entries = lr_src_tile.shape[0]
    members = [[tile for tile in range(tiles) if in_group(tile) == k] for k in range(2)]
    pair = [(i, i ^ 1) for i in range(tiles)]
    cross = [(i, i + 1) for i in range(1, tiles - 1, 2)]
    cross = cross + [(target, source) for source, target in cross]

    def spread(values):
        near = lax.all_to_all(
            values, "azim", split_axis=0, concat_axis=0, tiled=True, axis_index_groups=members
        )
        return near, lax.ppermute(near, "azim", pair)

    state = ((rows, neurons), f32)
    source = ((blocks // GROUP, GROUP * rows, WIDE), bf16)
    sources = ((2, *source[0]), bf16)
    fetched = ((entries // GROUP, GROUP * rows, LANES), bf16)
    block_row = pltpu.VMEM((blocks, rows, LANES), f32)
    sums = [block_row] * ACCS
    back_scratch = [
        block_row,
        pltpu.VMEM((CAP, tiles, rows, LANES), f32),
        pltpu.VMEM((tiles, rows, LANES), bf16),
        pltpu.SemaphoreType.DMA,
        *sums,
    ]
    back_outs = [
        ((blocks // GROUP, GROUP * rows, WIDE), bf16),
        ((entries // GROUP, GROUP * rows, WIDE), bf16),
        state,
        ((rows, neurons), bf16),
        ((rows, neurons), bf16),
        ((tiles, rows, LANES), bf16),
    ]
    held = (
        v_init, spikes, w_local.reshape(3, SIDE, neurons), w_long, g_init, decay, adj_v_end,
        adj_g_end,
    )
    entry_row = pltpu.SMEM((1, entries), jnp.int32)
    out, me, entry_list, v_start, spikes, w_all, w_long, g_start, decay, adj_volt, adj_cond = call(
        start_kernel,
        [
            ((chips, rows, neurons + LANES), bf16), ((1,), jnp.int32),
            ((FIELDS * entries,), jnp.int32),
        ]
        + [(array.shape, array.dtype) for array in held],
        (lr_src_tile.T, lr_src_block.T, lr_tgt_block.T, *held),
        [
            entry_row, entry_row, entry_row, pltpu.SMEM((tiles,), jnp.int32),
            pltpu.VMEM((chips, rows, LANES), f32),
            pltpu.SemaphoreType.DMA((3 + len(held),)),
        ],
        hbm_args=True,
    )
    voltages, conducts, gates, nears, fars, fetches = [v_start], [g_start], [], [], [], []
    for moment in range(STEPS - 1):
        near, far = spread(out)
        partial, near_t = call(near_kernel, [state, sources], (near, me, w_all))
        nears.append(near_t)
        outs = [state, state, state, source, fetched, ((chips, rows, neurons), bf16)]
        results = call(
            functools.partial(forward_kernel, moment),
            outs,
            (
                near, far, partial, me, entry_list, w_all, w_long, voltages[-1], conducts[-1], decay,
                spikes,
            ),
            sums,
        )
        if moment == 0:
            (wanted,) = call(wanted_kernel, [((CAP * tiles,), jnp.int32)], (near, far, me))
        voltage, conduct, gate, far_t, fetched_t, out = results
        voltages.append(voltage)
        conducts.append(conduct)
        gates.append(gate)
        fars.append(far_t)
        fetches.append(fetched_t)
    near, far = spread(out)
    partial, near_t = call(near_kernel, [state, sources], (near, me, w_all))
    nears.append(near_t)
    conduct, far_t, fetched_t, *back = call(
        turn_kernel,
        [state, source, fetched] + back_outs,
        (
            near, far, partial, me, entry_list, w_all, w_long, voltages[-1], conducts[-1], decay,
            adj_volt, adj_cond,
        ),
        back_scratch,
        hbm_outs=(8,),
    )
    conducts.append(conduct)
    fars.append(far_t)
    fetches.append(fetched_t)
    adjs, gathers = [], []
    for moment in reversed(range(STEPS)):
        adj_t, gathered_t, adj_cond, to_pair, to_cross, placed = back
        adjs.insert(0, adj_t)
        gathers.insert(0, gathered_t)
        arrived = lax.all_to_all(placed, "azim", split_axis=0, concat_axis=0, tiled=True)
        from_cross = lax.ppermute(to_cross, "azim", cross)
        from_pair = lax.ppermute(to_pair, "azim", pair)
        base, gain = call(
            functools.partial(own_kernel, moment),
            [state, state],
            (adj_t, w_all, adj_volt, voltages[moment], conducts[moment + 1], spikes),
        )
        received = (arrived, from_pair, from_cross, base, gain, wanted)
        if moment > 0:
            adj_volt, *back = call(
                backward_kernel,
                [state] + back_outs,
                received
                + (
                    adj_cond, voltages[moment - 1], gates[moment - 1], decay, me, entry_list, w_all,
                    w_long,
                ),
                back_scratch,
                hbm_outs=(6,),
            )
    grad_local, grad_long, adj_cond = call(
        grad_kernel,
        [((3, SIDE, neurons), bf16), ((BLK, entries * BLK), bf16), state],
        (*nears, *fars, *fetches, *adjs, *gathers, me, adj_cond),
    )
    (adj_volt,) = call(last_kernel, [state], received, sums)
    return (adj_volt, adj_cond, grad_local.reshape(9, BLK, neurons), grad_long)


def solution(mesh):
    return jax.shard_map(
        local,
        mesh=mesh,
        in_specs=(
            P("groups", "azim"),
            P("groups", "azim"),
            P(None, "groups", "azim"),
            P("groups", "azim"),
            P("groups", None, "azim"),
            P("groups", "azim"),
            P("azim", "groups"),
            P("azim", "groups"),
            P("azim", "groups"),
            P("groups", "azim"),
            P("groups", "azim"),
        ),
        out_specs=(
            P("groups", "azim"),
            P("groups", "azim"),
            P("groups", None, "azim"),
            P("groups", "azim"),
        ),
        check_vma=False,
    )
```

```python
import functools

import jax
import jax.numpy as jnp
from jax import lax
from jax.experimental import pallas as pl
from jax.experimental.pallas import tpu as pltpu
from jax.sharding import PartitionSpec as P

BLK = 64
CAP = 2
STEPS = 4
LANES = 128
GROUP = 4
WIDE = GROUP * BLK
SIDE = 3 * BLK

f32 = jnp.float32
bf16 = jnp.bfloat16


def surrogate(voltage):
    return jax.nn.sigmoid(2.0 * (voltage - 1.0))


def lane_half(rows):
    return lax.broadcasted_iota(jnp.int32, (rows, LANES), 1) // BLK


def half_only(piece, half, which):
    return jnp.where(half == which, piece, 0.0)


def half_pair(first, second, half):
    return jnp.where(half == 0, first, second)


def swapped(piece):
    return pltpu.roll(piece, BLK, 1)


def chunks_of(values):
    return [values[:, c * LANES : (c + 1) * LANES] for c in range(values.shape[1] // LANES)]


def odd_chunks(chunks, half):
    turned = [swapped(piece) for piece in chunks]
    zero = jnp.zeros_like(chunks[0])
    return [
        half_pair(left, right, half) for left, right in zip([zero] + turned, turned + [zero])
    ]


def product(left, right):
    return lax.dot_general(left, right, (((1,), (0,)), ((), ())), preferred_element_type=f32)


def product_back(left, right):
    return lax.dot_general(left, right, (((1,), (1,)), ((), ())), preferred_element_type=f32)


def product_over(left, right):
    return lax.dot_general(left, right, (((0,), (0,)), ((), ())), preferred_element_type=f32)


def stacked(pieces):
    return jnp.concatenate(pieces, axis=0)


def folded(acc_refs, half):
    chunks = []
    for block in range(0, acc_refs[0].shape[0], 2):
        (low, low_next), (high, high_next) = (
            (sum(ref[block] for ref in refs), sum(ref[block + 1] for ref in refs))
            for refs in (acc_refs[0::2], acc_refs[1::2])
        )
        chunks.append(half_pair(low, high_next, half) + swapped(half_pair(low_next, high, half)))
    return chunks


def in_group(tile):
    return (tile ^ (tile >> 1)) & 1


FIELDS = 7
ACCS = 4


def source_of(entry_ref, entry):
    return tuple(entry_ref[FIELDS * entry + field] for field in range(5))


def slot_of(entry_ref, entry):
    return tuple(entry_ref[FIELDS * entry + field] for field in range(4, 7))


def start_kernel(*refs):
    heads, rest = refs[:3], refs[3:]
    count = (len(rest) - 9) // 2
    held, (out_ref, me_ref, entry_ref) = rest[:count], rest[count : count + 3]
    kept = rest[count + 3 : 2 * count + 3]
    tile_ref, block_ref, target_ref, used_ref, ask_ref, sems = rest[2 * count + 3 :]
    lists = (tile_ref, block_ref, target_ref)
    copies = [
        pltpu.make_async_copy(source, target, sems.at[number])
        for number, (source, target) in enumerate(zip((*heads, *held), (*lists, *kept)))
    ]
    for copy in copies[3:6] + copies[:3] + copies[6:]:
        copy.start()
    chips = out_ref.shape[0]
    v_ref, spikes_ref = kept[:2]
    rows, neurons = v_ref.shape
    entries = tile_ref.shape[1]
    me = lax.axis_index("azim")
    me_ref[0] = me
    lane = lax.broadcasted_iota(jnp.int32, (rows, LANES), 1)
    ask_ref[...] = jnp.zeros_like(ask_ref)
    for tile in range(2 * chips):
        used_ref[tile] = 0
    for copy in copies[:3]:
        copy.wait()
    for entry in range(entries):
        tile = tile_ref[0, entry]
        block = block_ref[0, entry]
        rank = used_ref[tile]
        used_ref[tile] = rank + 1
        fields = (
            tile >> 1, (block >> 1) * LANES, in_group(tile) ^ in_group(me), block & 1,
            target_ref[0, entry], tile, rank,
        )
        for number, field in enumerate(fields):
            entry_ref[FIELDS * entry + number] = field
        place = CAP * (tile & 1) + rank
        ask_ref[tile >> 1] = jnp.where(lane == place, block.astype(f32), ask_ref[tile >> 1])
    for copy in copies[3:5]:
        copy.wait()
    activity = (spikes_ref[0].astype(f32) * surrogate(v_ref[...])).astype(bf16)
    for chip in range(chips):
        out_ref[chip, :, :neurons] = activity
        out_ref[chip, :, neurons:] = ask_ref[chip].astype(bf16)
    for copy in copies[5:]:
        copy.wait()


def wanted_kernel(near_ref, far_ref, me_ref, wanted_ref):
    chips, _, width = near_ref.shape
    me = me_ref[0]
    for chip in range(chips):
        near_core = in_group(me) ^ (chip & 1)
        for ref, core in ((near_ref, near_core), (far_ref, 1 - near_core)):
            asked = ref[chip, :, width - LANES :].astype(f32)
            asked = jnp.where((me & 1) == 1, pltpu.roll(asked, LANES - CAP, 1), asked)
            asked = asked.astype(jnp.int32)
            for slot in range(CAP):
                wanted_ref[CAP * (2 * chip + core) + slot] = asked[0, slot]


def tile_drive(values, weights, source_ref, half):
    rows = values.shape[0]
    even = chunks_of(values)
    odd = odd_chunks(even, half)
    even = even + [jnp.zeros((rows, LANES), f32)]
    drive = []
    for group in range((len(even) - 1) * 2 // GROUP):
        pieces = []
        for block in range(GROUP * group, GROUP * (group + 1)):
            line = even if block % 2 else odd
            pieces.append((line[block // 2], line[block // 2 + 1]))
        source = jnp.concatenate(
            [stacked([piece[k] for piece in pieces]) for k in range(2)], axis=1
        ).astype(bf16)
        source_ref[group] = source
        total = product(source[:, :SIDE], weights(slice(group * WIDE, (group + 1) * WIDE)))
        for pair in range(GROUP // 2):
            lanes = slice(pair * LANES, (pair + 1) * LANES)
            at = 2 * pair * rows
            drive.append(
                half_pair(
                    total[at : at + rows, lanes], total[at + rows : at + 2 * rows, lanes], half
                )
            )
    return drive


def near_kernel(near_ref, me_ref, w_ref, drive_out, source_ref):
    chips = near_ref.shape[0]
    neurons = w_ref.shape[2]
    half = lane_half(near_ref.shape[1])
    me = me_ref[0]
    chip = me >> 1
    core = me & 1
    own = near_ref[chip, :, :neurons].astype(f32)
    beyond = chip - 1 + 2 * core
    cross = near_ref[jnp.clip(beyond, 0, chips - 1), :, :neurons].astype(f32)
    cross = jnp.where((beyond >= 0) & (beyond < chips), cross, 0.0)
    first = tile_drive(own, lambda columns: w_ref[1, :, columns], source_ref.at[0], half)
    second = tile_drive(
        cross, lambda columns: w_ref[2 * core, :, columns], source_ref.at[1], half
    )
    drive_out[...] = jnp.concatenate([a + b for a, b in zip(first, second)], axis=1)


def forward_part(
    near_ref, far_ref, partial_ref, me_ref, entry_ref, w_ref, w_long_ref, source_ref, fetched_ref,
    acc_refs,
):
    rows = near_ref.shape[1]
    neurons = w_ref.shape[2]
    entries = fetched_ref.shape[0] * GROUP
    half = lane_half(rows)
    me = me_ref[0]
    for ref in acc_refs:
        ref[...] = jnp.zeros_like(ref)
    for group in range(entries // GROUP):
        columns = slice(group * WIDE, (group + 1) * WIDE)
        pieces, targets = [], []
        for entry in range(GROUP * group, GROUP * (group + 1)):
            place, lane, far, side, target = source_of(entry_ref, entry)
            targets.append(target)
            lanes = pl.ds(pl.multiple_of(lane, LANES), LANES)
            piece = jnp.where(far == 0, near_ref[place, :, lanes], far_ref[place, :, lanes])
            pieces.append(half_only(piece.astype(f32), half, side))
        fetched = stacked(pieces).astype(bf16)
        fetched_ref[group] = fetched
        weights = w_long_ref[:, columns]
        total = product(fetched, stacked([weights, weights]))
        for at, target in enumerate(targets):
            lanes = slice(at // 2 * LANES, (at // 2 + 1) * LANES)
            acc_refs[(at + 2 * group) % len(acc_refs)][target] += total[
                at * rows : (at + 1) * rows, lanes
            ]
    mate = far_ref[me >> 1, :, :neurons].astype(f32)
    drive = tile_drive(
        mate, lambda columns: w_ref[2 - 2 * (me & 1), :, columns], source_ref, half
    )
    extra = folded(acc_refs, half)
    return partial_ref[...] + jnp.concatenate([a + b for a, b in zip(drive, extra)], axis=1)


def forward_kernel(moment, *refs):
    (
        near_ref, far_ref, partial_ref, me_ref, entry_ref, w_ref, w_long_ref, v_ref, g_ref,
        decay_ref, spikes_ref,
    ) = refs[:11]
    v_out, g_out, gate_out, source_ref, fetched_ref, act_ref = refs[11:17]
    acc_refs = refs[17:]
    rows, neurons = v_ref.shape
    chips = act_ref.shape[0]
    drive = forward_part(
        near_ref, far_ref, partial_ref, me_ref, entry_ref, w_ref, w_long_ref, source_ref,
        fetched_ref, acc_refs,
    )
    voltage = v_ref[...]
    conduct = decay_ref[...] * g_ref[...] + jax.nn.softplus(drive)
    voltage = (
        voltage + 0.1 * (conduct * (3.0 - voltage) - voltage) - spikes_ref[moment].astype(f32)
    )
    v_out[...] = voltage
    g_out[...] = conduct
    gate_out[...] = jax.nn.sigmoid(drive)
    activity = (spikes_ref[moment + 1].astype(f32) * surrogate(voltage)).astype(bf16)
    for chip in range(chips):
        act_ref[chip] = activity


def toward_tile(side, adj_ref, w_ref):
    groups, rows, _ = adj_ref.shape
    rows = rows // GROUP
    blocks = groups * GROUP
    half = lane_half(rows)
    zero = jnp.zeros((rows, LANES), f32)
    even = [zero] * (blocks // 2 + 1)
    odd = [zero] * (blocks // 2 + 1)
    for group in range(groups):
        columns = slice(group * WIDE, (group + 1) * WIDE)
        back = product_back(adj_ref[group], w_ref[side, :, columns])
        for at in range(GROUP):
            block = GROUP * group + at
            line = even if block % 2 else odd
            lower = back[at * rows : (at + 1) * rows, :LANES]
            upper = back[at * rows : (at + 1) * rows, LANES:]
            upper = jnp.concatenate([upper, jnp.zeros_like(upper)], axis=1)
            line[block // 2] = line[block // 2] + lower
            line[block // 2 + 1] = line[block // 2 + 1] + upper
    turned = [swapped(piece) for piece in odd]
    return jnp.concatenate(
        [even[c] + half_pair(turned[c], turned[c + 1], half) for c in range(blocks // 2)], axis=1
    )


def backward_part(
    adj_cond, adj_volt, voltage, gate, decay, me_ref, entry_ref, w_ref, w_long_ref,
    adj_ref, gathered_ref, cond_out, cross_out, pair_out, placed_out, block_ref, slot_ref,
    stage_ref, sem,
):
    rows, neurons = voltage.shape
    blocks = neurons // BLK
    entries = gathered_ref.shape[0] * GROUP
    half = lane_half(rows)
    core = me_ref[0] & 1
    total_g = adj_cond + adj_volt * 0.1 * (3.0 - voltage)
    adj_drive = (total_g * gate).astype(bf16).astype(f32)
    cond_out[...] = decay * total_g
    chunks = chunks_of(adj_drive)
    zero = jnp.zeros((rows, LANES), f32)
    for number, piece in enumerate(chunks):
        turned = swapped(piece)
        block_ref[2 * number] = half_pair(piece, turned, half)
        block_ref[2 * number + 1] = half_pair(turned, piece, half)
    slot_ref[...] = jnp.zeros_like(slot_ref)
    for group in range(entries // GROUP):
        columns = slice(group * WIDE, (group + 1) * WIDE)
        left, right, slots = [], [], []
        for at in range(GROUP):
            target, tile, rank = slot_of(entry_ref, GROUP * group + at)
            slots.append((rank, tile))
            piece = half_only(block_ref[target], half, at % 2)
            left.append(piece if at < 2 else zero)
            right.append(zero if at < 2 else piece)
        gathered = jnp.concatenate([stacked(left), stacked(right)], axis=1).astype(bf16)
        gathered_ref[group] = gathered
        weights = w_long_ref[:, columns]
        back = product_back(gathered, stacked([weights, weights]))
        for at, slot in enumerate(slots):
            slot_ref[slot] = back[at * rows : (at + 1) * rows]
    for tile in range(stage_ref.shape[0]):
        stage_ref[tile] = half_pair(slot_ref[0, tile], slot_ref[1, tile], half).astype(bf16)
    copy = pltpu.make_async_copy(stage_ref, placed_out, sem)
    copy.start()
    for group in range(blocks // GROUP):
        left = stacked([half_only(chunks[2 * group], half, k) for k in range(2)] + [zero, zero])
        right = stacked(
            [zero, zero] + [half_only(chunks[2 * group + 1], half, k) for k in range(2)]
        )
        adj_ref[group] = jnp.concatenate([left, right], axis=1).astype(bf16)
    cross_out[...] = toward_tile(2 * core, adj_ref, w_ref).astype(bf16)
    pair_out[...] = toward_tile(2 - 2 * core, adj_ref, w_ref).astype(bf16)
    copy.wait()


def own_kernel(
    moment, adj_ref, w_ref, adj_v_ref, v_ref, g_ref, spikes_ref, base_out, gain_out
):
    slope = surrogate(v_ref[...])
    gain = spikes_ref[moment].astype(f32) * (2.0 * slope * (1.0 - slope))
    gain_out[...] = gain
    base_out[...] = (
        adj_v_ref[...] * (0.9 - 0.1 * g_ref[...]) + toward_tile(1, adj_ref, w_ref) * gain
    )


def turn_kernel(*refs):
    (
        near_ref, far_ref, partial_ref, me_ref, entry_ref, w_ref, w_long_ref, v_ref, g_ref,
        decay_ref, adj_v_ref, adj_g_ref,
    ) = refs[:12]
    g_out, source_ref, fetched_ref = refs[12:15]
    acc_refs = refs[25:]
    drive = forward_part(
        near_ref, far_ref, partial_ref, me_ref, entry_ref, w_ref, w_long_ref, source_ref,
        fetched_ref, acc_refs,
    )
    decay = decay_ref[...]
    g_out[...] = decay * g_ref[...] + jax.nn.softplus(drive)
    backward_part(
        adj_g_ref[...], adj_v_ref[...], v_ref[...], jax.nn.sigmoid(drive), decay,
        me_ref, entry_ref, w_ref, w_long_ref, *refs[15:25],
    )


def receive_part(placed_ref, pair_ref, cross_ref, base_ref, gain_ref, wanted_ref, acc_refs):
    half = lane_half(base_ref.shape[0])
    for ref in acc_refs:
        ref[...] = jnp.zeros_like(ref)
    tiles = placed_ref.shape[0]
    for tile in range(tiles):
        arrived = placed_ref[tile].astype(f32)
        for slot in range(CAP):
            number = (slot + CAP * tile) % len(acc_refs)
            acc_refs[number][wanted_ref[CAP * tile + slot]] += arrived
    rest = pair_ref[...].astype(f32) + cross_ref[...].astype(f32)
    rest = rest + jnp.concatenate(folded(acc_refs, half), axis=1)
    return base_ref[...] + rest * gain_ref[...]


def backward_kernel(*refs):
    adj_g_ref, v_ref, gate_ref, decay_ref, me_ref, entry_ref, w_ref, w_long_ref = refs[6:14]
    adj_v_out = refs[14]
    adj_volt = receive_part(*refs[:6], refs[25:])
    adj_v_out[...] = adj_volt
    backward_part(
        adj_g_ref[...], adj_volt, v_ref[...], gate_ref[...], decay_ref[...],
        me_ref, entry_ref, w_ref, w_long_ref, *refs[15:25],
    )


def last_kernel(*refs):
    refs[6][...] = receive_part(*refs[:6], refs[7:])


def grad_kernel(*refs):
    near, far, fetched, adjs, gathered = (refs[k * STEPS : (k + 1) * STEPS] for k in range(5))
    me_ref, cond_ref, local_ref, long_ref, cond_out = refs[5 * STEPS :]
    cond_out[...] = cond_ref[...]
    core = me_ref[0] & 1
    for group in range(adjs[0].shape[0]):
        columns = slice(group * WIDE, (group + 1) * WIDE)
        adj = stacked([ref[group] for ref in adjs])
        for side, sources in (
            (1, [ref[0, group] for ref in near]),
            (2 * core, [ref[1, group] for ref in near]),
            (2 - 2 * core, [ref[group] for ref in far]),
        ):
            total = product_over(stacked(sources)[:, :SIDE], adj)
            local_ref[side, :, columns] = total.astype(bf16)
    for group in range(gathered[0].shape[0]):
        columns = slice(group * WIDE, (group + 1) * WIDE)
        total = product_over(
            stacked([ref[group] for ref in fetched]), stacked([ref[group] for ref in gathered])
        )
        long_ref[:, columns] = (total[:BLK] + total[BLK:]).astype(bf16)


def call(kernel, outs, args, scratch=(), hbm_outs=(), hbm_args=False):
    def spec(space):
        return pl.BlockSpec(memory_space=space)

    vmem, hbm, smem = (spec(space) for space in (pltpu.VMEM, pltpu.HBM, pltpu.SMEM))
    if hbm_args:
        args = [pltpu.with_memory_space_constraint(array, pltpu.HBM) for array in args]
    in_specs = [smem if array.ndim == 1 else hbm if hbm_args else vmem for array in args]
    out_specs = [
        smem if len(shape) == 1 else hbm if number in hbm_outs else vmem
        for number, (shape, _) in enumerate(outs)
    ]
    return pl.pallas_call(
        kernel,
        out_shape=[
            pltpu.SMEM(shape, dtype) if len(shape) == 1 else jax.ShapeDtypeStruct(shape, dtype)
            for shape, dtype in outs
        ],
        in_specs=in_specs,
        out_specs=out_specs,
        scratch_shapes=scratch,
        compiler_params=pltpu.CompilerParams(vmem_limit_bytes=24 * 2**20),
    )(*args)


def local(
    v_init, g_init, spikes, decay, w_local, w_long, lr_src_tile, lr_src_block, lr_tgt_block,
    adj_v_end, adj_g_end,
):
    rows, neurons = v_init.shape
    blocks = neurons // BLK
    tiles = lax.axis_size("azim")
    chips = tiles // 2
    entries = lr_src_tile.shape[0]
    members = [[tile for tile in range(tiles) if in_group(tile) == k] for k in range(2)]
    pair = [(i, i ^ 1) for i in range(tiles)]
    cross = [(i, i + 1) for i in range(1, tiles - 1, 2)]
    cross = cross + [(target, source) for source, target in cross]

    def spread(values):
        near = lax.all_to_all(
            values, "azim", split_axis=0, concat_axis=0, tiled=True, axis_index_groups=members
        )
        return near, lax.ppermute(near, "azim", pair)

    state = ((rows, neurons), f32)
    source = ((blocks // GROUP, GROUP * rows, WIDE), bf16)
    sources = ((2, *source[0]), bf16)
    fetched = ((entries // GROUP, GROUP * rows, LANES), bf16)
    block_row = pltpu.VMEM((blocks, rows, LANES), f32)
    sums = [block_row] * ACCS
    back_scratch = [
        block_row,
        pltpu.VMEM((CAP, tiles, rows, LANES), f32),
        pltpu.VMEM((tiles, rows, LANES), bf16),
        pltpu.SemaphoreType.DMA,
        *sums,
    ]
    back_outs = [
        ((blocks // GROUP, GROUP * rows, WIDE), bf16),
        ((entries // GROUP, GROUP * rows, WIDE), bf16),
        state,
        ((rows, neurons), bf16),
        ((rows, neurons), bf16),
        ((tiles, rows, LANES), bf16),
    ]
    held = (
        v_init, spikes, w_local.reshape(3, SIDE, neurons), w_long, g_init, decay, adj_v_end,
        adj_g_end,
    )
    entry_row = pltpu.SMEM((1, entries), jnp.int32)
    out, me, entry_list, v_start, spikes, w_all, w_long, g_start, decay, adj_volt, adj_cond = call(
        start_kernel,
        [
            ((chips, rows, neurons + LANES), bf16), ((1,), jnp.int32),
            ((FIELDS * entries,), jnp.int32),
        ]
        + [(array.shape, array.dtype) for array in held],
        (lr_src_tile.T, lr_src_block.T, lr_tgt_block.T, *held),
        [
            entry_row, entry_row, entry_row, pltpu.SMEM((tiles,), jnp.int32),
            pltpu.VMEM((chips, rows, LANES), f32),
            pltpu.SemaphoreType.DMA((3 + len(held),)),
        ],
        hbm_args=True,
    )
    voltages, conducts, gates, nears, fars, fetches = [v_start], [g_start], [], [], [], []
    for moment in range(STEPS - 1):
        near, far = spread(out)
        partial, near_t = call(near_kernel, [state, sources], (near, me, w_all))
        nears.append(near_t)
        outs = [state, state, state, source, fetched, ((chips, rows, neurons), bf16)]
        results = call(
            functools.partial(forward_kernel, moment),
            outs,
            (
                near, far, partial, me, entry_list, w_all, w_long, voltages[-1], conducts[-1], decay,
                spikes,
            ),
            sums,
        )
        if moment == 0:
            (wanted,) = call(wanted_kernel, [((CAP * tiles,), jnp.int32)], (near, far, me))
        voltage, conduct, gate, far_t, fetched_t, out = results
        voltages.append(voltage)
        conducts.append(conduct)
        gates.append(gate)
        fars.append(far_t)
        fetches.append(fetched_t)
    near, far = spread(out)
    partial, near_t = call(near_kernel, [state, sources], (near, me, w_all))
    nears.append(near_t)
    conduct, far_t, fetched_t, *back = call(
        turn_kernel,
        [state, source, fetched] + back_outs,
        (
            near, far, partial, me, entry_list, w_all, w_long, voltages[-1], conducts[-1], decay,
            adj_volt, adj_cond,
        ),
        back_scratch,
        hbm_outs=(8,),
    )
    conducts.append(conduct)
    fars.append(far_t)
    fetches.append(fetched_t)
    adjs, gathers = [], []
    for moment in reversed(range(STEPS)):
        adj_t, gathered_t, adj_cond, to_cross, to_pair, placed = back
        adjs.insert(0, adj_t)
        gathers.insert(0, gathered_t)
        arrived = lax.all_to_all(placed, "azim", split_axis=0, concat_axis=0, tiled=True)
        from_cross = lax.ppermute(to_cross, "azim", cross)
        from_pair = lax.ppermute(to_pair, "azim", pair)
        base, gain = call(
            functools.partial(own_kernel, moment),
            [state, state],
            (adj_t, w_all, adj_volt, voltages[moment], conducts[moment + 1], spikes),
        )
        received = (arrived, from_cross, from_pair, base, gain, wanted)
        if moment > 0:
            adj_volt, *back = call(
                backward_kernel,
                [state] + back_outs,
                received
                + (
                    adj_cond, voltages[moment - 1], gates[moment - 1], decay, me, entry_list, w_all,
                    w_long,
                ),
                back_scratch,
                hbm_outs=(6,),
            )
    grad_local, grad_long, adj_cond = call(
        grad_kernel,
        [((3, SIDE, neurons), bf16), ((BLK, entries * BLK), bf16), state],
        (*nears, *fars, *fetches, *adjs, *gathers, me, adj_cond),
    )
    (adj_volt,) = call(last_kernel, [state], received, sums)
    return (adj_volt, adj_cond, grad_local.reshape(9, BLK, neurons), grad_long)


def solution(mesh):
    return jax.shard_map(
        local,
        mesh=mesh,
        in_specs=(
            P("groups", "azim"),
            P("groups", "azim"),
            P(None, "groups", "azim"),
            P("groups", "azim"),
            P("groups", None, "azim"),
            P("groups", "azim"),
            P("azim", "groups"),
            P("azim", "groups"),
            P("azim", "groups"),
            P("groups", "azim"),
            P("groups", "azim"),
        ),
        out_specs=(
            P("groups", "azim"),
            P("groups", "azim"),
            P("groups", None, "azim"),
            P("groups", "azim"),
        ),
        check_vma=False,
    )
```

```python
import functools

import jax
import jax.numpy as jnp
from jax import lax
from jax.experimental import pallas as pl
from jax.experimental.pallas import tpu as pltpu
from jax.sharding import PartitionSpec as P

BLK = 64
CAP = 2
STEPS = 4
LANES = 128
GROUP = 4
WIDE = GROUP * BLK
SIDE = 3 * BLK

f32 = jnp.float32
bf16 = jnp.bfloat16


def surrogate(voltage):
    return jax.nn.sigmoid(2.0 * (voltage - 1.0))


def lane_half(rows):
    return lax.broadcasted_iota(jnp.int32, (rows, LANES), 1) // BLK


def half_only(piece, half, which):
    return jnp.where(half == which, piece, 0.0)


def half_pair(first, second, half):
    return jnp.where(half == 0, first, second)


def swapped(piece):
    return pltpu.roll(piece, BLK, 1)


def chunks_of(values):
    return [values[:, c * LANES : (c + 1) * LANES] for c in range(values.shape[1] // LANES)]


def odd_chunks(chunks, half):
    turned = [swapped(piece) for piece in chunks]
    zero = jnp.zeros_like(chunks[0])
    return [
        half_pair(left, right, half) for left, right in zip([zero] + turned, turned + [zero])
    ]


def product(left, right):
    return lax.dot_general(left, right, (((1,), (0,)), ((), ())), preferred_element_type=f32)


def product_back(left, right):
    return lax.dot_general(left, right, (((1,), (1,)), ((), ())), preferred_element_type=f32)


def product_over(left, right):
    return lax.dot_general(left, right, (((0,), (0,)), ((), ())), preferred_element_type=f32)


def stacked(pieces):
    return jnp.concatenate(pieces, axis=0)


def folded(acc_refs, half):
    chunks = []
    for block in range(0, acc_refs[0].shape[0], 2):
        (low, low_next), (high, high_next) = (
            (sum(ref[block] for ref in refs), sum(ref[block + 1] for ref in refs))
            for refs in (acc_refs[0::2], acc_refs[1::2])
        )
        chunks.append(half_pair(low, high_next, half) + swapped(half_pair(low_next, high, half)))
    return chunks


def in_group(tile):
    return (tile ^ (tile >> 1)) & 1


ACCS = 4


def sublane_half(rows, lanes):
    return lax.broadcasted_iota(jnp.int32, (rows, lanes), 0) // (rows // 2)


def turned(values):
    return pltpu.roll(values, values.shape[0] // 2, 0)


def row_halves(upper, lower):
    return jnp.where(sublane_half(*upper.shape) == 0, upper, lower)


def tile_rows(lanes, rows=GROUP * 8):
    return (lax.broadcasted_iota(jnp.int32, (rows, lanes), 0) // 4) % 2


def copied(pairs, sems):
    copies = [
        pltpu.make_async_copy(source, target, sems.at[number])
        for number, (source, target) in enumerate(pairs)
    ]
    for copy in copies:
        copy.start()
    return copies


def start_kernel(*refs):
    ins, (keep_out, send_out), scratch = refs[:9], refs[9:11], refs[11:]
    kept, sems = scratch[:-1], scratch[-1]
    copies = copied(zip(ins, kept), sems)
    v, spikes, g, adj_v, adj_g, decay, tile_ref, block_ref, target_ref = kept
    rows, neurons = v.shape
    entries = tile_ref.shape[1]
    half = in_group(lax.axis_index("azim"))
    for copy in copies:
        copy.wait()
    across = lax.broadcasted_iota(jnp.int32, (entries, entries), 1)
    down = lax.broadcasted_iota(jnp.int32, (entries, entries), 0)
    tiles = tile_ref[...]
    tiles_down = jnp.sum(
        jnp.where(across == down, tiles.astype(f32), 0.0), axis=1, keepdims=True
    ).astype(jnp.int32)
    earlier = (tiles_down == tiles) & (down < across)
    rank = jnp.sum(jnp.where(earlier, 1.0, 0.0), axis=0, keepdims=True).astype(jnp.int32)
    code = ((tiles * CAP + rank) * 16 + target_ref[...]) * 16 + block_ref[...]
    pairs = ((v[...], g[...]), (adj_v[...], adj_g[...])) + tuple(
        (spikes[k].astype(f32), spikes[k + 1].astype(f32)) for k in range(0, STEPS, 2)
    )
    for number, (first, second) in enumerate(pairs):
        straight = row_halves(first, turned(second))
        crossed = row_halves(turned(first), second)
        keep_out[number] = jnp.where(half == 0, straight, crossed)
        send_out[number] = jnp.where(half == 0, crossed, straight)
    for out in (keep_out, send_out):
        out[len(pairs)] = jnp.zeros((rows, neurons), f32)
        out[len(pairs), 0:1, :] = decay[...]
        out[len(pairs), 1:2, :entries] = code.astype(f32)


def hold_kernel(w_ref, w_long_ref, w_out, w_long_out, sems):
    for copy in copied(((w_ref, w_out), (w_long_ref, w_long_out)), sems):
        copy.wait()


def merge_kernel(
    keep_ref, got_ref, out_ref, v_out, g_out, adj_v_out, adj_g_out, spikes_out, decay_out,
    entry_out, fields_ref, sem,
):
    core = lax.axis_index("azim") & 1
    rows, neurons = v_out.shape
    first = [jnp.where(core == 0, keep_ref[k], got_ref[k]) for k in range(keep_ref.shape[0])]
    second = [jnp.where(core == 0, got_ref[k], keep_ref[k]) for k in range(keep_ref.shape[0])]
    lanes = fields_ref.shape[1] // 2
    for at, block in enumerate((keep_ref[len(first) - 1], got_ref[len(first) - 1])):
        code = block[1:2, :lanes].astype(jnp.int32)
        columns = slice(at * lanes, (at + 1) * lanes)
        fields = (
            code >> 10, ((code & 15) >> 1) * LANES, (code >> 9) & 1, code & 1, (code >> 4) & 15,
            code >> 9, (code >> 8) & 1, code & 15,
        )
        fields_ref[:, columns] = jnp.concatenate(fields, axis=0)
    copy = pltpu.make_async_copy(fields_ref, entry_out, sem)
    copy.start()
    merged = []
    for low, high in zip(first[:-1], second[:-1]):
        merged += [row_halves(low, turned(high)), row_halves(turned(low), high)]
    v, g, adj_v, adj_g, *spikes = merged
    activity = (spikes[0] * surrogate(v)).astype(bf16)
    for chip in range(out_ref.shape[0]):
        out_ref[chip] = activity
    v_out[...] = v
    g_out[...] = g
    adj_v_out[...] = adj_v
    adj_g_out[...] = adj_g
    for moment, spiking in enumerate(spikes):
        spikes_out[moment] = spiking
    decay_out[...] = row_halves(
        jnp.broadcast_to(first[-1][0:1, :], (rows, neurons)),
        jnp.broadcast_to(second[-1][0:1, :], (rows, neurons)),
    )
    copy.wait()


def entry_index(entry_ref, role, entry):
    return role * (entry_ref.shape[1] // 2) + entry


def forward_part(
    near_ref, entry_ref, w_ref, w_mate_ref, w_long_ref, w_long_mate_ref, source_ref, fetched_ref,
    acc_refs,
):
    chips, rows, _ = near_ref.shape
    neurons = w_ref.shape[2]
    blocks = neurons // BLK
    half = lane_half(rows)
    me = lax.axis_index("azim")
    chip = me >> 1
    core = me & 1
    for ref in acc_refs:
        ref[...] = jnp.zeros_like(ref)
    groups = fetched_ref.shape[0] // 2
    row_half = sublane_half(rows, LANES)
    for role, long_ref in enumerate((w_long_ref, w_long_mate_ref)):
        own_row = core if role == 0 else 1 - core
        for group in range(groups):
            pieces, targets = [], []
            for entry in range(GROUP * group, GROUP * (group + 1)):
                at = entry_index(entry_ref, role, entry)
                lanes = pl.ds(pl.multiple_of(entry_ref[1, at], LANES), LANES)
                piece = near_ref[entry_ref[0, at], :, lanes].astype(f32)
                piece = jnp.where(entry_ref[2, at] == own_row, piece, turned(piece))
                chosen = (row_half == own_row) & (half == entry_ref[3, at])
                pieces.append(jnp.where(chosen, piece, 0.0))
                targets.append(entry_ref[4, at])
            fetched = stacked(pieces).astype(bf16)
            fetched_ref[role * groups + group] = fetched
            weights = long_ref[:, group * WIDE : (group + 1) * WIDE]
            total = product(fetched, stacked([weights, weights]))
            for at, target in enumerate(targets):
                lanes = slice(at // 2 * LANES, (at // 2 + 1) * LANES)
                acc_refs[(at + 2 * group) % len(acc_refs)][target] += total[
                    at * rows : (at + 1) * rows, lanes
                ]
    own = near_ref[chip, :, :neurons].astype(f32)
    left = near_ref[jnp.maximum(chip - 1, 0), :, :neurons].astype(f32)
    right = near_ref[jnp.minimum(chip + 1, chips - 1), :, :neurons].astype(f32)
    left = jnp.where(chip > 0, turned(left), 0.0)
    right = jnp.where(chip < chips - 1, turned(right), 0.0)
    sides = (row_halves(left, turned(own)), own, row_halves(turned(own), right))
    for side, values in enumerate(sides):
        even = chunks_of(values)
        odd = odd_chunks(even, half)
        even = even + [jnp.zeros((rows, LANES), f32)]
        for group in range(blocks // GROUP):
            pieces = []
            for block in range(GROUP * group, GROUP * (group + 1)):
                line = even if block % 2 else odd
                pieces.append((line[block // 2], line[block // 2 + 1]))
            source_ref[side, group] = jnp.concatenate(
                [stacked([piece[k] for piece in pieces]) for k in range(2)], axis=1
            ).astype(bf16)
    own_rows = tile_rows(WIDE) == core
    drive = []
    for group in range(blocks // GROUP):
        columns = slice(group * WIDE, (group + 1) * WIDE)
        totals = []
        for ref in (w_ref, w_mate_ref):
            total = product(source_ref[0, group][:, :SIDE], ref[0, :, columns])
            for side in range(1, 3):
                total = total + product(source_ref[side, group][:, :SIDE], ref[side, :, columns])
            totals.append(total)
        total = jnp.where(own_rows, *totals)
        for pair in range(GROUP // 2):
            lanes = slice(pair * LANES, (pair + 1) * LANES)
            at = 2 * pair * rows
            drive.append(
                half_pair(
                    total[at : at + rows, lanes], total[at + rows : at + 2 * rows, lanes], half
                )
            )
    extra = folded(acc_refs, half)
    return jnp.concatenate([a + b for a, b in zip(drive, extra)], axis=1)


def forward_kernel(moment, *refs):
    near_ref, entry_ref, w_ref, w_mate_ref, w_long_ref, w_long_mate_ref = refs[:6]
    v_ref, g_ref, decay_ref, spikes_ref = refs[6:10]
    v_out, g_out, gate_out, source_ref, fetched_ref, act_ref = refs[10:16]
    acc_refs = refs[16 : 16 + ACCS] if moment != 1 else refs[17 : 17 + ACCS]
    chips = act_ref.shape[0]
    rows, neurons = v_ref.shape
    if moment == 1:
        asked_ref = refs[16]
        for chip in range(chips):
            asked = near_ref[chip, :, neurons:].astype(f32)
            asked_ref[chip : chip + 1, :] = asked[0:1, :].astype(jnp.int32)
    drive = forward_part(
        near_ref, entry_ref, w_ref, w_mate_ref, w_long_ref, w_long_mate_ref, source_ref,
        fetched_ref, acc_refs,
    )
    voltage = v_ref[...]
    conduct = decay_ref[...] * g_ref[...] + jax.nn.softplus(drive)
    voltage = voltage + 0.1 * (conduct * (3.0 - voltage) - voltage) - spikes_ref[moment]
    v_out[...] = voltage
    g_out[...] = conduct
    gate_out[...] = jax.nn.sigmoid(drive)
    activity = (spikes_ref[moment + 1] * surrogate(voltage)).astype(bf16)
    for chip in range(chips):
        act_ref[chip, :, :neurons] = activity
    if moment == 0:
        ask_ref = refs[-1]
        core = lax.axis_index("azim") & 1
        lane = lax.broadcasted_iota(jnp.int32, (rows, LANES), 1)
        ask_ref[...] = jnp.zeros_like(ask_ref)
        for role in range(2):
            own_row = core if role == 0 else 1 - core
            for entry in range(fetched_ref.shape[0] // 2 * GROUP):
                at = entry_index(entry_ref, role, entry)
                place = own_row * 4 + entry_ref[2, at] * CAP + entry_ref[6, at]
                chip = entry_ref[0, at]
                ask_ref[chip] = jnp.where(
                    lane == place, entry_ref[7, at].astype(f32), ask_ref[chip]
                )
        for chip in range(chips):
            act_ref[chip, :, neurons:] = ask_ref[chip].astype(bf16)


def toward_side(side, adj_ref, w_ref, w_mate_ref, own_rows):
    groups, rows, _ = adj_ref.shape
    rows = rows // GROUP
    blocks = groups * GROUP
    half = lane_half(rows)
    zero = jnp.zeros((rows, LANES), f32)
    even = [zero] * (blocks // 2 + 1)
    odd = [zero] * (blocks // 2 + 1)
    for group in range(groups):
        columns = slice(group * WIDE, (group + 1) * WIDE)
        adj = adj_ref[group]
        back = jnp.where(
            own_rows,
            product_back(adj, w_ref[side, :, columns]),
            product_back(adj, w_mate_ref[side, :, columns]),
        )
        for at in range(GROUP):
            block = GROUP * group + at
            line = even if block % 2 else odd
            lower = back[at * rows : (at + 1) * rows, :LANES]
            upper = back[at * rows : (at + 1) * rows, LANES:]
            upper = jnp.concatenate([upper, jnp.zeros_like(upper)], axis=1)
            line[block // 2] = line[block // 2] + lower
            line[block // 2 + 1] = line[block // 2 + 1] + upper
    moved = [swapped(piece) for piece in odd]
    return jnp.concatenate(
        [even[c] + half_pair(moved[c], moved[c + 1], half) for c in range(blocks // 2)], axis=1
    )


def backward_part(
    adj_cond, adj_volt, voltage, gate, decay, entry_ref, w_ref, w_mate_ref, w_long_ref,
    w_long_mate_ref, adj_ref, gathered_ref, cond_out, own_out, placed_out, block_ref, slot_ref,
):
    rows, neurons = voltage.shape
    blocks = neurons // BLK
    chips = placed_out.shape[0]
    half = lane_half(rows)
    me = lax.axis_index("azim")
    chip = me >> 1
    core = me & 1
    total_g = adj_cond + adj_volt * 0.1 * (3.0 - voltage)
    adj_drive = (total_g * gate).astype(bf16).astype(f32)
    cond_out[...] = decay * total_g
    chunks = chunks_of(adj_drive)
    zero = jnp.zeros((rows, LANES), f32)
    for number, piece in enumerate(chunks):
        moved = swapped(piece)
        block_ref[2 * number] = half_pair(piece, moved, half)
        block_ref[2 * number + 1] = half_pair(moved, piece, half)
    slot_ref[...] = jnp.zeros_like(slot_ref)
    groups = gathered_ref.shape[0] // 2
    row_half = sublane_half(rows, LANES)
    for role, long_ref in enumerate((w_long_ref, w_long_mate_ref)):
        own_row = core if role == 0 else 1 - core
        for group in range(groups):
            left, right, slots = [], [], []
            for at in range(GROUP):
                entry = entry_index(entry_ref, role, GROUP * group + at)
                slots.append((entry_ref[6, entry], entry_ref[5, entry]))
                chosen = (row_half == own_row) & (half == at % 2)
                piece = jnp.where(chosen, block_ref[entry_ref[4, entry]], 0.0)
                left.append(piece if at < 2 else zero)
                right.append(zero if at < 2 else piece)
            gathered = jnp.concatenate([stacked(left), stacked(right)], axis=1).astype(bf16)
            gathered_ref[role * groups + group] = gathered
            weights = long_ref[:, group * WIDE : (group + 1) * WIDE]
            back = product_back(gathered, stacked([weights, weights]))
            for at, slot in enumerate(slots):
                slot_ref[slot] += back[at * rows : (at + 1) * rows]
    for tile in range(2 * chips):
        lanes = slice(tile % 2 * LANES, (tile % 2 + 1) * LANES)
        placed_out[tile // 2, :, lanes] = half_pair(
            slot_ref[0, tile], slot_ref[1, tile], half
        ).astype(bf16)
    for group in range(blocks // GROUP):
        left = stacked([half_only(chunks[2 * group], half, k) for k in range(2)] + [zero, zero])
        right = stacked(
            [zero, zero] + [half_only(chunks[2 * group + 1], half, k) for k in range(2)]
        )
        adj_ref[group] = jnp.concatenate([left, right], axis=1).astype(bf16)
    own_rows = tile_rows(SIDE) == core
    before, own, after = (
        toward_side(side, adj_ref, w_ref, w_mate_ref, own_rows) for side in range(3)
    )
    own_out[...] = own + row_halves(turned(before), turned(after))
    middle = neurons // 2
    to_left = row_halves(before[:, :middle], turned(before[:, middle:])).astype(bf16)
    to_right = row_halves(turned(after[:, :middle]), after[:, middle:]).astype(bf16)
    unused = jnp.zeros_like(to_left)
    for other in range(chips):
        placed_out[other, :, 2 * LANES :] = unused
    placed_out[jnp.where(chip > 0, chip - 1, chip), :, 2 * LANES :] = to_left
    placed_out[jnp.where(chip < chips - 1, chip + 1, chip), :, 2 * LANES :] = to_right


def turn_kernel(*refs):
    near_ref, entry_ref, w_ref, w_mate_ref, w_long_ref, w_long_mate_ref = refs[:6]
    v_ref, g_ref, decay_ref, adj_v_ref, adj_g_ref, asked_ref = refs[6:12]
    g_out, wanted_out, source_ref, fetched_ref = refs[12:16]
    copy = pltpu.make_async_copy(asked_ref, wanted_out, refs[-1])
    copy.start()
    drive = forward_part(
        near_ref, entry_ref, w_ref, w_mate_ref, w_long_ref, w_long_mate_ref, source_ref,
        fetched_ref, refs[23:-1],
    )
    decay = decay_ref[...]
    g_out[...] = decay * g_ref[...] + jax.nn.softplus(drive)
    backward_part(
        adj_g_ref[...], adj_v_ref[...], v_ref[...], jax.nn.sigmoid(drive), decay,
        entry_ref, w_ref, w_mate_ref, w_long_ref, w_long_mate_ref, *refs[16:23],
    )
    copy.wait()


def receive_part(
    moment, placed_ref, own_ref, wanted_ref, adj_v_ref, v_ref, g_ref, spikes_ref, acc_refs
):
    chips, rows, _ = placed_ref.shape
    half = lane_half(rows)
    row_half = sublane_half(rows, LANES)
    chip = lax.axis_index("azim") >> 1
    for ref in acc_refs:
        ref[...] = jnp.zeros_like(ref)
    for other in range(chips):
        for source in range(2):
            arrived = placed_ref[other, :, source * LANES : (source + 1) * LANES].astype(f32)
            for target, piece in ((source, arrived), (1 - source, turned(arrived))):
                piece = jnp.where(row_half == source, piece, 0.0)
                for slot in range(CAP):
                    number = (slot + CAP * target) % len(acc_refs)
                    block = wanted_ref[other, target * 4 + source * CAP + slot]
                    acc_refs[number][block] += piece
    left = placed_ref[jnp.maximum(chip - 1, 0), :, 2 * LANES :].astype(f32)
    right = placed_ref[jnp.minimum(chip + 1, chips - 1), :, 2 * LANES :].astype(f32)
    left = jnp.where(chip > 0, left, 0.0)
    right = jnp.where(chip < chips - 1, right, 0.0)
    beside = row_halves(
        jnp.concatenate([left, turned(left)], axis=1),
        jnp.concatenate([turned(right), right], axis=1),
    )
    adj_act = own_ref[...] + beside + jnp.concatenate(folded(acc_refs, half), axis=1)
    slope = surrogate(v_ref[...])
    slope = 2.0 * slope * (1.0 - slope)
    return adj_v_ref[...] * (0.9 - 0.1 * g_ref[...]) + adj_act * spikes_ref[moment] * slope


def backward_kernel(moment, *refs):
    adj_g_ref, v_ref, gate_ref, decay_ref, entry_ref = refs[7:12]
    weights = refs[12:16]
    adj_v_out = refs[16]
    adj_volt = receive_part(moment, *refs[:7], refs[24:])
    adj_v_out[...] = adj_volt
    backward_part(
        adj_g_ref[...], adj_volt, v_ref[...], gate_ref[...], decay_ref[...],
        entry_ref, *weights, *refs[17:24],
    )


def last_kernel(*refs):
    refs[8][0] = receive_part(0, *refs[:7], refs[9:])
    refs[8][1] = refs[7][...]


def end_kernel(last_ref, got_ref, *outs):
    me = lax.axis_index("azim")
    core = me & 1
    half = in_group(me)
    for number, out in enumerate(outs):
        keep, got = last_ref[number], got_ref[number]
        keep = jnp.where(half == core, keep, turned(keep))
        got = jnp.where(half == core, turned(got), got)
        out[...] = jnp.where(half == 0, row_halves(keep, got), row_halves(got, keep))


def grad_kernel(*refs):
    sources, fetched, adjs, gathered = (refs[k * STEPS : (k + 1) * STEPS] for k in range(4))
    outs = refs[4 * STEPS :]
    core = lax.axis_index("azim") & 1
    row_tile = tile_rows(WIDE, STEPS * GROUP * 8)
    for role, out in enumerate(outs):
        chosen = row_tile == (core if role == 0 else 1 - core)
        for group in range(adjs[0].shape[0]):
            columns = slice(group * WIDE, (group + 1) * WIDE)
            adj = stacked([ref[group] for ref in adjs])
            adj = jnp.where(chosen, adj.astype(f32), 0.0).astype(bf16)
            for side in range(3):
                source = stacked([ref[side, group] for ref in sources])
                total = product_over(source[:, :SIDE], adj)
                out[side * SIDE : (side + 1) * SIDE, columns] = total.astype(bf16)
        groups = gathered[0].shape[0] // 2
        for group in range(groups):
            at = role * groups + group
            total = product_over(
                stacked([ref[at] for ref in fetched]), stacked([ref[at] for ref in gathered])
            )
            fold, place = divmod(group * WIDE, out.shape[1])
            first = 3 * SIDE + fold * BLK
            out[first : first + BLK, place : place + WIDE] = (total[:BLK] + total[BLK:]).astype(bf16)


def add_kernel(own_ref, got_ref, local_out, long_out):
    total = own_ref[...].astype(f32) + got_ref[...].astype(f32)
    width = own_ref.shape[1]
    local_out[...] = total[: 3 * SIDE].astype(bf16)
    for fold in range(long_out.shape[1] // width):
        first = 3 * SIDE + fold * BLK
        long_out[:, fold * width : (fold + 1) * width] = total[first : first + BLK].astype(bf16)


def call(kernel, outs, args, scratch=(), hbm_args=(), smem_args=(), smem_outs=(), flops=None):
    def spec(space):
        return pl.BlockSpec(memory_space=space)

    vmem, hbm, smem = (spec(space) for space in (pltpu.VMEM, pltpu.HBM, pltpu.SMEM))
    args = [
        pltpu.with_memory_space_constraint(array, pltpu.HBM) if number in hbm_args else array
        for number, array in enumerate(args)
    ]
    return pl.pallas_call(
        kernel,
        out_shape=[
            pltpu.SMEM(shape, dtype) if number in smem_outs else jax.ShapeDtypeStruct(shape, dtype)
            for number, (shape, dtype) in enumerate(outs)
        ],
        in_specs=[
            smem if number in smem_args else hbm if number in hbm_args else vmem
            for number in range(len(args))
        ],
        out_specs=[smem if number in smem_outs else vmem for number in range(len(outs))],
        scratch_shapes=scratch,
        compiler_params=pltpu.CompilerParams(vmem_limit_bytes=24 * 2**20),
        cost_estimate=flops and pl.CostEstimate(flops=flops, bytes_accessed=0, transcendentals=0),
    )(*args)


def local(
    v_init, g_init, spikes, decay, w_local, w_long, lr_src_tile, lr_src_block, lr_tgt_block,
    adj_v_end, adj_g_end,
):
    rows, neurons = v_init.shape
    blocks = neurons // BLK
    tiles = lax.axis_size("azim")
    chips = tiles // 2
    entries = lr_src_tile.shape[0]
    members = [[tile for tile in range(tiles) if in_group(tile) == k] for k in range(2)]
    pair = [(i, i ^ 1) for i in range(tiles)]

    def spread(values):
        return lax.all_to_all(
            values, "azim", split_axis=0, concat_axis=0, tiled=True, axis_index_groups=members
        )

    state = ((rows, neurons), f32)
    fields = (8, 2 * max(entries, LANES))
    source = ((3, blocks // GROUP, GROUP * rows, WIDE), bf16)
    fetched = ((2 * entries // GROUP, GROUP * rows, LANES), bf16)
    block_row = pltpu.VMEM((blocks, rows, LANES), f32)
    sums = [block_row] * ACCS
    back_scratch = [block_row, pltpu.VMEM((CAP, tiles, rows, LANES), f32), *sums]
    back_outs = [
        ((blocks // GROUP, GROUP * rows, WIDE), bf16),
        ((2 * entries // GROUP, GROUP * rows, WIDE), bf16),
        state,
        state,
        ((chips, rows, 2 * LANES + neurons // 2), bf16),
    ]
    w_sides = w_local.reshape(3, SIDE, neurons)
    w_mate = lax.ppermute(w_sides, "azim", pair)
    w_long_mate = lax.ppermute(w_long, "azim", pair)
    held = (
        v_init, spikes, g_init, adj_v_end, adj_g_end, decay,
        lr_src_tile.T, lr_src_block.T, lr_tgt_block.T,
    )
    pack = ((3 + STEPS // 2, rows, neurons), f32)
    keep, send = call(
        start_kernel,
        [pack, pack],
        held,
        [pltpu.VMEM(array.shape, array.dtype) for array in held]
        + [pltpu.SemaphoreType.DMA((len(held),))],
        hbm_args=range(len(held)),
    )
    w_own, w_long = call(
        hold_kernel,
        [(w_sides.shape, bf16), (w_long.shape, bf16)],
        (w_sides, w_long),
        [pltpu.SemaphoreType.DMA((2,))],
        hbm_args=range(2),
    )
    got = lax.ppermute(send, "azim", pair)
    got, w_mate, w_long_mate, w_own, w_long = lax.optimization_barrier(
        (got, w_mate, w_long_mate, w_own, w_long)
    )
    out, v_start, g_start, adj_volt, adj_cond, spikes, decay, entry_list = call(
        merge_kernel,
        [((chips, rows, neurons), bf16)]
        + [state] * 4
        + [((STEPS, rows, neurons), f32), state, (fields, jnp.int32)],
        (keep, got),
        [pltpu.VMEM(fields, jnp.int32), pltpu.SemaphoreType.DMA],
        smem_outs=(7,),
    )
    weights = (w_own, w_mate, w_long, w_long_mate)
    voltages, conducts, gates, sources, fetches = [v_start], [g_start], [], [], []
    for moment in range(STEPS - 1):
        near = spread(out)
        width = neurons + LANES if moment == 0 else neurons
        outs = [state, state, state, source, fetched, ((chips, rows, width), bf16)]
        scratch = list(sums)
        if moment == 0:
            scratch.append(pltpu.VMEM((chips, rows, LANES), f32))
        if moment == 1:
            outs.append(((chips, LANES), jnp.int32))
        voltage, conduct, gate, source_t, fetched_t, out, *asked = call(
            functools.partial(forward_kernel, moment),
            outs,
            (near, entry_list, *weights, voltages[-1], conducts[-1], decay, spikes),
            scratch,
            smem_args=(1,),
        )
        if moment == 1:
            (asked_blocks,) = asked
        voltages.append(voltage)
        conducts.append(conduct)
        gates.append(gate)
        sources.append(source_t)
        fetches.append(fetched_t)
    near = spread(out)
    conduct, wanted, source_t, fetched_t, *back = call(
        turn_kernel,
        [state, ((chips, LANES), jnp.int32), source, fetched] + back_outs,
        (
            near, entry_list, *weights, voltages[-1], conducts[-1], decay, adj_volt, adj_cond,
            asked_blocks,
        ),
        back_scratch + [pltpu.SemaphoreType.DMA],
        smem_args=(1,),
        smem_outs=(1,),
    )
    conducts.append(conduct)
    sources.append(source_t)
    fetches.append(fetched_t)
    adjs, gathers = [], []
    for moment in reversed(range(STEPS)):
        adj_t, gathered_t, adj_cond, own, placed = back
        adjs.insert(0, adj_t)
        gathers.insert(0, gathered_t)
        received = (
            spread(placed), own, wanted, adj_volt, voltages[moment], conducts[moment + 1], spikes,
        )
        if moment > 0:
            adj_volt, *back = call(
                functools.partial(backward_kernel, moment),
                [state] + back_outs,
                received
                + (
                    adj_cond, voltages[moment - 1], gates[moment - 1], decay, entry_list, *weights,
                ),
                back_scratch,
                smem_args=(2, 11),
            )
    grads = ((3 * SIDE + entries * BLK * BLK // neurons, neurons), bf16)
    grads_own, grads_mate = call(
        grad_kernel, [grads, grads], (*sources, *fetches, *adjs, *gathers)
    )
    got_grads = lax.ppermute(grads_mate, "azim", pair)
    (last,) = call(
        last_kernel, [((2, rows, neurons), f32)], (*received, adj_cond), sums, smem_args=(2,)
    )
    got_last = lax.ppermute(last, "azim", pair)
    grad_local, grad_long = call(
        add_kernel,
        [((3 * SIDE, neurons), bf16), ((BLK, entries * BLK), bf16)],
        (grads_own, got_grads),
        flops=10**10,
    )
    got_last, grad_local, grad_long = lax.optimization_barrier((got_last, grad_local, grad_long))
    adj_volt, adj_cond = call(end_kernel, [state, state], (last, got_last))
    return (adj_volt, adj_cond, grad_local.reshape(9, BLK, neurons), grad_long)


def solution(mesh):
    return jax.shard_map(
        local,
        mesh=mesh,
        in_specs=(
            P("groups", "azim"),
            P("groups", "azim"),
            P(None, "groups", "azim"),
            P("groups", "azim"),
            P("groups", None, "azim"),
            P("groups", "azim"),
            P("azim", "groups"),
            P("azim", "groups"),
            P("azim", "groups"),
            P("groups", "azim"),
            P("groups", "azim"),
        ),
        out_specs=(
            P("groups", "azim"),
            P("groups", "azim"),
            P("groups", None, "azim"),
            P("groups", "azim"),
        ),
        check_vma=False,
    )
```

```python
import functools

import jax
import jax.numpy as jnp
from jax import lax
from jax.experimental import pallas as pl
from jax.experimental.pallas import tpu as pltpu
from jax.sharding import PartitionSpec as P

BLK = 64
CAP = 2
STEPS = 4
LANES = 128
GROUP = 4
WIDE = GROUP * BLK
SIDE = 3 * BLK

f32 = jnp.float32
bf16 = jnp.bfloat16


def surrogate(voltage):
    return jax.nn.sigmoid(2.0 * (voltage - 1.0))


def lane_half(rows):
    return lax.broadcasted_iota(jnp.int32, (rows, LANES), 1) // BLK


def half_only(piece, half, which):
    return jnp.where(half == which, piece, 0.0)


def half_pair(first, second, half):
    return jnp.where(half == 0, first, second)


def swapped(piece):
    return pltpu.roll(piece, BLK, 1)


def chunks_of(values):
    return [values[:, c * LANES : (c + 1) * LANES] for c in range(values.shape[1] // LANES)]


def odd_chunks(chunks, half):
    turned = [swapped(piece) for piece in chunks]
    zero = jnp.zeros_like(chunks[0])
    return [
        half_pair(left, right, half) for left, right in zip([zero] + turned, turned + [zero])
    ]


def product(left, right):
    return lax.dot_general(left, right, (((1,), (0,)), ((), ())), preferred_element_type=f32)


def product_back(left, right):
    return lax.dot_general(left, right, (((1,), (1,)), ((), ())), preferred_element_type=f32)


def product_over(left, right):
    return lax.dot_general(left, right, (((0,), (0,)), ((), ())), preferred_element_type=f32)


def stacked(pieces):
    return jnp.concatenate(pieces, axis=0)


def folded(acc_refs, half):
    chunks = []
    for block in range(0, acc_refs[0].shape[0], 2):
        (low, low_next), (high, high_next) = (
            (sum(ref[block] for ref in refs), sum(ref[block + 1] for ref in refs))
            for refs in (acc_refs[0::2], acc_refs[1::2])
        )
        chunks.append(half_pair(low, high_next, half) + swapped(half_pair(low_next, high, half)))
    return chunks


def in_group(tile):
    return (tile ^ (tile >> 1)) & 1


ACCS = 4


def sublane_half(rows, lanes):
    return lax.broadcasted_iota(jnp.int32, (rows, lanes), 0) // (rows // 2)


def turned(values):
    return pltpu.roll(values, values.shape[0] // 2, 0)


def row_halves(upper, lower):
    return jnp.where(sublane_half(*upper.shape) == 0, upper, lower)


def tile_rows(lanes, rows=GROUP * 8):
    return (lax.broadcasted_iota(jnp.int32, (rows, lanes), 0) // 4) % 2


def copied(pairs, sems):
    copies = [
        pltpu.make_async_copy(source, target, sems.at[number])
        for number, (source, target) in enumerate(pairs)
    ]
    for copy in copies:
        copy.start()
    return copies


def start_kernel(*refs):
    ins, (keep_out, send_out), scratch = refs[:9], refs[9:11], refs[11:]
    kept, sems = scratch[:-1], scratch[-1]
    copies = copied(zip(ins, kept), sems)
    v, spikes, g, adj_v, adj_g, decay, tile_ref, block_ref, target_ref = kept
    rows, neurons = v.shape
    entries = tile_ref.shape[1]
    half = in_group(lax.axis_index("azim"))
    for copy in copies:
        copy.wait()
    across = lax.broadcasted_iota(jnp.int32, (entries, entries), 1)
    down = lax.broadcasted_iota(jnp.int32, (entries, entries), 0)
    tiles = tile_ref[...]
    tiles_down = jnp.sum(
        jnp.where(across == down, tiles.astype(f32), 0.0), axis=1, keepdims=True
    ).astype(jnp.int32)
    earlier = (tiles_down == tiles) & (down < across)
    rank = jnp.sum(jnp.where(earlier, 1.0, 0.0), axis=0, keepdims=True).astype(jnp.int32)
    code = ((tiles * CAP + rank) * 16 + target_ref[...]) * 16 + block_ref[...]
    pairs = ((v[...], g[...]), (adj_v[...], adj_g[...])) + tuple(
        (spikes[k].astype(f32), spikes[k + 1].astype(f32)) for k in range(0, STEPS, 2)
    )
    for number, (first, second) in enumerate(pairs):
        straight = row_halves(first, turned(second))
        crossed = row_halves(turned(first), second)
        keep_out[number] = jnp.where(half == 0, straight, crossed)
        send_out[number] = jnp.where(half == 0, crossed, straight)
    for out in (keep_out, send_out):
        out[len(pairs)] = jnp.zeros((rows, neurons), f32)
        out[len(pairs), 0:1, :] = decay[...]
        out[len(pairs), 1:2, :entries] = code.astype(f32)


def hold_kernel(w_ref, w_long_ref, w_out, w_long_out, sems):
    for copy in copied(((w_ref, w_out), (w_long_ref, w_long_out)), sems):
        copy.wait()


def merge_kernel(
    keep_ref, got_ref, out_ref, v_out, g_out, adj_v_out, adj_g_out, spikes_out, decay_out,
    fields_ref,
):
    core = lax.axis_index("azim") & 1
    rows, neurons = v_out.shape
    first = [jnp.where(core == 0, keep_ref[k], got_ref[k]) for k in range(keep_ref.shape[0])]
    second = [jnp.where(core == 0, got_ref[k], keep_ref[k]) for k in range(keep_ref.shape[0])]
    lanes = fields_ref.shape[1] // 2
    for at, block in enumerate((keep_ref[len(first) - 1], got_ref[len(first) - 1])):
        code = block[1:2, :lanes].astype(jnp.int32)
        columns = slice(at * lanes, (at + 1) * lanes)
        fields = (
            code >> 10, ((code & 15) >> 1) * LANES, (code >> 9) & 1, code & 1, (code >> 4) & 15,
            code >> 9, (code >> 8) & 1, code & 15,
        )
        fields_ref[:, columns] = jnp.concatenate(fields, axis=0)
    merged = []
    for low, high in zip(first[:-1], second[:-1]):
        merged += [row_halves(low, turned(high)), row_halves(turned(low), high)]
    v, g, adj_v, adj_g, *spikes = merged
    activity = (spikes[0] * surrogate(v)).astype(bf16)
    for chip in range(out_ref.shape[0]):
        out_ref[chip] = activity
    v_out[...] = v
    g_out[...] = g
    adj_v_out[...] = adj_v
    adj_g_out[...] = adj_g
    for moment, spiking in enumerate(spikes):
        spikes_out[moment] = spiking
    decay_out[...] = row_halves(
        jnp.broadcast_to(first[-1][0:1, :], (rows, neurons)),
        jnp.broadcast_to(second[-1][0:1, :], (rows, neurons)),
    )


def entry_index(entry_ref, role, entry):
    return role * (entry_ref.shape[1] // 2) + entry


def forward_part(
    near_ref, entry_ref, w_ref, w_mate_ref, w_long_ref, w_long_mate_ref, source_ref, fetched_ref,
    acc_refs, ready=None,
):
    chips, rows, _ = near_ref.shape
    neurons = w_ref.shape[2]
    blocks = neurons // BLK
    half = lane_half(rows)
    me = lax.axis_index("azim")
    chip = me >> 1
    core = me & 1
    for ref in acc_refs:
        ref[...] = jnp.zeros_like(ref)
    def local_part():
        own = near_ref[chip, :, :neurons].astype(f32)
        left = near_ref[jnp.maximum(chip - 1, 0), :, :neurons].astype(f32)
        right = near_ref[jnp.minimum(chip + 1, chips - 1), :, :neurons].astype(f32)
        left = jnp.where(chip > 0, turned(left), 0.0)
        right = jnp.where(chip < chips - 1, turned(right), 0.0)
        sides = (row_halves(left, turned(own)), own, row_halves(turned(own), right))
        for side, values in enumerate(sides):
            even = chunks_of(values)
            odd = odd_chunks(even, half)
            even = even + [jnp.zeros((rows, LANES), f32)]
            for group in range(blocks // GROUP):
                pieces = []
                for block in range(GROUP * group, GROUP * (group + 1)):
                    line = even if block % 2 else odd
                    pieces.append((line[block // 2], line[block // 2 + 1]))
                source_ref[side, group] = jnp.concatenate(
                    [stacked([piece[k] for piece in pieces]) for k in range(2)], axis=1
                ).astype(bf16)
        own_rows = tile_rows(WIDE) == core
        drive = []
        for group in range(blocks // GROUP):
            columns = slice(group * WIDE, (group + 1) * WIDE)
            totals = []
            for ref in (w_ref, w_mate_ref):
                total = product(source_ref[0, group][:, :SIDE], ref[0, :, columns])
                for side in range(1, 3):
                    total = total + product(source_ref[side, group][:, :SIDE], ref[side, :, columns])
                totals.append(total)
            total = jnp.where(own_rows, *totals)
            for pair in range(GROUP // 2):
                lanes = slice(pair * LANES, (pair + 1) * LANES)
                at = 2 * pair * rows
                drive.append(
                    half_pair(
                        total[at : at + rows, lanes], total[at + rows : at + 2 * rows, lanes], half
                    )
                )
        return drive

    def long_part():
        groups = fetched_ref.shape[0] // 2
        row_half = sublane_half(rows, LANES)
        for role, long_ref in enumerate((w_long_ref, w_long_mate_ref)):
            own_row = core if role == 0 else 1 - core
            for group in range(groups):
                pieces, targets = [], []
                for entry in range(GROUP * group, GROUP * (group + 1)):
                    at = entry_index(entry_ref, role, entry)
                    lanes = pl.ds(pl.multiple_of(entry_ref[1, at], LANES), LANES)
                    piece = near_ref[entry_ref[0, at], :, lanes].astype(f32)
                    piece = jnp.where(entry_ref[2, at] == own_row, piece, turned(piece))
                    chosen = (row_half == own_row) & (half == entry_ref[3, at])
                    pieces.append(jnp.where(chosen, piece, 0.0))
                    targets.append(entry_ref[4, at])
                fetched = stacked(pieces).astype(bf16)
                fetched_ref[role * groups + group] = fetched
                weights = long_ref[:, group * WIDE : (group + 1) * WIDE]
                total = product(fetched, stacked([weights, weights]))
                for at, target in enumerate(targets):
                    lanes = slice(at // 2 * LANES, (at // 2 + 1) * LANES)
                    acc_refs[(at + 2 * group) % len(acc_refs)][target] += total[
                        at * rows : (at + 1) * rows, lanes
                    ]

    if ready is None:
        long_part()
        drive = local_part()
    else:
        drive = local_part()
        ready.wait()
        long_part()
    extra = folded(acc_refs, half)
    return jnp.concatenate([a + b for a, b in zip(drive, extra)], axis=1)


def forward_kernel(moment, *refs):
    near_ref, entry_ref, w_ref, w_mate_ref, w_long_ref, w_long_mate_ref = refs[:6]
    v_ref, g_ref, decay_ref, spikes_ref = refs[6:10]
    v_out, g_out, gate_out, source_ref, fetched_ref, act_ref = refs[10:16]
    acc_refs = refs[16 : 16 + ACCS] if moment == 2 else refs[17 : 17 + ACCS]
    ready = None
    if moment == 0:
        ready = pltpu.make_async_copy(entry_ref, refs[16], refs[-1])
        ready.start()
        entry_ref = refs[16]
    chips = act_ref.shape[0]
    rows, neurons = v_ref.shape
    if moment == 1:
        asked_ref = refs[16]
        for chip in range(chips):
            asked = near_ref[chip, :, neurons:].astype(f32)
            asked_ref[chip : chip + 1, :] = asked[0:1, :].astype(jnp.int32)
    drive = forward_part(
        near_ref, entry_ref, w_ref, w_mate_ref, w_long_ref, w_long_mate_ref, source_ref,
        fetched_ref, acc_refs, ready,
    )
    voltage = v_ref[...]
    conduct = decay_ref[...] * g_ref[...] + jax.nn.softplus(drive)
    voltage = voltage + 0.1 * (conduct * (3.0 - voltage) - voltage) - spikes_ref[moment]
    v_out[...] = voltage
    g_out[...] = conduct
    gate_out[...] = jax.nn.sigmoid(drive)
    activity = (spikes_ref[moment + 1] * surrogate(voltage)).astype(bf16)
    for chip in range(chips):
        act_ref[chip, :, :neurons] = activity
    if moment == 0:
        ask_ref = refs[-2]
        core = lax.axis_index("azim") & 1
        lane = lax.broadcasted_iota(jnp.int32, (rows, LANES), 1)
        ask_ref[...] = jnp.zeros_like(ask_ref)
        for role in range(2):
            own_row = core if role == 0 else 1 - core
            for entry in range(fetched_ref.shape[0] // 2 * GROUP):
                at = entry_index(entry_ref, role, entry)
                place = own_row * 4 + entry_ref[2, at] * CAP + entry_ref[6, at]
                chip = entry_ref[0, at]
                ask_ref[chip] = jnp.where(
                    lane == place, entry_ref[7, at].astype(f32), ask_ref[chip]
                )
        for chip in range(chips):
            act_ref[chip, :, neurons:] = ask_ref[chip].astype(bf16)


def toward_side(side, adj_ref, w_ref, w_mate_ref, own_rows):
    groups, rows, _ = adj_ref.shape
    rows = rows // GROUP
    blocks = groups * GROUP
    half = lane_half(rows)
    zero = jnp.zeros((rows, LANES), f32)
    even = [zero] * (blocks // 2 + 1)
    odd = [zero] * (blocks // 2 + 1)
    for group in range(groups):
        columns = slice(group * WIDE, (group + 1) * WIDE)
        adj = adj_ref[group]
        back = jnp.where(
            own_rows,
            product_back(adj, w_ref[side, :, columns]),
            product_back(adj, w_mate_ref[side, :, columns]),
        )
        for at in range(GROUP):
            block = GROUP * group + at
            line = even if block % 2 else odd
            lower = back[at * rows : (at + 1) * rows, :LANES]
            upper = back[at * rows : (at + 1) * rows, LANES:]
            upper = jnp.concatenate([upper, jnp.zeros_like(upper)], axis=1)
            line[block // 2] = line[block // 2] + lower
            line[block // 2 + 1] = line[block // 2 + 1] + upper
    moved = [swapped(piece) for piece in odd]
    return jnp.concatenate(
        [even[c] + half_pair(moved[c], moved[c + 1], half) for c in range(blocks // 2)], axis=1
    )


def backward_part(
    adj_cond, adj_volt, voltage, gate, decay, entry_ref, w_ref, w_mate_ref, w_long_ref,
    w_long_mate_ref, adj_ref, gathered_ref, cond_out, own_out, placed_out, block_ref, slot_ref,
):
    rows, neurons = voltage.shape
    blocks = neurons // BLK
    chips = placed_out.shape[0]
    half = lane_half(rows)
    me = lax.axis_index("azim")
    chip = me >> 1
    core = me & 1
    total_g = adj_cond + adj_volt * 0.1 * (3.0 - voltage)
    adj_drive = (total_g * gate).astype(bf16).astype(f32)
    cond_out[...] = decay * total_g
    chunks = chunks_of(adj_drive)
    zero = jnp.zeros((rows, LANES), f32)
    for number, piece in enumerate(chunks):
        moved = swapped(piece)
        block_ref[2 * number] = half_pair(piece, moved, half)
        block_ref[2 * number + 1] = half_pair(moved, piece, half)
    slot_ref[...] = jnp.zeros_like(slot_ref)
    groups = gathered_ref.shape[0] // 2
    row_half = sublane_half(rows, LANES)
    for role, long_ref in enumerate((w_long_ref, w_long_mate_ref)):
        own_row = core if role == 0 else 1 - core
        for group in range(groups):
            left, right, slots = [], [], []
            for at in range(GROUP):
                entry = entry_index(entry_ref, role, GROUP * group + at)
                slots.append((entry_ref[6, entry], entry_ref[5, entry]))
                chosen = (row_half == own_row) & (half == at % 2)
                piece = jnp.where(chosen, block_ref[entry_ref[4, entry]], 0.0)
                left.append(piece if at < 2 else zero)
                right.append(zero if at < 2 else piece)
            gathered = jnp.concatenate([stacked(left), stacked(right)], axis=1).astype(bf16)
            gathered_ref[role * groups + group] = gathered
            weights = long_ref[:, group * WIDE : (group + 1) * WIDE]
            back = product_back(gathered, weights)
            for at, (rank, tile) in enumerate(slots):
                slot_ref[role, rank, tile] = back[at * rows : (at + 1) * rows]
    for tile in range(2 * chips):
        lanes = slice(tile % 2 * LANES, (tile % 2 + 1) * LANES)
        parts = [slot_ref[0, rank, tile] + slot_ref[1, rank, tile] for rank in range(CAP)]
        placed_out[tile // 2, :, lanes] = jnp.concatenate(parts, axis=1).astype(bf16)
    for group in range(blocks // GROUP):
        left = stacked([half_only(chunks[2 * group], half, k) for k in range(2)] + [zero, zero])
        right = stacked(
            [zero, zero] + [half_only(chunks[2 * group + 1], half, k) for k in range(2)]
        )
        adj_ref[group] = jnp.concatenate([left, right], axis=1).astype(bf16)
    own_rows = tile_rows(SIDE) == core
    before, own, after = (
        toward_side(side, adj_ref, w_ref, w_mate_ref, own_rows) for side in range(3)
    )
    own_out[...] = own + row_halves(turned(before), turned(after))
    middle = neurons // 2
    to_left = row_halves(before[:, :middle], turned(before[:, middle:])).astype(bf16)
    to_right = row_halves(turned(after[:, :middle]), after[:, middle:]).astype(bf16)
    unused = jnp.zeros_like(to_left)
    for other in range(chips):
        placed_out[other, :, 2 * LANES :] = unused
    placed_out[jnp.where(chip > 0, chip - 1, chip), :, 2 * LANES :] = to_left
    placed_out[jnp.where(chip < chips - 1, chip + 1, chip), :, 2 * LANES :] = to_right


def turn_kernel(*refs):
    near_ref, entry_ref, w_ref, w_mate_ref, w_long_ref, w_long_mate_ref = refs[:6]
    v_ref, g_ref, decay_ref, adj_v_ref, adj_g_ref, asked_ref = refs[6:12]
    g_out, wanted_out, source_ref, fetched_ref = refs[12:16]
    copy = pltpu.make_async_copy(asked_ref, wanted_out, refs[-1])
    copy.start()
    drive = forward_part(
        near_ref, entry_ref, w_ref, w_mate_ref, w_long_ref, w_long_mate_ref, source_ref,
        fetched_ref, refs[23:-1],
    )
    decay = decay_ref[...]
    g_out[...] = decay * g_ref[...] + jax.nn.softplus(drive)
    backward_part(
        adj_g_ref[...], adj_v_ref[...], v_ref[...], jax.nn.sigmoid(drive), decay,
        entry_ref, w_ref, w_mate_ref, w_long_ref, w_long_mate_ref, *refs[16:23],
    )
    copy.wait()


def receive_part(
    moment, placed_ref, own_ref, wanted_ref, adj_v_ref, v_ref, g_ref, spikes_ref, acc_refs
):
    chips, rows, _ = placed_ref.shape
    half = lane_half(rows)
    row_half = sublane_half(rows, LANES)
    chip = lax.axis_index("azim") >> 1
    for ref in acc_refs:
        ref[...] = jnp.zeros_like(ref)
    for other in range(chips):
        for source in range(2):
            arrived = placed_ref[other, :, source * LANES : (source + 1) * LANES].astype(f32)
            for target, piece in ((source, arrived), (1 - source, turned(arrived))):
                piece = jnp.where(row_half == source, piece, 0.0)
                for slot in range(CAP):
                    number = (slot + CAP * target) % len(acc_refs)
                    block = wanted_ref[other, target * 4 + source * CAP + slot]
                    acc_refs[number][block] += piece
    left = placed_ref[jnp.maximum(chip - 1, 0), :, 2 * LANES :].astype(f32)
    right = placed_ref[jnp.minimum(chip + 1, chips - 1), :, 2 * LANES :].astype(f32)
    left = jnp.where(chip > 0, left, 0.0)
    right = jnp.where(chip < chips - 1, right, 0.0)
    beside = row_halves(
        jnp.concatenate([left, turned(left)], axis=1),
        jnp.concatenate([turned(right), right], axis=1),
    )
    adj_act = own_ref[...] + beside + jnp.concatenate(folded(acc_refs, half), axis=1)
    slope = surrogate(v_ref[...])
    slope = 2.0 * slope * (1.0 - slope)
    return adj_v_ref[...] * (0.9 - 0.1 * g_ref[...]) + adj_act * spikes_ref[moment] * slope


def backward_kernel(moment, *refs):
    adj_g_ref, v_ref, gate_ref, decay_ref, entry_ref = refs[7:12]
    weights = refs[12:16]
    adj_v_out = refs[16]
    adj_volt = receive_part(moment, *refs[:7], refs[24:])
    adj_v_out[...] = adj_volt
    backward_part(
        adj_g_ref[...], adj_volt, v_ref[...], gate_ref[...], decay_ref[...],
        entry_ref, *weights, *refs[17:24],
    )


def last_kernel(*refs):
    refs[8][0] = receive_part(0, *refs[:7], refs[9:])
    refs[8][1] = refs[7][...]


def end_kernel(last_ref, got_ref, *outs):
    me = lax.axis_index("azim")
    core = me & 1
    half = in_group(me)
    for number, out in enumerate(outs):
        keep, got = last_ref[number], got_ref[number]
        keep = jnp.where(half == core, keep, turned(keep))
        got = jnp.where(half == core, turned(got), got)
        out[...] = jnp.where(half == 0, row_halves(keep, got), row_halves(got, keep))


def grad_kernel(*refs):
    sources, fetched, adjs, gathered = (refs[k * STEPS : (k + 1) * STEPS] for k in range(4))
    outs = refs[4 * STEPS :]
    core = lax.axis_index("azim") & 1
    row_tile = tile_rows(WIDE, STEPS * GROUP * 8)
    for role, out in enumerate(outs):
        chosen = row_tile == (core if role == 0 else 1 - core)
        for group in range(adjs[0].shape[0]):
            columns = slice(group * WIDE, (group + 1) * WIDE)
            adj = stacked([ref[group] for ref in adjs])
            adj = jnp.where(chosen, adj.astype(f32), 0.0).astype(bf16)
            for side in range(3):
                source = stacked([ref[side, group] for ref in sources])
                total = product_over(source[:, :SIDE], adj)
                out[side * SIDE : (side + 1) * SIDE, columns] = total.astype(out.dtype)
        groups = gathered[0].shape[0] // 2
        for group in range(groups):
            at = role * groups + group
            total = product_over(
                stacked([ref[at] for ref in fetched]), stacked([ref[at] for ref in gathered])
            )
            fold, place = divmod(group * WIDE, out.shape[1])
            first = 3 * SIDE + fold * BLK
            out[first : first + BLK, place : place + WIDE] = (total[:BLK] + total[BLK:]).astype(
                out.dtype
            )


def add_kernel(own_ref, got_ref, local_out, long_out):
    total = own_ref[...] + got_ref[...].astype(f32)
    width = own_ref.shape[1]
    local_out[...] = total[: 3 * SIDE].astype(bf16)
    for fold in range(long_out.shape[1] // width):
        first = 3 * SIDE + fold * BLK
        long_out[:, fold * width : (fold + 1) * width] = total[first : first + BLK].astype(bf16)


def call(kernel, outs, args, scratch=(), hbm_args=(), smem_args=(), smem_outs=(), flops=None):
    def spec(space):
        return pl.BlockSpec(memory_space=space)

    vmem, hbm, smem = (spec(space) for space in (pltpu.VMEM, pltpu.HBM, pltpu.SMEM))
    args = [
        pltpu.with_memory_space_constraint(array, pltpu.HBM) if number in hbm_args else array
        for number, array in enumerate(args)
    ]
    return pl.pallas_call(
        kernel,
        out_shape=[
            pltpu.SMEM(shape, dtype) if number in smem_outs else jax.ShapeDtypeStruct(shape, dtype)
            for number, (shape, dtype) in enumerate(outs)
        ],
        in_specs=[
            smem if number in smem_args else hbm if number in hbm_args else vmem
            for number in range(len(args))
        ],
        out_specs=[smem if number in smem_outs else vmem for number in range(len(outs))],
        scratch_shapes=scratch,
        compiler_params=pltpu.CompilerParams(vmem_limit_bytes=24 * 2**20),
        cost_estimate=flops and pl.CostEstimate(flops=flops, bytes_accessed=0, transcendentals=0),
    )(*args)


def local(
    v_init, g_init, spikes, decay, w_local, w_long, lr_src_tile, lr_src_block, lr_tgt_block,
    adj_v_end, adj_g_end,
):
    rows, neurons = v_init.shape
    blocks = neurons // BLK
    tiles = lax.axis_size("azim")
    chips = tiles // 2
    entries = lr_src_tile.shape[0]
    members = [[tile for tile in range(tiles) if in_group(tile) == k] for k in range(2)]
    pair = [(i, i ^ 1) for i in range(tiles)]

    def spread(values):
        return lax.all_to_all(
            values, "azim", split_axis=0, concat_axis=0, tiled=True, axis_index_groups=members
        )

    state = ((rows, neurons), f32)
    fields = (8, 2 * max(entries, LANES))
    source = ((3, blocks // GROUP, GROUP * rows, WIDE), bf16)
    fetched = ((2 * entries // GROUP, GROUP * rows, LANES), bf16)
    block_row = pltpu.VMEM((blocks, rows, LANES), f32)
    sums = [block_row] * ACCS
    back_scratch = [block_row, pltpu.VMEM((2, CAP, tiles, rows, BLK), f32), *sums]
    back_outs = [
        ((blocks // GROUP, GROUP * rows, WIDE), bf16),
        ((2 * entries // GROUP, GROUP * rows, WIDE), bf16),
        state,
        state,
        ((chips, rows, 2 * LANES + neurons // 2), bf16),
    ]
    w_sides = w_local.reshape(3, SIDE, neurons)
    w_mate = lax.ppermute(w_sides, "azim", pair)
    w_long_mate = lax.ppermute(w_long, "azim", pair)
    held = (
        v_init, spikes, g_init, adj_v_end, adj_g_end, decay,
        lr_src_tile.T, lr_src_block.T, lr_tgt_block.T,
    )
    pack = ((3 + STEPS // 2, rows, neurons), f32)
    keep, send = call(
        start_kernel,
        [pack, pack],
        held,
        [pltpu.VMEM(array.shape, array.dtype) for array in held]
        + [pltpu.SemaphoreType.DMA((len(held),))],
        hbm_args=range(len(held)),
    )
    w_own, w_long = call(
        hold_kernel,
        [(w_sides.shape, bf16), (w_long.shape, bf16)],
        (w_sides, w_long),
        [pltpu.SemaphoreType.DMA((2,))],
        hbm_args=range(2),
    )
    got = lax.ppermute(send, "azim", pair)
    got, w_mate, w_long_mate, w_own, w_long = lax.optimization_barrier(
        (got, w_mate, w_long_mate, w_own, w_long)
    )
    out, v_start, g_start, adj_volt, adj_cond, spikes, decay, entry_rows = call(
        merge_kernel,
        [((chips, rows, neurons), bf16)]
        + [state] * 4
        + [((STEPS, rows, neurons), f32), state, (fields, jnp.int32)],
        (keep, got),
    )
    weights = (w_own, w_mate, w_long, w_long_mate)
    voltages, conducts, gates, sources, fetches = [v_start], [g_start], [], [], []
    for moment in range(STEPS - 1):
        near = spread(out)
        width = neurons + LANES if moment == 0 else neurons
        outs = [state, state, state, source, fetched, ((chips, rows, width), bf16)]
        scratch = list(sums)
        if moment == 0:
            outs.append((fields, jnp.int32))
            scratch += [pltpu.VMEM((chips, rows, LANES), f32), pltpu.SemaphoreType.DMA]
        if moment == 1:
            outs.append(((chips, LANES), jnp.int32))
        voltage, conduct, gate, source_t, fetched_t, out, *asked = call(
            functools.partial(forward_kernel, moment),
            outs,
            (
                near, entry_rows if moment == 0 else entry_list, *weights, voltages[-1],
                conducts[-1], decay, spikes,
            ),
            scratch,
            smem_args=(1,) if moment else (),
            smem_outs=() if moment else (6,),
        )
        if moment == 0:
            (entry_list,) = asked
        if moment == 1:
            (asked_blocks,) = asked
        voltages.append(voltage)
        conducts.append(conduct)
        gates.append(gate)
        sources.append(source_t)
        fetches.append(fetched_t)
    near = spread(out)
    conduct, wanted, source_t, fetched_t, *back = call(
        turn_kernel,
        [state, ((chips, LANES), jnp.int32), source, fetched] + back_outs,
        (
            near, entry_list, *weights, voltages[-1], conducts[-1], decay, adj_volt, adj_cond,
            asked_blocks,
        ),
        back_scratch + [pltpu.SemaphoreType.DMA],
        smem_args=(1,),
        smem_outs=(1,),
    )
    conducts.append(conduct)
    sources.append(source_t)
    fetches.append(fetched_t)
    adjs, gathers = [], []
    for moment in reversed(range(STEPS)):
        adj_t, gathered_t, adj_cond, own, placed = back
        adjs.insert(0, adj_t)
        gathers.insert(0, gathered_t)
        received = (
            spread(placed), own, wanted, adj_volt, voltages[moment], conducts[moment + 1], spikes,
        )
        if moment > 0:
            adj_volt, *back = call(
                functools.partial(backward_kernel, moment),
                [state] + back_outs,
                received
                + (
                    adj_cond, voltages[moment - 1], gates[moment - 1], decay, entry_list, *weights,
                ),
                back_scratch,
                smem_args=(2, 11),
            )
    grads = (3 * SIDE + entries * BLK * BLK // neurons, neurons)
    grads_own, grads_mate = call(
        grad_kernel, [(grads, f32), (grads, bf16)], (*sources, *fetches, *adjs, *gathers)
    )
    got_grads = lax.ppermute(grads_mate, "azim", pair)
    (last,) = call(
        last_kernel, [((2, rows, neurons), f32)], (*received, adj_cond), sums, smem_args=(2,)
    )
    got_last = lax.ppermute(last, "azim", pair)
    grad_local, grad_long = call(
        add_kernel,
        [((3 * SIDE, neurons), bf16), ((BLK, entries * BLK), bf16)],
        (grads_own, got_grads),
        flops=10**10,
    )
    got_last, grad_local, grad_long = lax.optimization_barrier((got_last, grad_local, grad_long))
    adj_volt, adj_cond = call(end_kernel, [state, state], (last, got_last))
    return (adj_volt, adj_cond, grad_local.reshape(9, BLK, neurons), grad_long)


def solution(mesh):
    return jax.shard_map(
        local,
        mesh=mesh,
        in_specs=(
            P("groups", "azim"),
            P("groups", "azim"),
            P(None, "groups", "azim"),
            P("groups", "azim"),
            P("groups", None, "azim"),
            P("groups", "azim"),
            P("azim", "groups"),
            P("azim", "groups"),
            P("azim", "groups"),
            P("groups", "azim"),
            P("groups", "azim"),
        ),
        out_specs=(
            P("groups", "azim"),
            P("groups", "azim"),
            P("groups", None, "azim"),
            P("groups", "azim"),
        ),
        check_vma=False,
    )
```

```python
import functools

import jax
import jax.numpy as jnp
from jax import lax
from jax.experimental import pallas as pl
from jax.experimental.pallas import tpu as pltpu
from jax.sharding import PartitionSpec as P

BLK = 64
CAP = 2
STEPS = 4
LANES = 128
GROUP = 4
WIDE = GROUP * BLK
SIDE = 3 * BLK

f32 = jnp.float32
bf16 = jnp.bfloat16


def surrogate(voltage):
    return jax.nn.sigmoid(2.0 * (voltage - 1.0))


def lane_half(rows):
    return lax.broadcasted_iota(jnp.int32, (rows, LANES), 1) // BLK


def half_only(piece, half, which):
    return jnp.where(half == which, piece, 0.0)


def half_pair(first, second, half):
    return jnp.where(half == 0, first, second)


def swapped(piece):
    return pltpu.roll(piece, BLK, 1)


def chunks_of(values):
    return [values[:, c * LANES : (c + 1) * LANES] for c in range(values.shape[1] // LANES)]


def odd_chunks(chunks, half):
    turned = [swapped(piece) for piece in chunks]
    zero = jnp.zeros_like(chunks[0])
    return [
        half_pair(left, right, half) for left, right in zip([zero] + turned, turned + [zero])
    ]


def product(left, right):
    return lax.dot_general(left, right, (((1,), (0,)), ((), ())), preferred_element_type=f32)


def product_back(left, right):
    return lax.dot_general(left, right, (((1,), (1,)), ((), ())), preferred_element_type=f32)


def product_over(left, right):
    return lax.dot_general(left, right, (((0,), (0,)), ((), ())), preferred_element_type=f32)


def stacked(pieces):
    return jnp.concatenate(pieces, axis=0)


def folded(acc_refs, half):
    chunks = []
    for block in range(0, acc_refs[0].shape[0], 2):
        (low, low_next), (high, high_next) = (
            (sum(ref[block] for ref in refs), sum(ref[block + 1] for ref in refs))
            for refs in (acc_refs[0::2], acc_refs[1::2])
        )
        chunks.append(half_pair(low, high_next, half) + swapped(half_pair(low_next, high, half)))
    return chunks


def in_group(tile):
    return (tile ^ (tile >> 1)) & 1


ACCS = 4


def sublane_half(rows, lanes):
    return lax.broadcasted_iota(jnp.int32, (rows, lanes), 0) // (rows // 2)


def turned(values):
    return pltpu.roll(values, values.shape[0] // 2, 0)


def row_halves(upper, lower):
    return jnp.where(sublane_half(*upper.shape) == 0, upper, lower)


def tile_rows(lanes, rows=GROUP * 8):
    return (lax.broadcasted_iota(jnp.int32, (rows, lanes), 0) // 4) % 2


def copied(pairs, sems):
    copies = [
        pltpu.make_async_copy(source, target, sems.at[number])
        for number, (source, target) in enumerate(pairs)
    ]
    for copy in copies:
        copy.start()
    return copies


def start_kernel(*refs):
    ins, (keep_out, send_out), scratch = refs[:9], refs[9:11], refs[11:]
    kept, sems = scratch[:-1], scratch[-1]
    copies = copied(zip(ins, kept), sems)
    v, spikes, g, adj_v, adj_g, decay, tile_ref, block_ref, target_ref = kept
    rows, neurons = v.shape
    entries = tile_ref.shape[1]
    half = in_group(lax.axis_index("azim"))
    for copy in copies:
        copy.wait()
    across = lax.broadcasted_iota(jnp.int32, (entries, entries), 1)
    down = lax.broadcasted_iota(jnp.int32, (entries, entries), 0)
    tiles = tile_ref[...]
    tiles_down = jnp.sum(
        jnp.where(across == down, tiles.astype(f32), 0.0), axis=1, keepdims=True
    ).astype(jnp.int32)
    earlier = (tiles_down == tiles) & (down < across)
    rank = jnp.sum(jnp.where(earlier, 1.0, 0.0), axis=0, keepdims=True).astype(jnp.int32)
    code = ((tiles * CAP + rank) * 16 + target_ref[...]) * 16 + block_ref[...]
    pairs = ((v[...], g[...]), (adj_v[...], adj_g[...])) + tuple(
        (spikes[k].astype(f32), spikes[k + 1].astype(f32)) for k in range(0, STEPS, 2)
    )
    for number, (first, second) in enumerate(pairs):
        straight = row_halves(first, turned(second))
        crossed = row_halves(turned(first), second)
        keep_out[number] = jnp.where(half == 0, straight, crossed)
        send_out[number] = jnp.where(half == 0, crossed, straight)
    for out in (keep_out, send_out):
        out[len(pairs)] = jnp.zeros((rows, neurons), f32)
        out[len(pairs), 0:1, :] = decay[...]
        out[len(pairs), 1:2, :entries] = code.astype(f32)


def hold_kernel(w_ref, w_long_ref, w_out, w_long_out, sems):
    for copy in copied(((w_ref, w_out), (w_long_ref, w_long_out)), sems):
        copy.wait()


def merge_kernel(
    entries, keep_ref, got_ref, out_ref, v_out, g_out, adj_v_out, adj_g_out, spikes_out, decay_out,
    fields_ref,
):
    core = lax.axis_index("azim") & 1
    rows, neurons = v_out.shape
    first = [jnp.where(core == 0, keep_ref[k], got_ref[k]) for k in range(keep_ref.shape[0])]
    second = [jnp.where(core == 0, got_ref[k], keep_ref[k]) for k in range(keep_ref.shape[0])]
    lanes = fields_ref.shape[1]
    ours, mates = (ref[len(first) - 1][1:2, :lanes] for ref in (keep_ref, got_ref))
    lane = lax.broadcasted_iota(jnp.int32, (1, lanes), 1)
    code = jnp.where(lane < entries, ours, pltpu.roll(mates, entries, 1)).astype(jnp.int32)
    fields = (
        code >> 10, ((code & 15) >> 1) * LANES, (code >> 9) & 1, code & 1, (code >> 4) & 15,
        code >> 9, (code >> 8) & 1, code & 15,
    )
    fields_ref[...] = jnp.concatenate(fields, axis=0)
    merged = []
    for low, high in zip(first[:-1], second[:-1]):
        merged += [row_halves(low, turned(high)), row_halves(turned(low), high)]
    v, g, adj_v, adj_g, *spikes = merged
    activity = (spikes[0] * surrogate(v)).astype(bf16)
    for chip in range(out_ref.shape[0]):
        out_ref[chip] = activity
    v_out[...] = v
    g_out[...] = g
    adj_v_out[...] = adj_v
    adj_g_out[...] = adj_g
    for moment, spiking in enumerate(spikes):
        spikes_out[moment] = spiking
    decay_out[...] = row_halves(
        jnp.broadcast_to(first[-1][0:1, :], (rows, neurons)),
        jnp.broadcast_to(second[-1][0:1, :], (rows, neurons)),
    )


def forward_part(
    near_ref, entry_ref, w_ref, w_mate_ref, w_long_ref, w_long_mate_ref, source_ref, fetched_ref,
    acc_refs, ready=None,
):
    chips, rows, _ = near_ref.shape
    neurons = w_ref.shape[2]
    blocks = neurons // BLK
    half = lane_half(rows)
    me = lax.axis_index("azim")
    chip = me >> 1
    core = me & 1
    for ref in acc_refs:
        ref[...] = jnp.zeros_like(ref)
    def local_part():
        own = near_ref[chip, :, :neurons].astype(f32)
        left = near_ref[jnp.maximum(chip - 1, 0), :, :neurons].astype(f32)
        right = near_ref[jnp.minimum(chip + 1, chips - 1), :, :neurons].astype(f32)
        left = jnp.where(chip > 0, turned(left), 0.0)
        right = jnp.where(chip < chips - 1, turned(right), 0.0)
        sides = (row_halves(left, turned(own)), own, row_halves(turned(own), right))
        for side, values in enumerate(sides):
            even = chunks_of(values)
            odd = odd_chunks(even, half)
            even = even + [jnp.zeros((rows, LANES), f32)]
            for group in range(blocks // GROUP):
                pieces = []
                for block in range(GROUP * group, GROUP * (group + 1)):
                    line = even if block % 2 else odd
                    pieces.append((line[block // 2], line[block // 2 + 1]))
                source_ref[side, group] = jnp.concatenate(
                    [stacked([piece[k] for piece in pieces]) for k in range(2)], axis=1
                ).astype(bf16)
        own_rows = tile_rows(WIDE) == core
        drive = []
        for group in range(blocks // GROUP):
            columns = slice(group * WIDE, (group + 1) * WIDE)
            totals = []
            for ref in (w_ref, w_mate_ref):
                total = product(source_ref[0, group][:, :SIDE], ref[0, :, columns])
                for side in range(1, 3):
                    total = total + product(source_ref[side, group][:, :SIDE], ref[side, :, columns])
                totals.append(total)
            total = jnp.where(own_rows, *totals)
            for pair in range(GROUP // 2):
                lanes = slice(pair * LANES, (pair + 1) * LANES)
                at = 2 * pair * rows
                drive.append(
                    half_pair(
                        total[at : at + rows, lanes], total[at + rows : at + 2 * rows, lanes], half
                    )
                )
        return drive

    def long_part():
        groups = fetched_ref.shape[0] // 2
        row_half = sublane_half(rows, LANES)
        for role, long_ref in enumerate((w_long_ref, w_long_mate_ref)):
            own_row = core if role == 0 else 1 - core
            for group in range(groups):
                pieces, targets = [], []
                for entry in range(GROUP * group, GROUP * (group + 1)):
                    at = role * groups * GROUP + entry
                    lanes = pl.ds(pl.multiple_of(entry_ref[1, at], LANES), LANES)
                    piece = near_ref[entry_ref[0, at], :, lanes].astype(f32)
                    piece = jnp.where(entry_ref[2, at] == own_row, piece, turned(piece))
                    chosen = (row_half == own_row) & (half == entry_ref[3, at])
                    pieces.append(jnp.where(chosen, piece, 0.0))
                    targets.append(entry_ref[4, at])
                fetched = stacked(pieces).astype(bf16)
                fetched_ref[role * groups + group] = fetched
                weights = long_ref[:, group * WIDE : (group + 1) * WIDE]
                total = product(fetched, stacked([weights, weights]))
                for at, target in enumerate(targets):
                    lanes = slice(at // 2 * LANES, (at // 2 + 1) * LANES)
                    acc_refs[(at + 2 * group) % len(acc_refs)][target] += total[
                        at * rows : (at + 1) * rows, lanes
                    ]

    if ready is None:
        long_part()
        drive = local_part()
    else:
        drive = local_part()
        ready.wait()
        long_part()
    extra = folded(acc_refs, half)
    return jnp.concatenate([a + b for a, b in zip(drive, extra)], axis=1)


def forward_kernel(moment, *refs):
    near_ref, entry_ref, w_ref, w_mate_ref, w_long_ref, w_long_mate_ref = refs[:6]
    v_ref, g_ref, decay_ref, spikes_ref = refs[6:10]
    v_out, g_out, gate_out, source_ref, fetched_ref, act_ref = refs[10:16]
    acc_refs = refs[16 : 16 + ACCS] if moment == 2 else refs[17 : 17 + ACCS]
    ready = None
    if moment == 0:
        ready = pltpu.make_async_copy(entry_ref, refs[16], refs[-1])
        ready.start()
        entry_ref = refs[16]
    chips = act_ref.shape[0]
    rows, neurons = v_ref.shape
    if moment == 1:
        asked_ref = refs[16]
        for chip in range(chips):
            asked = near_ref[chip, :, neurons:].astype(f32)
            asked_ref[chip : chip + 1, :] = asked[0:1, :].astype(jnp.int32)
    drive = forward_part(
        near_ref, entry_ref, w_ref, w_mate_ref, w_long_ref, w_long_mate_ref, source_ref,
        fetched_ref, acc_refs, ready,
    )
    voltage = v_ref[...]
    conduct = decay_ref[...] * g_ref[...] + jax.nn.softplus(drive)
    voltage = voltage + 0.1 * (conduct * (3.0 - voltage) - voltage) - spikes_ref[moment]
    v_out[...] = voltage
    g_out[...] = conduct
    gate_out[...] = jax.nn.sigmoid(drive)
    activity = (spikes_ref[moment + 1] * surrogate(voltage)).astype(bf16)
    for chip in range(chips):
        act_ref[chip, :, :neurons] = activity
    if moment == 0:
        ask_ref = refs[-2]
        core = lax.axis_index("azim") & 1
        lane = lax.broadcasted_iota(jnp.int32, (rows, LANES), 1)
        ask_ref[...] = jnp.zeros_like(ask_ref)
        for role in range(2):
            own_row = core if role == 0 else 1 - core
            for entry in range(fetched_ref.shape[0] // 2 * GROUP):
                at = role * (fetched_ref.shape[0] // 2 * GROUP) + entry
                place = own_row * 4 + entry_ref[2, at] * CAP + entry_ref[6, at]
                chip = entry_ref[0, at]
                ask_ref[chip] = jnp.where(
                    lane == place, entry_ref[7, at].astype(f32), ask_ref[chip]
                )
        for chip in range(chips):
            act_ref[chip, :, neurons:] = ask_ref[chip].astype(bf16)


def toward_side(side, adj_ref, w_ref, w_mate_ref, own_rows):
    groups, rows, _ = adj_ref.shape
    rows = rows // GROUP
    blocks = groups * GROUP
    half = lane_half(rows)
    zero = jnp.zeros((rows, LANES), f32)
    even = [zero] * (blocks // 2 + 1)
    odd = [zero] * (blocks // 2 + 1)
    for group in range(groups):
        columns = slice(group * WIDE, (group + 1) * WIDE)
        adj = adj_ref[group]
        back = jnp.where(
            own_rows,
            product_back(adj, w_ref[side, :, columns]),
            product_back(adj, w_mate_ref[side, :, columns]),
        )
        for at in range(GROUP):
            block = GROUP * group + at
            line = even if block % 2 else odd
            lower = back[at * rows : (at + 1) * rows, :LANES]
            upper = back[at * rows : (at + 1) * rows, LANES:]
            upper = jnp.concatenate([upper, jnp.zeros_like(upper)], axis=1)
            line[block // 2] = line[block // 2] + lower
            line[block // 2 + 1] = line[block // 2 + 1] + upper
    moved = [swapped(piece) for piece in odd]
    return jnp.concatenate(
        [even[c] + half_pair(moved[c], moved[c + 1], half) for c in range(blocks // 2)], axis=1
    )


def backward_part(
    adj_cond, adj_volt, voltage, gate, decay, entry_ref, w_ref, w_mate_ref, w_long_ref,
    w_long_mate_ref, adj_ref, gathered_ref, cond_out, own_out, placed_out, block_ref, slot_ref,
    long_first,
):
    rows, neurons = voltage.shape
    blocks = neurons // BLK
    chips = placed_out.shape[0]
    half = lane_half(rows)
    me = lax.axis_index("azim")
    chip = me >> 1
    core = me & 1
    total_g = adj_cond + adj_volt * 0.1 * (3.0 - voltage)
    adj_drive = (total_g * gate).astype(bf16).astype(f32)
    cond_out[...] = decay * total_g
    chunks = chunks_of(adj_drive)
    zero = jnp.zeros((rows, LANES), f32)
    for number, piece in enumerate(chunks):
        moved = swapped(piece)
        block_ref[2 * number] = half_pair(piece, moved, half)
        block_ref[2 * number + 1] = half_pair(moved, piece, half)
    def long_part():
        slot_ref[...] = jnp.zeros_like(slot_ref)
        groups = gathered_ref.shape[0] // 2
        row_half = sublane_half(rows, LANES)
        for role, long_ref in enumerate((w_long_ref, w_long_mate_ref)):
            own_row = core if role == 0 else 1 - core
            for group in range(groups):
                left, right, slots = [], [], []
                for at in range(GROUP):
                    entry = GROUP * (role * groups + group) + at
                    slots.append((entry_ref[6, entry], entry_ref[5, entry]))
                    chosen = (row_half == own_row) & (half == at % 2)
                    piece = jnp.where(chosen, block_ref[entry_ref[4, entry]], 0.0)
                    left.append(piece if at < 2 else zero)
                    right.append(zero if at < 2 else piece)
                gathered = jnp.concatenate([stacked(left), stacked(right)], axis=1).astype(bf16)
                gathered_ref[role * groups + group] = gathered
                weights = long_ref[:, group * WIDE : (group + 1) * WIDE]
                back = product_back(gathered, weights)
                for at, (rank, tile) in enumerate(slots):
                    slot_ref[role, rank, tile] = back[at * rows : (at + 1) * rows]
        for tile in range(2 * chips):
            lanes = slice(tile % 2 * LANES, (tile % 2 + 1) * LANES)
            parts = [slot_ref[0, rank, tile] + slot_ref[1, rank, tile] for rank in range(CAP)]
            placed_out[tile // 2, :, lanes] = jnp.concatenate(parts, axis=1).astype(bf16)

    def local_part():
        for group in range(blocks // GROUP):
            left = stacked([half_only(chunks[2 * group], half, k) for k in range(2)] + [zero, zero])
            right = stacked(
                [zero, zero] + [half_only(chunks[2 * group + 1], half, k) for k in range(2)]
            )
            adj_ref[group] = jnp.concatenate([left, right], axis=1).astype(bf16)
        own_rows = tile_rows(SIDE) == core
        before, own, after = (
            toward_side(side, adj_ref, w_ref, w_mate_ref, own_rows) for side in range(3)
        )
        own_out[...] = own + row_halves(turned(before), turned(after))
        middle = neurons // 2
        to_left = row_halves(before[:, :middle], turned(before[:, middle:])).astype(bf16)
        to_right = row_halves(turned(after[:, :middle]), after[:, middle:]).astype(bf16)
        unused = jnp.zeros_like(to_left)
        for other in range(chips):
            placed_out[other, :, 2 * LANES :] = unused
        placed_out[jnp.where(chip > 0, chip - 1, chip), :, 2 * LANES :] = to_left
        placed_out[jnp.where(chip < chips - 1, chip + 1, chip), :, 2 * LANES :] = to_right

    for part in (long_part, local_part) if long_first else (local_part, long_part):
        part()


def turn_kernel(*refs):
    near_ref, entry_ref, w_ref, w_mate_ref, w_long_ref, w_long_mate_ref = refs[:6]
    v_ref, g_ref, decay_ref, adj_v_ref, adj_g_ref, asked_ref = refs[6:12]
    g_out, wanted_out, source_ref, fetched_ref = refs[12:16]
    copy = pltpu.make_async_copy(asked_ref, wanted_out, refs[-1])
    copy.start()
    drive = forward_part(
        near_ref, entry_ref, w_ref, w_mate_ref, w_long_ref, w_long_mate_ref, source_ref,
        fetched_ref, refs[23:-1],
    )
    decay = decay_ref[...]
    g_out[...] = decay * g_ref[...] + jax.nn.softplus(drive)
    backward_part(
        adj_g_ref[...], adj_v_ref[...], v_ref[...], jax.nn.sigmoid(drive), decay,
        entry_ref, w_ref, w_mate_ref, w_long_ref, w_long_mate_ref, *refs[16:23], True,
    )
    copy.wait()


def receive_part(
    moment, placed_ref, own_ref, wanted_ref, adj_v_ref, v_ref, g_ref, spikes_ref, acc_refs
):
    chips, rows, _ = placed_ref.shape
    half = lane_half(rows)
    row_half = sublane_half(rows, LANES)
    chip = lax.axis_index("azim") >> 1
    for ref in acc_refs:
        ref[...] = jnp.zeros_like(ref)
    for other in range(chips):
        for source in range(2):
            arrived = placed_ref[other, :, source * LANES : (source + 1) * LANES].astype(f32)
            for target, piece in ((source, arrived), (1 - source, turned(arrived))):
                piece = jnp.where(row_half == source, piece, 0.0)
                for slot in range(CAP):
                    number = (slot + CAP * target) % len(acc_refs)
                    block = wanted_ref[other, target * 4 + source * CAP + slot]
                    acc_refs[number][block] += piece
    left = placed_ref[jnp.maximum(chip - 1, 0), :, 2 * LANES :].astype(f32)
    right = placed_ref[jnp.minimum(chip + 1, chips - 1), :, 2 * LANES :].astype(f32)
    left = jnp.where(chip > 0, left, 0.0)
    right = jnp.where(chip < chips - 1, right, 0.0)
    beside = row_halves(
        jnp.concatenate([left, turned(left)], axis=1),
        jnp.concatenate([turned(right), right], axis=1),
    )
    adj_act = own_ref[...] + beside + jnp.concatenate(folded(acc_refs, half), axis=1)
    slope = surrogate(v_ref[...])
    slope = 2.0 * slope * (1.0 - slope)
    return adj_v_ref[...] * (0.9 - 0.1 * g_ref[...]) + adj_act * spikes_ref[moment] * slope


def backward_kernel(moment, *refs):
    adj_g_ref, v_ref, gate_ref, decay_ref, entry_ref = refs[7:12]
    weights = refs[12:16]
    adj_v_out = refs[16]
    adj_volt = receive_part(moment, *refs[:7], refs[24:])
    adj_v_out[...] = adj_volt
    backward_part(
        adj_g_ref[...], adj_volt, v_ref[...], gate_ref[...], decay_ref[...],
        entry_ref, *weights, *refs[17:24], False,
    )


def last_kernel(*refs):
    refs[8][0] = receive_part(0, *refs[:7], refs[9:])
    refs[8][1] = refs[7][...]


def end_kernel(last_ref, got_ref, *outs):
    me = lax.axis_index("azim")
    core = me & 1
    half = in_group(me)
    for number, out in enumerate(outs):
        keep, got = last_ref[number], got_ref[number]
        keep = jnp.where(half == core, keep, turned(keep))
        got = jnp.where(half == core, turned(got), got)
        out[...] = jnp.where(half == 0, row_halves(keep, got), row_halves(got, keep))


def grad_kernel(*refs):
    sources, fetched, adjs, gathered = (refs[k * STEPS : (k + 1) * STEPS] for k in range(4))
    outs = refs[4 * STEPS :]
    core = lax.axis_index("azim") & 1
    row_tile = tile_rows(WIDE, STEPS * GROUP * 8)
    for role, out in enumerate(outs):
        chosen = row_tile == (core if role == 0 else 1 - core)
        for group in range(adjs[0].shape[0]):
            columns = slice(group * WIDE, (group + 1) * WIDE)
            adj = stacked([ref[group] for ref in adjs])
            adj = jnp.where(chosen, adj.astype(f32), 0.0).astype(bf16)
            for side in range(3):
                source = stacked([ref[side, group] for ref in sources])
                total = product_over(source[:, :SIDE], adj)
                out[side * SIDE : (side + 1) * SIDE, columns] = total.astype(out.dtype)
        groups = gathered[0].shape[0] // 2
        for group in range(groups):
            at = role * groups + group
            total = product_over(
                stacked([ref[at] for ref in fetched]), stacked([ref[at] for ref in gathered])
            )
            fold, place = divmod(group * WIDE, out.shape[1])
            first = 3 * SIDE + fold * BLK
            out[first : first + BLK, place : place + WIDE] = (total[:BLK] + total[BLK:]).astype(
                out.dtype
            )


def add_kernel(own_ref, got_ref, local_out, long_out):
    total = own_ref[...] + got_ref[...].astype(f32)
    width = own_ref.shape[1]
    local_out[...] = total[: 3 * SIDE].astype(bf16)
    for fold in range(long_out.shape[1] // width):
        first = 3 * SIDE + fold * BLK
        long_out[:, fold * width : (fold + 1) * width] = total[first : first + BLK].astype(bf16)


def call(kernel, outs, args, scratch=(), hbm_args=(), smem_args=(), smem_outs=(), flops=None):
    def spec(space):
        return pl.BlockSpec(memory_space=space)

    vmem, hbm, smem = (spec(space) for space in (pltpu.VMEM, pltpu.HBM, pltpu.SMEM))
    args = [
        pltpu.with_memory_space_constraint(array, pltpu.HBM) if number in hbm_args else array
        for number, array in enumerate(args)
    ]
    return pl.pallas_call(
        kernel,
        out_shape=[
            pltpu.SMEM(shape, dtype) if number in smem_outs else jax.ShapeDtypeStruct(shape, dtype)
            for number, (shape, dtype) in enumerate(outs)
        ],
        in_specs=[
            smem if number in smem_args else hbm if number in hbm_args else vmem
            for number in range(len(args))
        ],
        out_specs=[smem if number in smem_outs else vmem for number in range(len(outs))],
        scratch_shapes=scratch,
        compiler_params=pltpu.CompilerParams(vmem_limit_bytes=24 * 2**20),
        cost_estimate=flops and pl.CostEstimate(flops=flops, bytes_accessed=0, transcendentals=0),
    )(*args)


def local(
    v_init, g_init, spikes, decay, w_local, w_long, lr_src_tile, lr_src_block, lr_tgt_block,
    adj_v_end, adj_g_end,
):
    rows, neurons = v_init.shape
    blocks = neurons // BLK
    tiles = lax.axis_size("azim")
    chips = tiles // 2
    entries = lr_src_tile.shape[0]
    members = [[tile for tile in range(tiles) if in_group(tile) == k] for k in range(2)]
    pair = [(i, i ^ 1) for i in range(tiles)]

    def spread(values):
        return lax.all_to_all(
            values, "azim", split_axis=0, concat_axis=0, tiled=True, axis_index_groups=members
        )

    state = ((rows, neurons), f32)
    fields = (8, max(2 * entries, LANES))
    source = ((3, blocks // GROUP, GROUP * rows, WIDE), bf16)
    fetched = ((2 * entries // GROUP, GROUP * rows, LANES), bf16)
    block_row = pltpu.VMEM((blocks, rows, LANES), f32)
    sums = [block_row] * ACCS
    back_scratch = [block_row, pltpu.VMEM((2, CAP, tiles, rows, BLK), f32), *sums]
    back_outs = [
        ((blocks // GROUP, GROUP * rows, WIDE), bf16),
        ((2 * entries // GROUP, GROUP * rows, WIDE), bf16),
        state,
        state,
        ((chips, rows, 2 * LANES + neurons // 2), bf16),
    ]
    w_sides = w_local.reshape(3, SIDE, neurons)
    w_mate = lax.ppermute(w_sides, "azim", pair)
    w_long_mate = lax.ppermute(w_long, "azim", pair)
    held = (
        v_init, spikes, g_init, adj_v_end, adj_g_end, decay,
        lr_src_tile.T, lr_src_block.T, lr_tgt_block.T,
    )
    pack = ((3 + STEPS // 2, rows, neurons), f32)
    keep, send = call(
        start_kernel,
        [pack, pack],
        held,
        [pltpu.VMEM(array.shape, array.dtype) for array in held]
        + [pltpu.SemaphoreType.DMA((len(held),))],
        hbm_args=range(len(held)),
    )
    w_own, w_long = call(
        hold_kernel,
        [(w_sides.shape, bf16), (w_long.shape, bf16)],
        (w_sides, w_long),
        [pltpu.SemaphoreType.DMA((2,))],
        hbm_args=range(2),
    )
    got = lax.ppermute(send, "azim", pair)
    got, w_mate, w_long_mate, w_own, w_long = lax.optimization_barrier(
        (got, w_mate, w_long_mate, w_own, w_long)
    )
    out, v_start, g_start, adj_volt, adj_cond, spikes, decay, entry_rows = call(
        functools.partial(merge_kernel, entries),
        [((chips, rows, neurons), bf16)]
        + [state] * 4
        + [((STEPS, rows, neurons), f32), state, (fields, jnp.int32)],
        (keep, got),
    )
    weights = (w_own, w_mate, w_long, w_long_mate)
    voltages, conducts, gates, sources, fetches = [v_start], [g_start], [], [], []
    for moment in range(STEPS - 1):
        near = spread(out)
        width = neurons + LANES if moment == 0 else neurons
        outs = [state, state, state, source, fetched, ((chips, rows, width), bf16)]
        scratch = list(sums)
        if moment == 0:
            outs.append((fields, jnp.int32))
            scratch += [pltpu.VMEM((chips, rows, LANES), f32), pltpu.SemaphoreType.DMA]
        if moment == 1:
            outs.append(((chips, LANES), jnp.int32))
        voltage, conduct, gate, source_t, fetched_t, out, *asked = call(
            functools.partial(forward_kernel, moment),
            outs,
            (
                near, entry_rows if moment == 0 else entry_list, *weights, voltages[-1],
                conducts[-1], decay, spikes,
            ),
            scratch,
            smem_args=(1,) if moment else (),
            smem_outs=() if moment else (6,),
        )
        if moment == 0:
            (entry_list,) = asked
        if moment == 1:
            (asked_blocks,) = asked
        voltages.append(voltage)
        conducts.append(conduct)
        gates.append(gate)
        sources.append(source_t)
        fetches.append(fetched_t)
    near = spread(out)
    conduct, wanted, source_t, fetched_t, *back = call(
        turn_kernel,
        [state, ((chips, LANES), jnp.int32), source, fetched] + back_outs,
        (
            near, entry_list, *weights, voltages[-1], conducts[-1], decay, adj_volt, adj_cond,
            asked_blocks,
        ),
        back_scratch + [pltpu.SemaphoreType.DMA],
        smem_args=(1,),
        smem_outs=(1,),
    )
    conducts.append(conduct)
    sources.append(source_t)
    fetches.append(fetched_t)
    adjs, gathers = [], []
    for moment in reversed(range(STEPS)):
        adj_t, gathered_t, adj_cond, own, placed = back
        adjs.insert(0, adj_t)
        gathers.insert(0, gathered_t)
        received = (
            spread(placed), own, wanted, adj_volt, voltages[moment], conducts[moment + 1], spikes,
        )
        if moment > 0:
            adj_volt, *back = call(
                functools.partial(backward_kernel, moment),
                [state] + back_outs,
                received
                + (
                    adj_cond, voltages[moment - 1], gates[moment - 1], decay, entry_list, *weights,
                ),
                back_scratch,
                smem_args=(2, 11),
            )
    grads = (3 * SIDE + entries * BLK * BLK // neurons, neurons)
    grads_own, grads_mate = call(
        grad_kernel, [(grads, f32), (grads, bf16)], (*sources, *fetches, *adjs, *gathers)
    )
    got_grads = lax.ppermute(grads_mate, "azim", pair)
    (last,) = call(
        last_kernel, [((2, rows, neurons), f32)], (*received, adj_cond), sums, smem_args=(2,)
    )
    got_last = lax.ppermute(last, "azim", pair)
    grad_local, grad_long = call(
        add_kernel,
        [((3 * SIDE, neurons), bf16), ((BLK, entries * BLK), bf16)],
        (grads_own, got_grads),
        flops=10**10,
    )
    got_last, grad_local, grad_long = lax.optimization_barrier((got_last, grad_local, grad_long))
    adj_volt, adj_cond = call(end_kernel, [state, state], (last, got_last))
    return (adj_volt, adj_cond, grad_local.reshape(9, BLK, neurons), grad_long)


def solution(mesh):
    return jax.shard_map(
        local,
        mesh=mesh,
        in_specs=(
            P("groups", "azim"),
            P("groups", "azim"),
            P(None, "groups", "azim"),
            P("groups", "azim"),
            P("groups", None, "azim"),
            P("groups", "azim"),
            P("azim", "groups"),
            P("azim", "groups"),
            P("azim", "groups"),
            P("groups", "azim"),
            P("groups", "azim"),
        ),
        out_specs=(
            P("groups", "azim"),
            P("groups", "azim"),
            P("groups", None, "azim"),
            P("groups", "azim"),
        ),
        check_vma=False,
    )
```
